256 devices in a mesh: layer: 2 (over core), cam: 32 (over z, x), pair: 4 (over y).
Axes of the slice: x: 4, y: 4, z: 8, core: 2. Of those that a mesh axis runs over, the one named last changes fastest.
Arguments:
- jac_blocks: bfloat16 [8192, 4, 27, 128], P(('layer', 'cam', 'pair')), may hold values from -0.071777344 to 0.071777344
- point_blocks: bfloat16 [8192, 6, 128], P(('layer', 'cam', 'pair')), may hold values from -3.6 to 8, as said below
- visibility: int32 [8192, 4, 128], P(('layer', 'cam', 'pair')), may hold values from 0 to 47, as said below
- obs_count: int32 [8192, 128], P(('layer', 'cam', 'pair')), may hold values from 2 to 4
- tile_count: int32 [8192], P(('layer', 'cam', 'pair')), may hold values from 64 to 128
- route: int32 [8192, 1], P(('layer', 'cam', 'pair')), may hold values from 0 to 31; in each aligned block of 32 rows (0 to 31, 32 to 63, ...) at most 2 rows name the same one
- camera_blocks: float32 [32, 9, 9, 48], P('cam'), may hold values from -6 to 6
Outputs:
- schur: float32 [32, 432, 432], P('cam', ('layer', 'pair'))
The draws below stay inside these ranges and needn't reach their ends.
Inputs may be any that keep to these rules, and one draw needn't show every extreme that they name: `visibility`: the 4 cameras of one point's list are distinct. `route`: of the 32 tiles of one device at most 2 name one camera group, and some device sends exactly 2 tiles to some group. `point_blocks`: each block is symmetric and diagonally dominant: every off-diagonal entry is at most 0.45 times the root of the product of its two diagonal entries, which lie in 1 to 8.
All inputs are finite; a program needn't handle non-finite values.
Results may differ from the reference program's by a relative error of at most 0.0003.
Values may be sent and summed in bfloat16 or wider, within the bound.
No kernel may reach another device: no remote copies, remote signals or barrier semaphores. Data moves between devices by JAX's collectives and lax.ppermute only.
A program may use at most 64 MiB of HBM per device.

```python
import math
import jax
import jax.numpy as jnp
import numpy as np
from jax import lax

CG = 48
PTS = 128
SLOTS = 4
TILES_DEV = 32
CAP = 2
TILES = 8192
N_CAM = 32


def draw_visibility(key, part):
    key = jax.random.fold_in(key, 11)
    key_base, key_step = jax.random.split(key)
    anchor = jax.random.randint(key_base, (TILES, 1, PTS), 0, CG, dtype=jnp.int32)
    strides = jax.random.randint(key_step, (TILES, SLOTS - 1, PTS), 1, CG // 4 + 1, dtype=jnp.int32)
    offsets = jnp.concatenate([jnp.zeros((TILES, 1, PTS), jnp.int32), jnp.cumsum(strides, axis=1)], axis=1)
    return (anchor + offsets) % CG


def draw_point_blocks(key, part):
    key = jax.random.fold_in(key, 23)
    key_diag, key_off = jax.random.split(key)
    diagonal = jnp.exp(jax.random.uniform(key_diag, (TILES, 3, PTS), jnp.float32, 0.0, math.log(8.0)))
    coupling = jnp.clip(0.2 * jax.random.normal(key_off, (TILES, 3, PTS), jnp.float32), -0.45, 0.45)
    sqrt_diag = jnp.sqrt(diagonal)
    cross_terms = jnp.stack([sqrt_diag[:, 0] * sqrt_diag[:, 1], sqrt_diag[:, 0] * sqrt_diag[:, 2], sqrt_diag[:, 1] * sqrt_diag[:, 2]], axis=1) * coupling
    return jnp.concatenate([diagonal, cross_terms], axis=1).astype(jnp.bfloat16)


def with_ends(array, stream_key, smallest, top_value):
    place = [jax.random.randint(jax.random.fold_in(stream_key, axis), (), 0, length) for axis, length in enumerate(array.shape)]
    longest = array.shape.index(max(array.shape))
    next_to = place[:longest] + [(place[longest] + 1) % array.shape[longest]] + place[longest + 1:]
    return array.at[tuple(place)].set(smallest).at[tuple(next_to)].set(top_value)


def block_levels(rng, dims, cuts, least, top_value):
    factor_of, own = 1.0, jax.random.fold_in(rng, 6)
    for dim, shards_of in cuts:
        draws = jnp.exp(jax.random.uniform(jax.random.fold_in(own, dim), (shards_of,), jnp.float32, least / len(cuts), top_value / len(cuts)))
        factor_of = factor_of * jnp.repeat(draws, dims[dim] // shards_of).reshape([-1 if axis == dim else 1 for axis in range(len(dims))])
    return factor_of


def deal_out(key, own, number, rows, number_of, top, most, skew):
    sequence = jax.random.permutation(key, number_of)
    crowded, ordinary = load_shares(number_of, rows * top, most, skew, True), load_shares(number_of, rows * top, most, skew, False)
    places = jnp.arange(number_of)

    def named(tallies, rotation):
        used = int((tallies > 0).sum())
        fixed = max(1, used // 4)
        shifted = fixed + (places - fixed + rotation * (used - fixed)) % max(1, number_of - fixed)
        return jnp.zeros((number_of,), jnp.int32).at[sequence[jnp.where(places < fixed, places, shifted)]].set(jnp.asarray(tallies, jnp.int32))

    tallies = jnp.where(number % 4 == 0, named(crowded, number // 4), named(ordinary, number - number // 4 - 1))
    mixed = jax.random.permutation(jax.random.fold_in(own, 3), number_of)
    donor, sink = mixed[0:number_of // 2 * 2:2], mixed[1:number_of // 2 * 2:2]
    margin = jnp.minimum(tallies[donor] - 1, most - tallies[sink]) // 2
    margin = jnp.where((donor == sequence[0]) | (sink == sequence[0]) | (tallies[sink] == 0), 0, jnp.maximum(margin, 0))
    shifted = jax.random.randint(jax.random.fold_in(own, 4), (number_of // 2,), 0, 1 << 20) % (margin + 1)
    tallies = tallies.at[donor].add(-shifted).at[sink].add(shifted)
    members = jnp.searchsorted(jnp.cumsum(tallies), jnp.arange(rows * top), side="right").astype(jnp.int32)
    table = members.reshape(top, rows).T
    table = table[jax.random.permutation(jax.random.fold_in(own, 1), rows)]
    rotation = jax.random.randint(jax.random.fold_in(own, 2), (rows, 1), 0, top)
    return jnp.take_along_axis(table, (jnp.arange(top)[None, :] + rotation) % top, axis=1)


def load_shares(number_of, total, limit, slope, full):
    weights = [(1 << 20) // math.isqrt(rank ** slope) + 1 for rank in range(1, number_of + 1)]
    largest = limit if full else min(limit, max(-(-total // number_of), total * weights[0] // sum(weights)))
    least = 1 if total - largest >= number_of - 1 else 0
    counts, surplus = [largest] + [least] * (number_of - 1), total - largest - least * (number_of - 1)
    while surplus > 0:
        movable = [i for i in range(1, number_of) if counts[i] < largest] or [i for i in range(1, number_of) if counts[i] < limit]
        mass, budget = sum([weights[i] for i in movable]), surplus
        for i in movable:
            extra = min(limit - counts[i], max(1, budget * weights[i] // mass), surplus)
            counts[i] = counts[i] + extra
            surplus = surplus - extra
    return np.array(counts)


def gaussian(own_key, extent, spread, limit, cuts=(), kind=jnp.bfloat16):
    values = jax.random.normal(own_key, extent, jnp.float32) * spread
    if len(cuts) > 0:
        values = block_levels(own_key, extent, cuts, -0.22, 0.18) * values
    return jnp.clip(values, min=-limit, max=limit).astype(kind)


def setup_inputs(seed: int = 0) -> dict:
    splits = jax.random.split(jax.random.key(seed), 8)
    jac_blocks = gaussian(splits[0], (TILES, SLOTS, 27, PTS), 0.012, 0.071777344, ((0, 256),))
    point_blocks = draw_point_blocks(jax.random.fold_in(splits[7], 71), 0)
    visibility = draw_visibility(jax.random.fold_in(splits[7], 71), 0)
    obs_count = with_ends(jax.random.randint(splits[3], (TILES, PTS), 2, SLOTS + 1), jax.random.fold_in(splits[3], 1), 2, SLOTS).astype(jnp.int32)
    tile_count = with_ends(jax.random.randint(splits[4], (TILES,), PTS // 2, PTS + 1), jax.random.fold_in(splits[4], 1), PTS // 2, PTS).astype(jnp.int32)
    route_keys = jax.random.split(jax.random.fold_in(splits[5], 1), TILES // TILES_DEV)
    route_turns = jax.random.permutation(jax.random.fold_in(splits[5], 3), TILES // TILES_DEV)
    route = jax.vmap(lambda own, number: deal_out(jax.random.fold_in(splits[5], 2), own, number, TILES_DEV, N_CAM, 1, CAP, 2))(route_keys, route_turns).reshape((TILES, 1))
    camera_blocks = gaussian(splits[6], (N_CAM, 9, 9, CG), 1.0, 6.0, ((0, 32),), jnp.float32)
    return {"jac_blocks": jac_blocks, "point_blocks": point_blocks, "visibility": visibility, "obs_count": obs_count, "tile_count": tile_count, "route": route, "camera_blocks": camera_blocks}


def point_inverse(blocks):
    values = blocks.astype(jnp.float32)
    entry_xx = values[..., 0, :]
    entry_yy = values[..., 1, :]
    entry_zz = values[..., 2, :]
    entry_xy = values[..., 3, :]
    entry_xz = values[..., 4, :]
    entry_yz = values[..., 5, :]
    cofac_xx = entry_yy * entry_zz - entry_yz * entry_yz
    cofac_yy = entry_xx * entry_zz - entry_xz * entry_xz
    cofac_zz = entry_xx * entry_yy - entry_xy * entry_xy
    cofac_xy = entry_xz * entry_yz - entry_xy * entry_zz
    cofac_xz = entry_xy * entry_yz - entry_xz * entry_yy
    cofac_yz = entry_xy * entry_xz - entry_xx * entry_yz
    determinant = entry_xx * cofac_xx + entry_xy * cofac_xy + entry_xz * cofac_xz
    inv_det = 1.0 / determinant
    return ((cofac_xx * inv_det, cofac_xy * inv_det, cofac_xz * inv_det),
            (cofac_xy * inv_det, cofac_yy * inv_det, cofac_yz * inv_det),
            (cofac_xz * inv_det, cofac_yz * inv_det, cofac_zz * inv_det))


def reduce_blocks(jacobian, blocks):
    inverse = point_inverse(blocks)
    lead_shape = jacobian.shape[:-2]
    tile_width = jacobian.shape[-1]
    factors = jacobian.astype(jnp.float32).reshape(lead_shape + (9, 3, tile_width))
    columns = []
    for out_col in range(3):
        running = factors[..., :, 0, :] * inverse[0][out_col][..., None, None, :]
        for in_row in range(1, 3):
            running = running + factors[..., :, in_row, :] * inverse[in_row][out_col][..., None, None, :]
        columns.append(running)
    stacked = jnp.stack(columns, axis=-2)
    return stacked.reshape(lead_shape + (27, tile_width)).astype(jnp.bfloat16)


def reference(jac_blocks, point_blocks, visibility, obs_count, tile_count, route, camera_blocks):
    tiles_all = jac_blocks.shape[0]
    step_tiles = math.gcd(tiles_all, 64)
    turn_count = tiles_all // step_tiles
    segments = N_CAM * CG * CG

    def accumulate(running, step_index):
        first_row = step_index * step_tiles
        jac_part = lax.dynamic_slice_in_dim(jac_blocks, first_row, step_tiles, 0)
        block_part = lax.dynamic_slice_in_dim(point_blocks, first_row, step_tiles, 0)
        vis_part = lax.dynamic_slice_in_dim(visibility, first_row, step_tiles, 0)
        count_part = lax.dynamic_slice_in_dim(obs_count, first_row, step_tiles, 0)
        fill_part = lax.dynamic_slice_in_dim(tile_count, first_row, step_tiles, 0)
        target = lax.dynamic_slice_in_dim(route, first_row, step_tiles, 0)[:, 0]
        left_side = reduce_blocks(jac_part, block_part).astype(jnp.float32).reshape(step_tiles, SLOTS, 9, 3, PTS)
        right_side = jac_part.astype(jnp.float32).reshape(step_tiles, SLOTS, 9, 3, PTS)
        pair_terms = jnp.einsum("tirkp,tjskp->tpijrs", left_side, right_side)
        slot_iota = lax.broadcasted_iota(jnp.int32, (step_tiles, SLOTS, PTS), 1)
        point_iota = lax.broadcasted_iota(jnp.int32, (step_tiles, SLOTS, PTS), 2)
        is_live = (slot_iota < count_part[:, None, :]) & (point_iota < fill_part[:, None, None])
        cam_marks = jnp.where(is_live, vis_part, -1).transpose(0, 2, 1)
        is_valid = (cam_marks[:, :, :, None] >= 0) & (cam_marks[:, :, None, :] >= 0)
        segment_id = (target[:, None, None, None] * CG + cam_marks[:, :, :, None]) * CG + cam_marks[:, :, None, :]
        segment_id = jnp.where(is_valid, segment_id, segments).astype(jnp.int32)
        summed = jax.ops.segment_sum(pair_terms.reshape(-1, 81), segment_id.reshape(-1), num_segments=segments + 1)
        return running + summed[:segments], None

    initial = jnp.zeros((segments, 81), jnp.float32)
    reduction, _ = lax.scan(accumulate, initial, jnp.arange(turn_count, dtype=jnp.int32))
    reduction = reduction.reshape(N_CAM, CG, CG, 9, 9).transpose(0, 3, 1, 4, 2).reshape(N_CAM, 9 * CG, 9 * CG)
    unit_matrix = jnp.eye(CG, dtype=jnp.float32)
    dense_hessian = camera_blocks.transpose(0, 1, 3, 2)[..., None] * unit_matrix[None, None, :, None, :]
    dense_hessian = dense_hessian.reshape(N_CAM, 9 * CG, 9 * CG)
    return dense_hessian - reduction
```

```python
import functools

import jax
import jax.numpy as jnp
from jax import lax
from jax.experimental import pallas as pl
from jax.experimental.pallas import tpu as pltpu
from jax.sharding import PartitionSpec as P

GROUPS_OF_ROWS = 30


def pack_kernel(route_ref, count_ref, jac_ref, block_ref, vis_ref, obs_ref, out_ref, block_scratch, fill_ref):
    tiles = jac_ref.shape[0]
    groups = out_ref.shape[0]
    width = jac_ref.shape[3]
    block_scratch[...] = block_ref[...].astype(jnp.float32)
    dead = jnp.full((4, width), -1.0, jnp.bfloat16)

    def clear(group, carry):
        fill_ref[group] = 0
        out_ref[group, 0, 27] = dead
        out_ref[group, 1, 27] = dead
        return carry

    lax.fori_loop(0, groups, clear, 0, unroll=8)
    slot_iota = lax.broadcasted_iota(jnp.int32, (4, width), 0)
    point_iota = lax.broadcasted_iota(jnp.int32, (4, width), 1)

    def place(tile, carry):
        group = route_ref[tile]
        slot = fill_ref[group]
        fill_ref[group] = slot + 1
        obs = jnp.broadcast_to(obs_ref[pl.ds(tile, 1), :], (4, width))
        live = (slot_iota < obs) & (point_iota < count_ref[tile])
        marks = jnp.where(live, vis_ref[tile], -1).astype(jnp.float32).astype(jnp.bfloat16)
        rows = [block_scratch[c, pl.ds(tile, 1), :] for c in range(6)]
        zero = jnp.zeros_like(rows[0])
        out_ref[group, slot, pl.ds(0, 27)] = jac_ref[tile]
        out_ref[group, slot, 27] = marks
        out_ref[group, slot, 28] = jnp.concatenate(rows[:4], axis=0).astype(jnp.bfloat16)
        out_ref[group, slot, 29] = jnp.concatenate(rows[4:] + [zero, zero], axis=0).astype(jnp.bfloat16)
        return carry

    lax.fori_loop(0, tiles, place, 0, unroll=4)


def pack(jac, blocks, vis, obs, counts, dest, groups):
    width = jac.shape[3]
    smem = pl.BlockSpec(memory_space=pltpu.SMEM)
    vmem = pl.BlockSpec(memory_space=pltpu.VMEM)
    return pl.pallas_call(
        pack_kernel,
        out_shape=jax.ShapeDtypeStruct((groups, 2, GROUPS_OF_ROWS, 4, width), jnp.bfloat16),
        in_specs=[smem, smem, vmem, vmem, vmem, vmem],
        out_specs=vmem,
        scratch_shapes=[pltpu.VMEM(blocks.shape, jnp.float32), pltpu.SMEM((groups,), jnp.int32)],
        compiler_params=pltpu.CompilerParams(vmem_limit_bytes=24 * 1024 * 1024),
        cost_estimate=pl.CostEstimate(flops=1000000, bytes_accessed=3000000, transcendentals=0),
        name="pack",
    )(dest, counts, jac, blocks, vis, obs)


def inverse_rows(first, second):
    xx, yy, zz, xy = (first[c : c + 1] for c in range(4))
    xz, yz = (second[c : c + 1] for c in range(2))
    cxx = yy * zz - yz * yz
    cyy = xx * zz - xz * xz
    czz = xx * yy - xy * xy
    cxy = xz * yz - xy * zz
    cxz = xy * yz - xz * yy
    cyz = xy * xz - xx * yz
    inv_det = 1.0 / (xx * cxx + xy * cxy + xz * cxz)
    ixx, iyy, izz, ixy, ixz, iyz = (c * inv_det for c in (cxx, cyy, czz, cxy, cxz, cyz))
    return ((ixx, ixy, ixz), (ixy, iyy, iyz), (ixz, iyz, izz))


def expand_slot(got_ref, source, slot, rows_ref, left_ref, right_ref, column, cameras):
    width = got_ref.shape[4]
    first = got_ref[source, slot, 28].astype(jnp.float32)
    second = got_ref[source, slot, 29].astype(jnp.float32)
    inverse = inverse_rows(first, second)
    wide = [[jnp.broadcast_to(entry, (4, width)) for entry in line] for line in inverse]
    for r in range(9):
        factors = [got_ref[source, slot, 3 * r + m].astype(jnp.float32) for m in range(3)]
        for k in range(3):
            value = factors[0] * wide[0][k] + factors[1] * wide[1][k] + factors[2] * wide[2][k]
            rows_ref[3 * r + k, 0:4] = value.astype(jnp.bfloat16).astype(jnp.float32)
            rows_ref[3 * r + k, 4:8] = factors[k]
    rows_ref[27, 0:4] = got_ref[source, slot, 27].astype(jnp.float32)
    blocks = cameras // 16
    iota = lax.broadcasted_iota(jnp.int32, (16, width), 0).astype(jnp.float32)
    masks = []
    for i in range(4):
        mark = jnp.broadcast_to(rows_ref[27, i : i + 1], (16, width)).astype(jnp.bfloat16)
        masks.append([mark == (iota + 16.0 * b).astype(jnp.bfloat16) for b in range(blocks)])
    zero = jnp.zeros((16, width), jnp.bfloat16)
    for r in range(9):
        for k in range(3):
            for side, out in ((0, left_ref), (4, right_ref)):
                sums = [zero] * blocks
                for i in range(4):
                    row = jnp.broadcast_to(rows_ref[3 * r + k, side + i : side + i + 1], (16, width))
                    row = row.astype(jnp.bfloat16)
                    sums = [jnp.where(masks[i][b], row, sums[b]) for b in range(blocks)]
                for b in range(blocks):
                    out[pl.ds(r * cameras + 16 * b, 16), pl.ds(column + k * width, width)] = sums[b]


def schur_kernel(cameras, got_ref, out_ref, total, rows_ref, left_ref, right_ref):
    sources = got_ref.shape[0]
    width = got_ref.shape[4]
    total[...] = jnp.zeros_like(total)

    def expand(source, buffer):
        for slot in range(2):
            expand_slot(
                got_ref, source, slot, rows_ref.at[slot], left_ref.at[buffer], right_ref.at[buffer],
                slot * 3 * width, cameras,
            )

    def multiply(buffer):
        total[...] += lax.dot_general(
            left_ref[buffer], right_ref[buffer], (((1,), (1,)), ((), ())), preferred_element_type=jnp.float32
        )

    expand(0, 0)

    def step(turn, carry):
        expand(2 * turn + 1, 1)
        multiply(0)
        expand(jnp.minimum(2 * turn + 2, sources - 1), 0)
        multiply(1)
        return carry

    lax.fori_loop(0, sources // 2, step, 0)
    share = out_ref.shape[1]
    for part in range(out_ref.shape[0]):
        out_ref[part] = total[pl.ds(part * share, share), :]


def schur_partial(got, cameras, shares):
    width = got.shape[4]
    side = 9 * cameras
    vmem = pl.BlockSpec(memory_space=pltpu.VMEM)
    return pl.pallas_call(
        functools.partial(schur_kernel, cameras),
        out_shape=jax.ShapeDtypeStruct((shares, side // shares, side), jnp.float32),
        in_specs=[vmem],
        out_specs=vmem,
        scratch_shapes=[
            pltpu.VMEM((side, side), jnp.float32),
            pltpu.VMEM((2, 28, 8, width), jnp.float32),
            pltpu.VMEM((2, side, 6 * width), jnp.bfloat16),
            pltpu.VMEM((2, side, 6 * width), jnp.bfloat16),
        ],
        compiler_params=pltpu.CompilerParams(vmem_limit_bytes=32 * 1024 * 1024),
        cost_estimate=pl.CostEstimate(flops=10000000000, bytes_accessed=3000000, transcendentals=0),
        name="schur_partial",
    )(got)


def local(jac_blocks, point_blocks, visibility, obs_count, tile_count, route, camera_blocks):
    groups = lax.axis_size("cam")
    cameras = camera_blocks.shape[3]
    side = 9 * cameras
    shares = lax.axis_size("layer") * lax.axis_size("pair")
    packed = pack(
        jac_blocks.transpose(0, 2, 1, 3), point_blocks.transpose(1, 0, 2), visibility, obs_count, tile_count,
        route[:, 0], groups,
    )
    got = lax.all_to_all(packed, "cam", split_axis=0, concat_axis=0, tiled=True)
    partial_value = schur_partial(got, cameras, shares)
    pieces = lax.all_to_all(partial_value, ("layer", "pair"), split_axis=0, concat_axis=0, tiled=True)
    share = lax.axis_index("layer") * lax.axis_size("pair") + lax.axis_index("pair")
    share_rows = side // shares
    row = share * share_rows + lax.broadcasted_iota(jnp.int32, (share_rows, side), 0)
    column = lax.broadcasted_iota(jnp.int32, (share_rows, side), 1)
    lines = camera_blocks[0].reshape(9, side)
    first = share * share_rows // cameras
    own = jnp.zeros((share_rows, side), jnp.float32)
    for step in range(-(-share_rows // cameras) + 1):
        line = lax.dynamic_slice_in_dim(lines, jnp.minimum(first + step, 8), 1, 0)
        own = jnp.where(row // cameras == first + step, line, own)
    own = jnp.where(row % cameras == column % cameras, own, 0.0)
    return (own - jnp.sum(pieces, axis=0))[None]


def solution(mesh):
    placed = (
        P(("layer", "cam", "pair"), None, None, None),
        P(("layer", "cam", "pair"), None, None),
        P(("layer", "cam", "pair"), None, None),
        P(("layer", "cam", "pair"), None),
        P(("layer", "cam", "pair")),
        P(("layer", "cam", "pair"), None),
        P("cam", None, None, None),
    )
    return jax.shard_map(
        local,
        mesh=mesh,
        in_specs=placed,
        out_specs=P("cam", ("layer", "pair"), None),
        check_vma=False,
    )
```

```python
import functools
import itertools

import jax
import jax.numpy as jnp
from jax import lax
from jax.experimental import pallas as pl
from jax.experimental.pallas import tpu as pltpu
from jax.sharding import PartitionSpec as P

GROUPS_OF_ROWS = 30


def pack_kernel(
    site_of, route_hbm, count_hbm, jac_hbm, block_hbm, vis_hbm, obs_hbm, out_ref,
    route_ref, count_ref, block_ref, vis_ref, obs_ref, block_scratch, fill_ref, small_sems, tile_sems,
):
    tiles = jac_hbm.shape[0]
    width = jac_hbm.shape[3]
    places = out_ref.shape[0]
    small = [
        pltpu.make_async_copy(source, target, small_sems.at[index])
        for index, (source, target) in enumerate((
            (route_hbm, route_ref), (count_hbm, count_ref), (block_hbm, block_ref),
            (vis_hbm, vis_ref), (obs_hbm, obs_ref),
        ))
    ]
    for copy in small:
        copy.start()
    dead = jnp.full((4, width), -1.0, jnp.bfloat16)

    def clear(place, carry):
        fill_ref[place] = 0
        out_ref[place, 0, 27] = dead
        out_ref[place, 1, 27] = dead
        return carry

    lax.fori_loop(0, places, clear, 0, unroll=8)
    small[0].wait()

    def send(tile, carry):
        place = site_of(route_ref[tile])
        slot = fill_ref[place]
        fill_ref[place] = slot + 1
        route_ref[tile] = 2 * place + slot
        pltpu.make_async_copy(
            jac_hbm.at[tile], out_ref.at[place, slot, pl.ds(0, 27)], tile_sems.at[tile]
        ).start()
        return carry

    lax.fori_loop(0, tiles, send, 0, unroll=4)
    for copy in small[1:]:
        copy.wait()
    block_scratch[...] = block_ref[...].astype(jnp.float32)
    slot_iota = lax.broadcasted_iota(jnp.int32, (4, width), 0)
    point_iota = lax.broadcasted_iota(jnp.int32, (4, width), 1)

    def fill(tile, carry):
        place = route_ref[tile] // 2
        slot = route_ref[tile] % 2
        obs = jnp.broadcast_to(obs_ref[pl.ds(tile, 1), :], (4, width))
        live = (slot_iota < obs) & (point_iota < count_ref[tile])
        marks = jnp.where(live, vis_ref[tile], -1).astype(jnp.float32).astype(jnp.bfloat16)
        rows = [block_scratch[c, pl.ds(tile, 1), :] for c in range(6)]
        zero = jnp.zeros_like(rows[0])
        out_ref[place, slot, 27] = marks
        out_ref[place, slot, 28] = jnp.concatenate(rows[:4], axis=0).astype(jnp.bfloat16)
        out_ref[place, slot, 29] = jnp.concatenate(rows[4:] + [zero, zero], axis=0).astype(jnp.bfloat16)
        return carry

    lax.fori_loop(0, tiles, fill, 0, unroll=4)

    def finish(tile, carry):
        pltpu.make_async_copy(jac_hbm.at[0], out_ref.at[0, 0, pl.ds(0, 27)], tile_sems.at[tile]).wait()
        return carry

    lax.fori_loop(0, tiles, finish, 0)


def pack(jac, blocks, vis, obs, counts, route, places, site_of):
    tiles, width = jac.shape[0], jac.shape[3]
    anywhere = pl.BlockSpec(memory_space=pl.ANY)
    return pl.pallas_call(
        functools.partial(pack_kernel, site_of),
        out_shape=jax.ShapeDtypeStruct((places, 2, GROUPS_OF_ROWS, 4, width), jnp.bfloat16),
        in_specs=[anywhere] * 6,
        out_specs=pl.BlockSpec(memory_space=pltpu.VMEM),
        scratch_shapes=[
            pltpu.SMEM(route.shape, jnp.int32),
            pltpu.SMEM(counts.shape, jnp.int32),
            pltpu.VMEM(blocks.shape, jnp.bfloat16),
            pltpu.VMEM(vis.shape, jnp.int32),
            pltpu.VMEM(obs.shape, jnp.int32),
            pltpu.VMEM(blocks.shape, jnp.float32),
            pltpu.SMEM((places,), jnp.int32),
            pltpu.SemaphoreType.DMA((5,)),
            pltpu.SemaphoreType.DMA((tiles,)),
        ],
        compiler_params=pltpu.CompilerParams(vmem_limit_bytes=24 * 1024 * 1024),
        cost_estimate=pl.CostEstimate(flops=1000000, bytes_accessed=3000000, transcendentals=0),
        name="pack",
    )(route, counts, jac, blocks, vis, obs)


def inverse_rows(first, second):
    xx, yy, zz, xy = (first[c : c + 1] for c in range(4))
    xz, yz = (second[c : c + 1] for c in range(2))
    cxx = yy * zz - yz * yz
    cyy = xx * zz - xz * xz
    czz = xx * yy - xy * xy
    cxy = xz * yz - xy * zz
    cxz = xy * yz - xz * yy
    cyz = xy * xz - xx * yz
    inv_det = 1.0 / (xx * cxx + xy * cxy + xz * cxz)
    ixx, iyy, izz, ixy, ixz, iyz = (c * inv_det for c in (cxx, cyy, czz, cxy, cxz, cyz))
    return ((ixx, ixy, ixz), (ixy, iyy, iyz), (ixz, iyz, izz))


def expand_slot(got_ref, source, slot, rows_ref, left_ref, right_ref, column, cameras):
    width = got_ref.shape[4]
    first = got_ref[source, slot, 28].astype(jnp.float32)
    second = got_ref[source, slot, 29].astype(jnp.float32)
    inverse = inverse_rows(first, second)
    wide = [[jnp.broadcast_to(entry, (4, width)) for entry in line] for line in inverse]
    for r in range(9):
        factors = [got_ref[source, slot, 3 * r + m].astype(jnp.float32) for m in range(3)]
        for k in range(3):
            value = factors[0] * wide[0][k] + factors[1] * wide[1][k] + factors[2] * wide[2][k]
            rows_ref[3 * r + k, 0:4] = value.astype(jnp.bfloat16).astype(jnp.float32)
            rows_ref[3 * r + k, 4:8] = factors[k]
    rows_ref[27, 0:4] = got_ref[source, slot, 27].astype(jnp.float32)
    blocks = cameras // 16
    iota = lax.broadcasted_iota(jnp.int32, (16, width), 0).astype(jnp.float32)
    masks = []
    for i in range(4):
        mark = jnp.broadcast_to(rows_ref[27, i : i + 1], (16, width)).astype(jnp.bfloat16)
        masks.append([mark == (iota + 16.0 * b).astype(jnp.bfloat16) for b in range(blocks)])
    zero = jnp.zeros((16, width), jnp.bfloat16)
    yield
    for r in range(9):
        for k in range(3):
            for side, out in ((0, left_ref), (4, right_ref)):
                sums = [zero] * blocks
                for i in range(4):
                    row = jnp.broadcast_to(rows_ref[3 * r + k, side + i : side + i + 1], (16, width))
                    row = row.astype(jnp.bfloat16)
                    sums = [jnp.where(masks[i][b], row, sums[b]) for b in range(blocks)]
                for b in range(blocks):
                    out[pl.ds(r * cameras + 16 * b, 16), pl.ds(column + 2 * k * width, width)] = sums[b]
        yield


def schur_kernel(cameras, pieces, got_ref, out_ref, *scratch):
    part, wide = 9 * cameras // pieces, 2 * got_ref.shape[4]
    sums = [pltpu.ACC(unit)((part, wide), jnp.float32) for unit in range(2) for _ in range(pieces)]
    pl.run_scoped(functools.partial(schur_body, cameras, got_ref, out_ref, *scratch), *sums)


def schur_body(cameras, got_ref, out_ref, rows_ref, left_a, left_b, right_a, right_b, *sums):
    sources = got_ref.shape[0]
    width = got_ref.shape[4]
    side = 9 * cameras
    lefts, rights = (left_a, left_b), (right_a, right_b)
    count = len(sums) // 2
    sums = (sums[:count], sums[count:])
    part = side // count
    wide = 2 * width
    for right in rights:
        right[pl.ds(side, 2 * wide - side), :] = jnp.zeros((2 * wide - side, 3 * wide), jnp.bfloat16)

    def expand(source, buffer):
        for slot in range(2):
            yield from expand_slot(
                got_ref, source, slot, rows_ref.at[slot], lefts[buffer], rights[buffer], slot * width, cameras,
            )

    def multiply(buffer):
        for k in range(3):
            columns = pl.ds(k * wide, wide)
            for unit in range(2):
                pltpu.matmul_push_rhs(
                    rights[buffer][pl.ds(unit * wide, wide), columns], k % 2, unit, transpose=True
                )
            for piece in range(count):
                value = lefts[buffer][pl.ds(piece * part, part), columns]
                for unit in range(2):
                    pltpu.matmul_acc_lhs(sums[unit][piece], value, k % 2 if piece == 0 else None)
                yield

    def both(source, buffer):
        one = expand(source, buffer)
        two = multiply(1 - buffer)
        each = -(-20 // (3 * count))
        steps, alive = 0, True
        while alive:
            alive = next(two, 1) is None
            steps += 20
            while steps >= 3 * count:
                steps -= 3 * count
                next(one, 1)
        for _ in one:
            pass

    for _ in expand(0, 0):
        pass

    def step(turn, carry):
        both(2 * turn + 1, 1)
        both(jnp.minimum(2 * turn + 2, sources - 1), 0)
        return carry

    lax.fori_loop(0, sources // 2, step, 0)
    for piece in range(count):
        rows = pl.ds(piece * part, part)
        out_ref[rows, 0:wide] = pltpu.matmul_pop(sums[0][piece])
        out_ref[rows, wide:side] = pltpu.matmul_pop(sums[1][piece])[:, : side - wide]


def schur_partial(got, cameras, shares):
    width = got.shape[4]
    side = 9 * cameras
    pieces = 9
    vmem = pl.BlockSpec(memory_space=pltpu.VMEM)
    out = pl.pallas_call(
        functools.partial(schur_kernel, cameras, pieces),
        out_shape=jax.ShapeDtypeStruct((side, side), jnp.float32),
        in_specs=[vmem],
        out_specs=vmem,
        scratch_shapes=[
            pltpu.VMEM((2, 28, 8, width), jnp.float32),
            pltpu.VMEM((side, 6 * width), jnp.bfloat16),
            pltpu.VMEM((side, 6 * width), jnp.bfloat16),
            pltpu.VMEM((4 * width, 6 * width), jnp.bfloat16),
            pltpu.VMEM((4 * width, 6 * width), jnp.bfloat16),
        ],
        compiler_params=pltpu.CompilerParams(vmem_limit_bytes=32 * 1024 * 1024),
        cost_estimate=pl.CostEstimate(flops=10000000000, bytes_accessed=3000000, transcendentals=0),
        name="schur_partial",
    )(got)
    return out.reshape(shares, side // shares, side)


def own_blocks(camera_blocks, share, share_rows):
    cameras = camera_blocks.shape[3]
    side = 9 * cameras
    row = share * share_rows + lax.broadcasted_iota(jnp.int32, (share_rows, side), 0)
    column = lax.broadcasted_iota(jnp.int32, (share_rows, side), 1)
    lines = camera_blocks[0].reshape(9, side)
    first = share * share_rows // cameras
    own = jnp.zeros((share_rows, side), jnp.float32)
    for step in range(-(-share_rows // cameras) + 1):
        line = lax.dynamic_slice_in_dim(lines, jnp.minimum(first + step, 8), 1, 0)
        own = jnp.where(row // cameras == first + step, line, own)
    return jnp.where(row % cameras == column % cameras, own, 0.0)


AXES = ("layer", "zp", "zb", "x", "pair")


def local(sizes, jac_blocks, point_blocks, visibility, obs_count, tile_count, route, camera_blocks):
    cameras = camera_blocks.shape[3]
    side = 9 * cameras
    layers, pairs, far, near, across = (lax.axis_size(a) for a in ("layer", "pair", "zp", "zb", "x"))
    shares = layers * pairs

    def site_of(group):
        return (group // across % near) * (across * pairs) + group % across * pairs + group // (across * near)

    packed = pack(
        jac_blocks.transpose(0, 2, 1, 3), point_blocks.transpose(1, 0, 2), visibility, obs_count, tile_count,
        route[:, 0], near * across * pairs, site_of,
    )
    got = lax.all_to_all(packed, ("zb", "x", "pair"), split_axis=0, concat_axis=0, tiled=True)
    partial_value = schur_partial(got, cameras, shares).reshape(layers, pairs, side // shares, side)
    layer, plane = lax.axis_index("layer"), lax.axis_index("zp")
    theirs = lax.dynamic_index_in_dim(partial_value, 1 - layer, 0, keepdims=False)
    ours = lax.dynamic_index_in_dim(partial_value, layer, 0, keepdims=False)
    ours = ours + lax.ppermute(theirs, "layer", [(0, 1), (1, 0)])
    total = None
    for turn in range(far):
        links = []
        for source in itertools.product(*(range(size) for size in sizes)):
            c, zp, zb, x, y = source
            links.append((flat(source, sizes), flat((c, y, zb, x, zp ^ turn), sizes)))
        piece = lax.dynamic_index_in_dim(ours, plane ^ turn, 0, keepdims=False)
        came = lax.ppermute(piece, AXES, links)
        total = came if total is None else total + came
    share = layer * pairs + lax.axis_index("pair")
    return (own_blocks(camera_blocks, share, side // shares) - total)[None]


def flat(place, sizes):
    index = 0
    for coordinate, size in zip(place, sizes):
        index = index * size + coordinate
    return index


def solution(mesh):
    layers, cams, pairs = mesh.devices.shape
    across = 4
    near = 2
    sizes = (layers, cams // (near * across), near, across, pairs)
    split = jax.sharding.Mesh(mesh.devices.reshape(sizes), AXES)
    cam = ("zp", "zb", "x")
    placed = (
        P(AXES, None, None, None),
        P(AXES, None, None),
        P(AXES, None, None),
        P(AXES, None),
        P(AXES),
        P(AXES, None),
        P(cam, None, None, None),
    )
    return jax.shard_map(
        functools.partial(local, sizes),
        mesh=split,
        in_specs=placed,
        out_specs=P(cam, ("layer", "pair"), None),
        check_vma=False,
    )
```

```python
import functools
import itertools

import jax
import jax.numpy as jnp
from jax import lax
from jax.experimental import pallas as pl
from jax.experimental.pallas import tpu as pltpu
from jax.sharding import PartitionSpec as P

GROUPS_OF_ROWS = 30


def pack_kernel(
    site_of, route_hbm, count_hbm, jac_hbm, block_hbm, vis_hbm, obs_hbm, out_ref,
    route_ref, count_ref, block_ref, vis_ref, obs_ref, block_scratch, fill_ref, small_sems, tile_sems,
):
    tiles = jac_hbm.shape[0]
    width = jac_hbm.shape[3]
    places = out_ref.shape[0]
    small = [
        pltpu.make_async_copy(source, target, small_sems.at[index])
        for index, (source, target) in enumerate((
            (route_hbm, route_ref), (count_hbm, count_ref), (block_hbm, block_ref),
            (vis_hbm, vis_ref), (obs_hbm, obs_ref),
        ))
    ]
    for copy in small:
        copy.start()
    dead = jnp.full((4, width), -1.0, jnp.bfloat16)

    def clear(place, carry):
        fill_ref[place] = 0
        out_ref[place, 0, 27] = dead
        out_ref[place, 1, 27] = dead
        return carry

    lax.fori_loop(0, places, clear, 0, unroll=8)
    small[0].wait()

    def send(tile, carry):
        place = site_of(route_ref[tile])
        slot = fill_ref[place]
        fill_ref[place] = slot + 1
        route_ref[tile] = 2 * place + slot
        pltpu.make_async_copy(
            jac_hbm.at[tile], out_ref.at[place, slot, pl.ds(0, 27)], tile_sems.at[tile]
        ).start()
        return carry

    lax.fori_loop(0, tiles, send, 0, unroll=4)
    for copy in small[1:]:
        copy.wait()
    block_scratch[...] = block_ref[...].astype(jnp.float32)
    slot_iota = lax.broadcasted_iota(jnp.int32, (4, width), 0)
    point_iota = lax.broadcasted_iota(jnp.int32, (4, width), 1)

    def fill(tile, carry):
        place = route_ref[tile] // 2
        slot = route_ref[tile] % 2
        obs = jnp.broadcast_to(obs_ref[pl.ds(tile, 1), :], (4, width))
        live = (slot_iota < obs) & (point_iota < count_ref[tile])
        marks = jnp.where(live, vis_ref[tile], -1).astype(jnp.float32).astype(jnp.bfloat16)
        rows = [block_scratch[c, pl.ds(tile, 1), :] for c in range(6)]
        zero = jnp.zeros_like(rows[0])
        out_ref[place, slot, 27] = marks
        out_ref[place, slot, 28] = jnp.concatenate(rows[:4], axis=0).astype(jnp.bfloat16)
        out_ref[place, slot, 29] = jnp.concatenate(rows[4:] + [zero, zero], axis=0).astype(jnp.bfloat16)
        return carry

    lax.fori_loop(0, tiles, fill, 0, unroll=4)

    def finish(tile, carry):
        pltpu.make_async_copy(jac_hbm.at[0], out_ref.at[0, 0, pl.ds(0, 27)], tile_sems.at[tile]).wait()
        return carry

    lax.fori_loop(0, tiles, finish, 0)


def pack(jac, blocks, vis, obs, counts, route, places, site_of):
    tiles, width = jac.shape[0], jac.shape[3]
    anywhere = pl.BlockSpec(memory_space=pltpu.HBM)
    return pl.pallas_call(
        functools.partial(pack_kernel, site_of),
        out_shape=jax.ShapeDtypeStruct((places, 2, GROUPS_OF_ROWS, 4, width), jnp.bfloat16),
        in_specs=[anywhere] * 6,
        out_specs=pl.BlockSpec(memory_space=pltpu.VMEM),
        scratch_shapes=[
            pltpu.SMEM(route.shape, jnp.int32),
            pltpu.SMEM(counts.shape, jnp.int32),
            pltpu.VMEM(blocks.shape, jnp.bfloat16),
            pltpu.VMEM(vis.shape, jnp.int32),
            pltpu.VMEM(obs.shape, jnp.int32),
            pltpu.VMEM(blocks.shape, jnp.float32),
            pltpu.SMEM((places,), jnp.int32),
            pltpu.SemaphoreType.DMA((5,)),
            pltpu.SemaphoreType.DMA((tiles,)),
        ],
        compiler_params=pltpu.CompilerParams(vmem_limit_bytes=24 * 1024 * 1024),
        cost_estimate=pl.CostEstimate(flops=1000000, bytes_accessed=3000000, transcendentals=0),
        name="pack",
    )(route, counts, jac, blocks, vis, obs)


def inverse_rows(first, second):
    xx, yy, zz, xy = (first[c : c + 1] for c in range(4))
    xz, yz = (second[c : c + 1] for c in range(2))
    cxx = yy * zz - yz * yz
    cyy = xx * zz - xz * xz
    czz = xx * yy - xy * xy
    cxy = xz * yz - xy * zz
    cxz = xy * yz - xz * yy
    cyz = xy * xz - xx * yz
    inv_det = 1.0 / (xx * cxx + xy * cxy + xz * cxz)
    ixx, iyy, izz, ixy, ixz, iyz = (c * inv_det for c in (cxx, cyy, czz, cxy, cxz, cyz))
    return ((ixx, ixy, ixz), (ixy, iyy, iyz), (ixz, iyz, izz))


def expand_slot(got_ref, source, slot, rows_ref, left_ref, right_ref, column, cameras):
    width = got_ref.shape[4]
    first = got_ref[source, slot, 28].astype(jnp.float32)
    second = got_ref[source, slot, 29].astype(jnp.float32)
    inverse = inverse_rows(first, second)
    wide = [[jnp.broadcast_to(entry, (4, width)) for entry in line] for line in inverse]
    for r in range(9):
        factors = [got_ref[source, slot, 3 * r + m].astype(jnp.float32) for m in range(3)]
        for k in range(3):
            value = factors[0] * wide[0][k] + factors[1] * wide[1][k] + factors[2] * wide[2][k]
            rows_ref[3 * r + k, 0:4] = value.astype(jnp.bfloat16).astype(jnp.float32)
            rows_ref[3 * r + k, 4:8] = factors[k]
    rows_ref[27, 0:4] = got_ref[source, slot, 27].astype(jnp.float32)
    blocks = cameras // 16
    iota = lax.broadcasted_iota(jnp.int32, (16, width), 0).astype(jnp.float32)
    masks = []
    for i in range(4):
        mark = jnp.broadcast_to(rows_ref[27, i : i + 1], (16, width)).astype(jnp.bfloat16)
        masks.append([mark == (iota + 16.0 * b).astype(jnp.bfloat16) for b in range(blocks)])
    zero = jnp.zeros((16, width), jnp.bfloat16)
    yield
    for r in range(9):
        for k in range(3):
            for side, out in ((0, left_ref), (4, right_ref)):
                sums = [zero] * blocks
                for i in range(4):
                    row = jnp.broadcast_to(rows_ref[3 * r + k, side + i : side + i + 1], (16, width))
                    row = row.astype(jnp.bfloat16)
                    sums = [jnp.where(masks[i][b], row, sums[b]) for b in range(blocks)]
                for b in range(blocks):
                    out[pl.ds(r * cameras + 16 * b, 16), pl.ds(column + 2 * k * width, width)] = sums[b]
        yield


def schur_kernel(cameras, pieces, got_ref, out_ref, *scratch):
    part, wide = 9 * cameras // pieces, 2 * got_ref.shape[4]
    sums = [pltpu.ACC(unit)((part, wide), jnp.float32) for unit in range(2) for _ in range(pieces)]
    pl.run_scoped(functools.partial(schur_body, cameras, got_ref, out_ref, *scratch), *sums)


def schur_body(cameras, got_ref, out_ref, rows_ref, left_a, left_b, right_a, right_b, *sums):
    sources = got_ref.shape[0]
    width = got_ref.shape[4]
    side = 9 * cameras
    lefts, rights = (left_a, left_b), (right_a, right_b)
    count = len(sums) // 2
    sums = (sums[:count], sums[count:])
    part = side // count
    wide = 2 * width
    for right in rights:
        right[pl.ds(side, 2 * wide - side), :] = jnp.zeros((2 * wide - side, 3 * wide), jnp.bfloat16)

    def expand(source, buffer):
        for slot in range(2):
            yield from expand_slot(
                got_ref, source, slot, rows_ref.at[slot], lefts[buffer], rights[buffer], slot * width, cameras,
            )

    def multiply(buffer):
        for k in range(3):
            columns = pl.ds(k * wide, wide)
            for unit in range(2):
                pltpu.matmul_push_rhs(
                    rights[buffer][pl.ds(unit * wide, wide), columns], k % 2, unit, transpose=True
                )
            for piece in range(count):
                value = lefts[buffer][pl.ds(piece * part, part), columns]
                for unit in range(2):
                    pltpu.matmul_acc_lhs(sums[unit][piece], value, k % 2 if piece == 0 else None)
                yield

    def both(source, buffer):
        one = expand(source, buffer)
        two = multiply(1 - buffer)
        each = -(-20 // (3 * count))
        steps, alive = 0, True
        while alive:
            alive = next(two, 1) is None
            steps += 20
            while steps >= 3 * count:
                steps -= 3 * count
                next(one, 1)
        for _ in one:
            pass

    for _ in expand(0, 0):
        pass

    def step(turn, carry):
        both(2 * turn + 1, 1)
        both(jnp.minimum(2 * turn + 2, sources - 1), 0)
        return carry

    lax.fori_loop(0, sources // 2, step, 0)
    for piece in range(count):
        rows = pl.ds(piece * part, part)
        out_ref[rows, 0:wide] = pltpu.matmul_pop(sums[0][piece])
        out_ref[rows, wide:side] = pltpu.matmul_pop(sums[1][piece])[:, : side - wide]


def schur_partial(got, cameras, shares):
    width = got.shape[4]
    side = 9 * cameras
    pieces = 9
    vmem = pl.BlockSpec(memory_space=pltpu.VMEM)
    out = pl.pallas_call(
        functools.partial(schur_kernel, cameras, pieces),
        out_shape=jax.ShapeDtypeStruct((side, side), jnp.float32),
        in_specs=[vmem],
        out_specs=vmem,
        scratch_shapes=[
            pltpu.VMEM((2, 28, 8, width), jnp.float32),
            pltpu.VMEM((side, 6 * width), jnp.bfloat16),
            pltpu.VMEM((side, 6 * width), jnp.bfloat16),
            pltpu.VMEM((4 * width, 6 * width), jnp.bfloat16),
            pltpu.VMEM((4 * width, 6 * width), jnp.bfloat16),
        ],
        compiler_params=pltpu.CompilerParams(vmem_limit_bytes=32 * 1024 * 1024),
        cost_estimate=pl.CostEstimate(flops=10000000000, bytes_accessed=3000000, transcendentals=0),
        name="schur_partial",
    )(got)
    return out.reshape(shares, side // shares, side)


def own_blocks(camera_blocks, share, share_rows):
    cameras = camera_blocks.shape[3]
    side = 9 * cameras
    row = share * share_rows + lax.broadcasted_iota(jnp.int32, (share_rows, side), 0)
    column = lax.broadcasted_iota(jnp.int32, (share_rows, side), 1)
    lines = camera_blocks[0].reshape(9, side)
    first = share * share_rows // cameras
    own = jnp.zeros((share_rows, side), jnp.float32)
    for step in range(-(-share_rows // cameras) + 1):
        line = lax.dynamic_slice_in_dim(lines, jnp.minimum(first + step, 8), 1, 0)
        own = jnp.where(row // cameras == first + step, line, own)
    return jnp.where(row % cameras == column % cameras, own, 0.0)


AXES = ("layer", "zp", "zb", "x", "pair")


def local(sizes, jac_blocks, point_blocks, visibility, obs_count, tile_count, route, camera_blocks):
    cameras = camera_blocks.shape[3]
    side = 9 * cameras
    layers, pairs, far, near, across = (lax.axis_size(a) for a in ("layer", "pair", "zp", "zb", "x"))
    shares = layers * pairs

    def site_of(group):
        side_z = group // across % near
        y = (group // (across * near) + 2 * lax.axis_index("zp") + 2 * side_z) % pairs
        return side_z * (across * pairs) + group % across * pairs + y

    packed = pack(
        jac_blocks.transpose(0, 2, 1, 3), point_blocks.transpose(1, 0, 2), visibility, obs_count, tile_count,
        route[:, 0], near * across * pairs, site_of,
    )
    got = lax.all_to_all(packed, ("zb", "x", "pair"), split_axis=0, concat_axis=0, tiled=True)
    partial_value = schur_partial(got, cameras, shares).reshape(layers, pairs, side // shares, side)
    layer, plane = lax.axis_index("layer"), lax.axis_index("zp")
    theirs = lax.dynamic_index_in_dim(partial_value, 1 - layer, 0, keepdims=False)
    ours = lax.dynamic_index_in_dim(partial_value, layer, 0, keepdims=False)
    ours = ours + lax.ppermute(theirs, "layer", [(0, 1), (1, 0)])
    total = None
    for turn in range(far):
        links = []
        for source in itertools.product(*(range(size) for size in sizes)):
            c, zp, zb, x, y = source
            links.append((flat(source, sizes), flat((c, (y + 2 * zp + 2 * zb) % far, zb, x, zp ^ turn), sizes)))
        piece = lax.dynamic_index_in_dim(ours, plane ^ turn, 0, keepdims=False)
        came = lax.ppermute(piece, AXES, links)
        total = came if total is None else total + came
    share = layer * pairs + lax.axis_index("pair")
    return (own_blocks(camera_blocks, share, side // shares) - total)[None]


def flat(place, sizes):
    index = 0
    for coordinate, size in zip(place, sizes):
        index = index * size + coordinate
    return index


def solution(mesh):
    layers, cams, pairs = mesh.devices.shape
    across = 4
    near = 2
    sizes = (layers, cams // (near * across), near, across, pairs)
    split = jax.sharding.Mesh(mesh.devices.reshape(sizes), AXES)
    cam = ("zp", "zb", "x")
    placed = (
        P(AXES, None, None, None),
        P(AXES, None, None),
        P(AXES, None, None),
        P(AXES, None),
        P(AXES),
        P(AXES, None),
        P(cam, None, None, None),
    )
    return jax.shard_map(
        functools.partial(local, sizes),
        mesh=split,
        in_specs=placed,
        out_specs=P(cam, ("layer", "pair"), None),
        check_vma=False,
    )
```

```python
import functools
import itertools

import jax
import jax.numpy as jnp
from jax import lax
from jax.experimental import pallas as pl
from jax.experimental.pallas import tpu as pltpu
from jax.sharding import PartitionSpec as P

GROUPS_OF_ROWS = 30


def pack_kernel(
    site_of, route_hbm, count_hbm, jac_hbm, block_hbm, vis_hbm, obs_hbm, out_ref,
    route_ref, count_ref, block_ref, vis_ref, obs_ref, block_scratch, fill_ref, small_sems, tile_sems,
):
    tiles = jac_hbm.shape[0]
    width = jac_hbm.shape[3]
    places = out_ref.shape[0]
    small = [
        pltpu.make_async_copy(source, target, small_sems.at[index])
        for index, (source, target) in enumerate((
            (route_hbm, route_ref), (count_hbm, count_ref), (block_hbm, block_ref),
            (vis_hbm, vis_ref), (obs_hbm, obs_ref),
        ))
    ]
    for copy in small:
        copy.start()
    dead = jnp.full((4, width), -1.0, jnp.bfloat16)

    def clear(place, carry):
        fill_ref[place] = 0
        out_ref[place, 0, 27] = dead
        out_ref[place, 1, 27] = dead
        return carry

    lax.fori_loop(0, places, clear, 0, unroll=8)
    small[0].wait()

    def send(tile, carry):
        place = site_of(route_ref[tile])
        slot = fill_ref[place]
        fill_ref[place] = slot + 1
        route_ref[tile] = 2 * place + slot
        pltpu.make_async_copy(
            jac_hbm.at[tile], out_ref.at[place, slot, pl.ds(0, 27)], tile_sems.at[tile]
        ).start()
        return carry

    lax.fori_loop(0, tiles, send, 0, unroll=4)
    for copy in small[1:]:
        copy.wait()
    block_scratch[...] = block_ref[...].astype(jnp.float32)
    slot_iota = lax.broadcasted_iota(jnp.int32, (4, width), 0)
    point_iota = lax.broadcasted_iota(jnp.int32, (4, width), 1)

    def fill(tile, carry):
        place = route_ref[tile] // 2
        slot = route_ref[tile] % 2
        obs = jnp.broadcast_to(obs_ref[pl.ds(tile, 1), :], (4, width))
        live = (slot_iota < obs) & (point_iota < count_ref[tile])
        marks = jnp.where(live, vis_ref[tile], -1).astype(jnp.float32).astype(jnp.bfloat16)
        rows = [block_scratch[c, pl.ds(tile, 1), :] for c in range(6)]
        zero = jnp.zeros_like(rows[0])
        out_ref[place, slot, 27] = marks
        out_ref[place, slot, 28] = jnp.concatenate(rows[:4], axis=0).astype(jnp.bfloat16)
        out_ref[place, slot, 29] = jnp.concatenate(rows[4:] + [zero, zero], axis=0).astype(jnp.bfloat16)
        return carry

    lax.fori_loop(0, tiles, fill, 0, unroll=4)

    def finish(tile, carry):
        pltpu.make_async_copy(jac_hbm.at[0], out_ref.at[0, 0, pl.ds(0, 27)], tile_sems.at[tile]).wait()
        return carry

    lax.fori_loop(0, tiles, finish, 0)


def pack(jac, blocks, vis, obs, counts, route, places, site_of):
    tiles, width = jac.shape[0], jac.shape[3]
    anywhere = pl.BlockSpec(memory_space=pltpu.HBM)
    return pl.pallas_call(
        functools.partial(pack_kernel, site_of),
        out_shape=jax.ShapeDtypeStruct((places, 2, GROUPS_OF_ROWS, 4, width), jnp.bfloat16),
        in_specs=[anywhere] * 6,
        out_specs=pl.BlockSpec(memory_space=pltpu.VMEM),
        scratch_shapes=[
            pltpu.SMEM(route.shape, jnp.int32),
            pltpu.SMEM(counts.shape, jnp.int32),
            pltpu.VMEM(blocks.shape, jnp.bfloat16),
            pltpu.VMEM(vis.shape, jnp.int32),
            pltpu.VMEM(obs.shape, jnp.int32),
            pltpu.VMEM(blocks.shape, jnp.float32),
            pltpu.SMEM((places,), jnp.int32),
            pltpu.SemaphoreType.DMA((5,)),
            pltpu.SemaphoreType.DMA((tiles,)),
        ],
        compiler_params=pltpu.CompilerParams(vmem_limit_bytes=60 * 1024 * 1024),
        cost_estimate=pl.CostEstimate(flops=1000000, bytes_accessed=3000000, transcendentals=0),
        name="pack",
    )(route, counts, jac, blocks, vis, obs)


def inverse_rows(first, second):
    xx, yy, zz, xy = (first[c : c + 1] for c in range(4))
    xz, yz = (second[c : c + 1] for c in range(2))
    cxx = yy * zz - yz * yz
    cyy = xx * zz - xz * xz
    czz = xx * yy - xy * xy
    cxy = xz * yz - xy * zz
    cxz = xy * yz - xz * yy
    cyz = xy * xz - xx * yz
    inv_det = 1.0 / (xx * cxx + xy * cxy + xz * cxz)
    ixx, iyy, izz, ixy, ixz, iyz = (c * inv_det for c in (cxx, cyy, czz, cxy, cxz, cyz))
    return ((ixx, ixy, ixz), (ixy, iyy, iyz), (ixz, iyz, izz))


def expand_slot(got_ref, source, slot, rows_ref, left_ref, right_ref, column, cameras):
    width = got_ref.shape[4]
    first = got_ref[source, slot, 28].astype(jnp.float32)
    second = got_ref[source, slot, 29].astype(jnp.float32)
    inverse = inverse_rows(first, second)
    wide = [[jnp.broadcast_to(entry, (4, width)) for entry in line] for line in inverse]
    rows_ref[27, 0, 0:4] = got_ref[source, slot, 27].astype(jnp.float32)
    iota = lax.broadcasted_iota(jnp.int32, (8, width), 0).astype(jnp.float32)
    marks = [jnp.broadcast_to(rows_ref[27, 0, i : i + 1], (8, width)) for i in range(4)]
    picks = []
    for b in range(cameras // 8):
        pick = jnp.full((8, width), 4, jnp.int32)
        for i in range(4):
            pick = jnp.where(marks[i] == iota + 8.0 * b, i, pick)
        picks.append(pick)
    yield
    for r in range(9):
        factors = [got_ref[source, slot, 3 * r + m].astype(jnp.float32) for m in range(3)]
        for k in range(3):
            value = factors[0] * wide[0][k] + factors[1] * wide[1][k] + factors[2] * wide[2][k]
            rows_ref[3 * r + k, 0, 0:4] = value
            rows_ref[3 * r + k, 1, 0:4] = factors[k]
        for k in range(3):
            for side, out in enumerate((left_ref, right_ref)):
                table = rows_ref[3 * r + k, side]
                for b in range(0, cameras // 8, 2):
                    pair = [
                        jnp.take_along_axis(table, picks[b + half], axis=0, mode="promise_in_bounds")
                        for half in range(2)
                    ]
                    out[pl.ds(r * cameras + 8 * b, 16), pl.ds(column + 2 * k * width, width)] = jnp.concatenate(
                        pair, axis=0
                    ).astype(jnp.bfloat16)
        yield


def schur_kernel(cameras, pieces, got_ref, out_ref, *scratch):
    part, wide = 9 * cameras // pieces, 2 * got_ref.shape[4]
    sums = [pltpu.ACC(unit)((part, wide), jnp.float32) for unit in range(2) for _ in range(pieces)]
    pl.run_scoped(functools.partial(schur_body, cameras, got_ref, out_ref, *scratch), *sums)


def schur_body(cameras, got_ref, out_ref, rows_ref, left_a, left_b, right_a, right_b, *sums):
    sources = got_ref.shape[0]
    width = got_ref.shape[4]
    side = 9 * cameras
    lefts, rights = (left_a, left_b), (right_a, right_b)
    count = len(sums) // 2
    sums = (sums[:count], sums[count:])
    part = side // count
    wide = 2 * width
    rows_ref[...] = jnp.zeros_like(rows_ref)
    for right in rights:
        right[pl.ds(side, 2 * wide - side), :] = jnp.zeros((2 * wide - side, 3 * wide), jnp.bfloat16)

    def expand(source, buffer):
        for slot in range(2):
            yield from expand_slot(
                got_ref, source, slot, rows_ref.at[slot], lefts[buffer], rights[buffer], slot * width, cameras,
            )

    def multiply(buffer):
        for k in range(3):
            columns = pl.ds(k * wide, wide)
            for unit in range(2):
                pltpu.matmul_push_rhs(
                    rights[buffer][pl.ds(unit * wide, wide), columns], k % 2, unit, transpose=True
                )
            for piece in range(count):
                value = lefts[buffer][pl.ds(piece * part, part), columns]
                for unit in range(2):
                    pltpu.matmul_acc_lhs(sums[unit][piece], value, k % 2 if piece == 0 else None)
                yield

    def both(source, buffer):
        one = expand(source, buffer)
        two = multiply(1 - buffer)
        each = -(-20 // (3 * count))
        steps, alive = 0, True
        while alive:
            alive = next(two, 1) is None
            steps += 20
            while steps >= 3 * count:
                steps -= 3 * count
                next(one, 1)
        for _ in one:
            pass

    for _ in expand(0, 0):
        pass

    def step(turn, carry):
        both(2 * turn + 1, 1)
        both(jnp.minimum(2 * turn + 2, sources - 1), 0)
        return carry

    lax.fori_loop(0, sources // 2, step, 0)
    for piece in range(count):
        rows = pl.ds(piece * part, part)
        out_ref[rows, 0:wide] = pltpu.matmul_pop(sums[0][piece])
        out_ref[rows, wide:side] = pltpu.matmul_pop(sums[1][piece])[:, : side - wide]


def schur_partial(got, cameras, shares):
    width = got.shape[4]
    side = 9 * cameras
    pieces = 9
    vmem = pl.BlockSpec(memory_space=pltpu.VMEM)
    out = pl.pallas_call(
        functools.partial(schur_kernel, cameras, pieces),
        out_shape=jax.ShapeDtypeStruct((side, side), jnp.float32),
        in_specs=[vmem],
        out_specs=vmem,
        scratch_shapes=[
            pltpu.VMEM((2, 28, 2, 8, width), jnp.float32),
            pltpu.VMEM((side, 6 * width), jnp.bfloat16),
            pltpu.VMEM((side, 6 * width), jnp.bfloat16),
            pltpu.VMEM((4 * width, 6 * width), jnp.bfloat16),
            pltpu.VMEM((4 * width, 6 * width), jnp.bfloat16),
        ],
        compiler_params=pltpu.CompilerParams(vmem_limit_bytes=32 * 1024 * 1024),
        cost_estimate=pl.CostEstimate(flops=10000000000, bytes_accessed=3000000, transcendentals=0),
        name="schur_partial",
    )(got)
    return out.reshape(shares, side // shares, side)


def own_blocks(camera_blocks, share, share_rows):
    cameras = camera_blocks.shape[3]
    side = 9 * cameras
    row = share * share_rows + lax.broadcasted_iota(jnp.int32, (share_rows, side), 0)
    column = lax.broadcasted_iota(jnp.int32, (share_rows, side), 1)
    lines = camera_blocks[0].reshape(9, side)
    first = share * share_rows // cameras
    own = jnp.zeros((share_rows, side), jnp.float32)
    for step in range(-(-share_rows // cameras) + 1):
        line = lax.dynamic_slice_in_dim(lines, jnp.minimum(first + step, 8), 1, 0)
        own = jnp.where(row // cameras == first + step, line, own)
    return jnp.where(row % cameras == column % cameras, own, 0.0)


AXES = ("layer", "zp", "zb", "x", "pair")


def local(sizes, jac_blocks, point_blocks, visibility, obs_count, tile_count, route, camera_blocks):
    cameras = camera_blocks.shape[3]
    side = 9 * cameras
    layers, pairs, far, near, across = (lax.axis_size(a) for a in ("layer", "pair", "zp", "zb", "x"))
    shares = layers * pairs

    def site_of(group):
        side_z = group // across % near
        y = (group // (across * near) + 2 * lax.axis_index("zp") + 2 * side_z) % pairs
        return side_z * (across * pairs) + group % across * pairs + y

    packed = pack(
        jac_blocks.transpose(0, 2, 1, 3), point_blocks.transpose(1, 0, 2), visibility, obs_count, tile_count,
        route[:, 0], near * across * pairs, site_of,
    )
    got = lax.all_to_all(packed, ("zb", "x", "pair"), split_axis=0, concat_axis=0, tiled=True)
    partial_value = schur_partial(got, cameras, shares).reshape(layers, pairs, side // shares, side)
    layer, plane = lax.axis_index("layer"), lax.axis_index("zp")
    theirs = lax.dynamic_index_in_dim(partial_value, 1 - layer, 0, keepdims=False)
    ours = lax.dynamic_index_in_dim(partial_value, layer, 0, keepdims=False)
    ours = ours + lax.ppermute(theirs, "layer", [(0, 1), (1, 0)])
    total = None
    for turn in range(far):
        links = []
        for source in itertools.product(*(range(size) for size in sizes)):
            c, zp, zb, x, y = source
            links.append((flat(source, sizes), flat((c, (y + 2 * zp + 2 * zb) % far, zb, x, zp ^ turn), sizes)))
        piece = lax.dynamic_index_in_dim(ours, plane ^ turn, 0, keepdims=False)
        came = lax.ppermute(piece, AXES, links)
        total = came if total is None else total + came
    share = layer * pairs + lax.axis_index("pair")
    return (own_blocks(camera_blocks, share, side // shares) - total)[None]


def flat(place, sizes):
    index = 0
    for coordinate, size in zip(place, sizes):
        index = index * size + coordinate
    return index


def solution(mesh):
    layers, cams, pairs = mesh.devices.shape
    across = 4
    near = 2
    sizes = (layers, cams // (near * across), near, across, pairs)
    split = jax.sharding.Mesh(mesh.devices.reshape(sizes), AXES)
    cam = ("zp", "zb", "x")
    placed = (
        P(AXES, None, None, None),
        P(AXES, None, None),
        P(AXES, None, None),
        P(AXES, None),
        P(AXES),
        P(AXES, None),
        P(cam, None, None, None),
    )
    return jax.shard_map(
        functools.partial(local, sizes),
        mesh=split,
        in_specs=placed,
        out_specs=P(cam, ("layer", "pair"), None),
        check_vma=False,
    )
```

```python
import functools
import itertools

import jax
import jax.numpy as jnp
from jax import lax
from jax.experimental import pallas as pl
from jax.experimental.pallas import tpu as pltpu
from jax.sharding import PartitionSpec as P

GROUPS_OF_ROWS = 30


def pack_kernel(
    site_of, route_hbm, count_hbm, jac_hbm, block_hbm, vis_hbm, obs_hbm, out_ref,
    route_ref, count_ref, block_ref, vis_ref, obs_ref, block_scratch, fill_ref, small_sems, tile_sems,
):
    tiles = jac_hbm.shape[0]
    width = jac_hbm.shape[3]
    places = out_ref.shape[0]
    small = [
        pltpu.make_async_copy(source, target, small_sems.at[index])
        for index, (source, target) in enumerate((
            (route_hbm, route_ref), (count_hbm, count_ref), (block_hbm, block_ref),
            (vis_hbm, vis_ref), (obs_hbm, obs_ref),
        ))
    ]
    for copy in small:
        copy.start()
    dead = jnp.full((4, width), -1.0, jnp.bfloat16)

    def clear(place, carry):
        fill_ref[place] = 0
        out_ref[place, 0, 27] = dead
        out_ref[place, 1, 27] = dead
        return carry

    lax.fori_loop(0, places, clear, 0, unroll=8)
    small[0].wait()

    def send(tile, carry):
        place = site_of(route_ref[tile])
        slot = fill_ref[place]
        fill_ref[place] = slot + 1
        route_ref[tile] = 2 * place + slot
        pltpu.make_async_copy(
            jac_hbm.at[tile], out_ref.at[place, slot, pl.ds(0, 27)], tile_sems.at[tile]
        ).start()
        return carry

    lax.fori_loop(0, tiles, send, 0, unroll=4)
    for copy in small[1:]:
        copy.wait()
    block_scratch[...] = block_ref[...].astype(jnp.float32)
    slot_iota = lax.broadcasted_iota(jnp.int32, (4, width), 0)
    point_iota = lax.broadcasted_iota(jnp.int32, (4, width), 1)

    def fill(tile, carry):
        place = route_ref[tile] // 2
        slot = route_ref[tile] % 2
        obs = jnp.broadcast_to(obs_ref[pl.ds(tile, 1), :], (4, width))
        live = (slot_iota < obs) & (point_iota < count_ref[tile])
        marks = jnp.where(live, vis_ref[tile], -1).astype(jnp.float32).astype(jnp.bfloat16)
        rows = [block_scratch[c, pl.ds(tile, 1), :] for c in range(6)]
        zero = jnp.zeros_like(rows[0])
        out_ref[place, slot, 27] = marks
        out_ref[place, slot, 28] = jnp.concatenate(rows[:4], axis=0).astype(jnp.bfloat16)
        out_ref[place, slot, 29] = jnp.concatenate(rows[4:] + [zero, zero], axis=0).astype(jnp.bfloat16)
        return carry

    lax.fori_loop(0, tiles, fill, 0, unroll=4)

    def finish(tile, carry):
        pltpu.make_async_copy(jac_hbm.at[0], out_ref.at[0, 0, pl.ds(0, 27)], tile_sems.at[tile]).wait()
        return carry

    lax.fori_loop(0, tiles, finish, 0)


def pack(jac, blocks, vis, obs, counts, route, places, site_of):
    tiles, width = jac.shape[0], jac.shape[3]
    anywhere = pl.BlockSpec(memory_space=pltpu.HBM)
    return pl.pallas_call(
        functools.partial(pack_kernel, site_of),
        out_shape=jax.ShapeDtypeStruct((places, 2, GROUPS_OF_ROWS, 4, width), jnp.bfloat16),
        in_specs=[anywhere] * 6,
        out_specs=pl.BlockSpec(memory_space=pltpu.VMEM),
        scratch_shapes=[
            pltpu.SMEM(route.shape, jnp.int32),
            pltpu.SMEM(counts.shape, jnp.int32),
            pltpu.VMEM(blocks.shape, jnp.bfloat16),
            pltpu.VMEM(vis.shape, jnp.int32),
            pltpu.VMEM(obs.shape, jnp.int32),
            pltpu.VMEM(blocks.shape, jnp.float32),
            pltpu.SMEM((places,), jnp.int32),
            pltpu.SemaphoreType.DMA((5,)),
            pltpu.SemaphoreType.DMA((tiles,)),
        ],
        compiler_params=pltpu.CompilerParams(vmem_limit_bytes=60 * 1024 * 1024),
        cost_estimate=pl.CostEstimate(flops=1000000, bytes_accessed=3000000, transcendentals=0),
        name="pack",
    )(route, counts, jac, blocks, vis, obs)


def inverse_rows(first, second):
    xx, yy, zz, xy = (first[c : c + 1] for c in range(4))
    xz, yz = (second[c : c + 1] for c in range(2))
    cxx = yy * zz - yz * yz
    cyy = xx * zz - xz * xz
    czz = xx * yy - xy * xy
    cxy = xz * yz - xy * zz
    cxz = xy * yz - xz * yy
    cyz = xy * xz - xx * yz
    inv_det = 1.0 / (xx * cxx + xy * cxy + xz * cxz)
    ixx, iyy, izz, ixy, ixz, iyz = (c * inv_det for c in (cxx, cyy, czz, cxy, cxz, cyz))
    return ((ixx, ixy, ixz), (ixy, iyy, iyz), (ixz, iyz, izz))


def expand_slot(got_ref, source, slot, rows_ref, left_ref, right_ref, column, cameras):
    width = got_ref.shape[4]
    first = got_ref[source, slot, 28].astype(jnp.float32)
    second = got_ref[source, slot, 29].astype(jnp.float32)
    inverse = inverse_rows(first, second)
    wide = [[jnp.broadcast_to(entry, (4, width)) for entry in line] for line in inverse]
    rows_ref[27, 0, 0:4] = got_ref[source, slot, 27].astype(jnp.float32)
    iota = lax.broadcasted_iota(jnp.int32, (8, width), 0).astype(jnp.float32)
    marks = [jnp.broadcast_to(rows_ref[27, 0, i : i + 1], (8, width)) for i in range(4)]
    picks = []
    for b in range(cameras // 8):
        pick = jnp.full((8, width), 4, jnp.int32)
        for i in range(4):
            pick = jnp.where(marks[i] == iota + 8.0 * b, i, pick)
        picks.append(pick)
    yield
    for r in range(9):
        factors = [got_ref[source, slot, 3 * r + m].astype(jnp.float32) for m in range(3)]
        values = [
            factors[0] * wide[0][k] + factors[1] * wide[1][k] + factors[2] * wide[2][k] for k in range(3)
        ]
        for k in range(3):
            for value, out in ((values[k], left_ref), (factors[k], right_ref)):
                table = jnp.concatenate([value, jnp.zeros_like(value)], axis=0)
                for b in range(0, cameras // 8, 2):
                    pair = [
                        jnp.take_along_axis(table, picks[b + half], axis=0, mode="promise_in_bounds")
                        for half in range(2)
                    ]
                    out[pl.ds(r * cameras + 8 * b, 16), pl.ds(column + 2 * k * width, width)] = jnp.concatenate(
                        pair, axis=0
                    ).astype(jnp.bfloat16)
        yield


def schur_kernel(cameras, pieces, got_ref, out_ref, *scratch):
    part, wide = 9 * cameras // pieces, 2 * got_ref.shape[4]
    sums = [pltpu.ACC(unit)((part, wide), jnp.float32) for unit in range(2) for _ in range(pieces)]
    pl.run_scoped(functools.partial(schur_body, cameras, got_ref, out_ref, *scratch), *sums)


def schur_body(cameras, got_ref, out_ref, rows_ref, left_a, left_b, right_a, right_b, *sums):
    sources = got_ref.shape[0]
    width = got_ref.shape[4]
    side = 9 * cameras
    lefts, rights = (left_a, left_b), (right_a, right_b)
    count = len(sums) // 2
    sums = (sums[:count], sums[count:])
    part = side // count
    wide = 2 * width
    rows_ref[...] = jnp.zeros_like(rows_ref)
    for right in rights:
        right[pl.ds(side, 2 * wide - side), :] = jnp.zeros((2 * wide - side, 3 * wide), jnp.bfloat16)

    def expand(source, buffer):
        for slot in range(2):
            yield from expand_slot(
                got_ref, source, slot, rows_ref.at[slot], lefts[buffer], rights[buffer], slot * width, cameras,
            )

    def multiply(buffer):
        for k in range(3):
            columns = pl.ds(k * wide, wide)
            for unit in range(2):
                pltpu.matmul_push_rhs(
                    rights[buffer][pl.ds(unit * wide, wide), columns], k % 2, unit, transpose=True
                )
            for piece in range(count):
                value = lefts[buffer][pl.ds(piece * part, part), columns]
                for unit in range(2):
                    pltpu.matmul_acc_lhs(sums[unit][piece], value, k % 2 if piece == 0 else None)
                yield

    def both(source, buffer):
        one = expand(source, buffer)
        two = multiply(1 - buffer)
        each = -(-20 // (3 * count))
        steps, alive = 0, True
        while alive:
            alive = next(two, 1) is None
            steps += 20
            while steps >= 3 * count:
                steps -= 3 * count
                next(one, 1)
        for _ in one:
            pass

    for _ in expand(0, 0):
        pass

    def step(turn, carry):
        both(2 * turn + 1, 1)
        both(jnp.minimum(2 * turn + 2, sources - 1), 0)
        return carry

    lax.fori_loop(0, sources // 2, step, 0)
    for piece in range(count):
        rows = pl.ds(piece * part, part)
        out_ref[rows, 0:wide] = pltpu.matmul_pop(sums[0][piece])
        out_ref[rows, wide:side] = pltpu.matmul_pop(sums[1][piece])[:, : side - wide]


def schur_partial(got, cameras, shares):
    width = got.shape[4]
    side = 9 * cameras
    pieces = 9
    vmem = pl.BlockSpec(memory_space=pltpu.VMEM)
    out = pl.pallas_call(
        functools.partial(schur_kernel, cameras, pieces),
        out_shape=jax.ShapeDtypeStruct((side, side), jnp.float32),
        in_specs=[vmem],
        out_specs=vmem,
        scratch_shapes=[
            pltpu.VMEM((2, 28, 2, 8, width), jnp.float32),
            pltpu.VMEM((side, 6 * width), jnp.bfloat16),
            pltpu.VMEM((side, 6 * width), jnp.bfloat16),
            pltpu.VMEM((4 * width, 6 * width), jnp.bfloat16),
            pltpu.VMEM((4 * width, 6 * width), jnp.bfloat16),
        ],
        compiler_params=pltpu.CompilerParams(vmem_limit_bytes=32 * 1024 * 1024),
        cost_estimate=pl.CostEstimate(flops=10000000000, bytes_accessed=3000000, transcendentals=0),
        name="schur_partial",
    )(got)
    return out.reshape(shares, side // shares, side)


def own_blocks(camera_blocks, share, share_rows):
    cameras = camera_blocks.shape[3]
    side = 9 * cameras
    row = share * share_rows + lax.broadcasted_iota(jnp.int32, (share_rows, side), 0)
    column = lax.broadcasted_iota(jnp.int32, (share_rows, side), 1)
    lines = camera_blocks[0].reshape(9, side)
    first = share * share_rows // cameras
    own = jnp.zeros((share_rows, side), jnp.float32)
    for step in range(-(-share_rows // cameras) + 1):
        line = lax.dynamic_slice_in_dim(lines, jnp.minimum(first + step, 8), 1, 0)
        own = jnp.where(row // cameras == first + step, line, own)
    return jnp.where(row % cameras == column % cameras, own, 0.0)


AXES = ("layer", "zp", "zb", "x", "pair")


def local(sizes, jac_blocks, point_blocks, visibility, obs_count, tile_count, route, camera_blocks):
    cameras = camera_blocks.shape[3]
    side = 9 * cameras
    layers, pairs, far, near, across = (lax.axis_size(a) for a in ("layer", "pair", "zp", "zb", "x"))
    shares = layers * pairs

    def site_of(group):
        side_z = group // across % near
        y = (group // (across * near) + pairs - lax.axis_index("zp") + 2 * side_z) % pairs
        return side_z * (across * pairs) + group % across * pairs + y

    packed = pack(
        jac_blocks.transpose(0, 2, 1, 3), point_blocks.transpose(1, 0, 2), visibility, obs_count, tile_count,
        route[:, 0], near * across * pairs, site_of,
    )
    got = lax.all_to_all(packed, ("zb", "x", "pair"), split_axis=0, concat_axis=0, tiled=True)
    partial_value = schur_partial(got, cameras, shares).reshape(layers, pairs, side // shares, side)
    layer, row = lax.axis_index("layer"), lax.axis_index("pair")
    theirs = lax.dynamic_index_in_dim(partial_value, 1 - layer, 0, keepdims=False)
    ours = lax.dynamic_index_in_dim(partial_value, layer, 0, keepdims=False)
    ours = ours + lax.ppermute(theirs, "layer", [(0, 1), (1, 0)])
    total = None
    for turn in range(far):
        links = []
        for source in itertools.product(*(range(size) for size in sizes)):
            c, zp, zb, x, y = source
            links.append((flat(source, sizes), flat((c, (y + zp + 2 * zb) % far, zb, x, y ^ turn), sizes)))
        piece = lax.dynamic_slice_in_dim(ours, row ^ turn, 1, 0)
        came = lax.ppermute(piece, AXES, links)
        total = came if total is None else total + came
    share = layer * pairs + row
    return own_blocks(camera_blocks, share, side // shares)[None] - total


def flat(place, sizes):
    index = 0
    for coordinate, size in zip(place, sizes):
        index = index * size + coordinate
    return index


def solution(mesh):
    layers, cams, pairs = mesh.devices.shape
    across = 4
    near = 2
    sizes = (layers, cams // (near * across), near, across, pairs)
    split = jax.sharding.Mesh(mesh.devices.reshape(sizes), AXES)
    cam = ("zp", "zb", "x")
    placed = (
        P(AXES, None, None, None),
        P(AXES, None, None),
        P(AXES, None, None),
        P(AXES, None),
        P(AXES),
        P(AXES, None),
        P(cam, None, None, None),
    )
    return jax.shard_map(
        functools.partial(local, sizes),
        mesh=split,
        in_specs=placed,
        out_specs=P(cam, ("layer", "pair"), None),
        check_vma=False,
    )
```

```python
import functools
import itertools

import jax
import jax.numpy as jnp
from jax import lax
from jax.experimental import pallas as pl
from jax.experimental.pallas import tpu as pltpu
from jax.sharding import PartitionSpec as P

GROUPS_OF_ROWS = 30


def pack_kernel(
    site_of, route_hbm, count_hbm, jac_hbm, block_hbm, vis_hbm, obs_hbm, out_ref,
    route_ref, count_ref, block_ref, vis_ref, obs_ref, block_scratch, fill_ref, small_sems, tile_sems,
):
    tiles = jac_hbm.shape[0]
    width = jac_hbm.shape[3]
    places = out_ref.shape[0]
    small = [
        pltpu.make_async_copy(source, target, small_sems.at[index])
        for index, (source, target) in enumerate((
            (route_hbm, route_ref), (count_hbm, count_ref), (block_hbm, block_ref),
            (vis_hbm, vis_ref), (obs_hbm, obs_ref),
        ))
    ]
    for copy in small:
        copy.start()
    dead = jnp.full((4, width), -1.0, jnp.bfloat16)

    def clear(place, carry):
        fill_ref[place] = 0
        out_ref[place, 0, 27] = dead
        out_ref[place, 1, 27] = dead
        return carry

    lax.fori_loop(0, places, clear, 0, unroll=8)
    small[0].wait()

    def send(tile, carry):
        place = site_of(route_ref[tile])
        slot = fill_ref[place]
        fill_ref[place] = slot + 1
        route_ref[tile] = 2 * place + slot
        pltpu.make_async_copy(
            jac_hbm.at[tile], out_ref.at[place, slot, pl.ds(0, 27)], tile_sems.at[tile]
        ).start()
        return carry

    lax.fori_loop(0, tiles, send, 0, unroll=4)
    for copy in small[1:]:
        copy.wait()
    block_scratch[...] = block_ref[...].astype(jnp.float32)
    slot_iota = lax.broadcasted_iota(jnp.int32, (4, width), 0)
    point_iota = lax.broadcasted_iota(jnp.int32, (4, width), 1)

    def fill(tile, carry):
        place = route_ref[tile] // 2
        slot = route_ref[tile] % 2
        obs = jnp.broadcast_to(obs_ref[pl.ds(tile, 1), :], (4, width))
        live = (slot_iota < obs) & (point_iota < count_ref[tile])
        marks = jnp.where(live, vis_ref[tile], -1).astype(jnp.float32).astype(jnp.bfloat16)
        rows = [block_scratch[c, pl.ds(tile, 1), :] for c in range(6)]
        zero = jnp.zeros_like(rows[0])
        out_ref[place, slot, 27] = marks
        out_ref[place, slot, 28] = jnp.concatenate(rows[:4], axis=0).astype(jnp.bfloat16)
        out_ref[place, slot, 29] = jnp.concatenate(rows[4:] + [zero, zero], axis=0).astype(jnp.bfloat16)
        return carry

    lax.fori_loop(0, tiles, fill, 0, unroll=4)

    def finish(tile, carry):
        pltpu.make_async_copy(jac_hbm.at[0], out_ref.at[0, 0, pl.ds(0, 27)], tile_sems.at[tile]).wait()
        return carry

    lax.fori_loop(0, tiles, finish, 0)


def pack(jac, blocks, vis, obs, counts, route, places, site_of):
    tiles, width = jac.shape[0], jac.shape[3]
    anywhere = pl.BlockSpec(memory_space=pltpu.HBM)
    return pl.pallas_call(
        functools.partial(pack_kernel, site_of),
        out_shape=jax.ShapeDtypeStruct((places, 2, GROUPS_OF_ROWS, 4, width), jnp.bfloat16),
        in_specs=[anywhere] * 6,
        out_specs=pl.BlockSpec(memory_space=pltpu.VMEM),
        scratch_shapes=[
            pltpu.SMEM(route.shape, jnp.int32),
            pltpu.SMEM(counts.shape, jnp.int32),
            pltpu.VMEM(blocks.shape, jnp.bfloat16),
            pltpu.VMEM(vis.shape, jnp.int32),
            pltpu.VMEM(obs.shape, jnp.int32),
            pltpu.VMEM(blocks.shape, jnp.float32),
            pltpu.SMEM((places,), jnp.int32),
            pltpu.SemaphoreType.DMA((5,)),
            pltpu.SemaphoreType.DMA((tiles,)),
        ],
        compiler_params=pltpu.CompilerParams(vmem_limit_bytes=60 * 1024 * 1024),
        cost_estimate=pl.CostEstimate(flops=1000000, bytes_accessed=3000000, transcendentals=0),
        name="pack",
    )(route, counts, jac, blocks, vis, obs)


def inverse_rows(first, second):
    xx, yy, zz, xy = (first[c : c + 1] for c in range(4))
    xz, yz = (second[c : c + 1] for c in range(2))
    cxx = yy * zz - yz * yz
    cyy = xx * zz - xz * xz
    czz = xx * yy - xy * xy
    cxy = xz * yz - xy * zz
    cxz = xy * yz - xz * yy
    cyz = xy * xz - xx * yz
    inv_det = 1.0 / (xx * cxx + xy * cxy + xz * cxz)
    ixx, iyy, izz, ixy, ixz, iyz = (c * inv_det for c in (cxx, cyy, czz, cxy, cxz, cyz))
    return ((ixx, ixy, ixz), (ixy, iyy, iyz), (ixz, iyz, izz))


def expand_slot(got_ref, source, slot, rows_ref, left_ref, right_ref, column, cameras):
    width = got_ref.shape[4]
    first = got_ref[source, slot, 28].astype(jnp.float32)
    second = got_ref[source, slot, 29].astype(jnp.float32)
    inverse = inverse_rows(first, second)
    wide = [[jnp.broadcast_to(entry, (4, width)) for entry in line] for line in inverse]
    rows_ref[27, 0, 0:4] = got_ref[source, slot, 27].astype(jnp.float32)
    iota = lax.broadcasted_iota(jnp.int32, (8, width), 0).astype(jnp.float32)
    marks = [jnp.broadcast_to(rows_ref[27, 0, i : i + 1], (8, width)) for i in range(4)]
    picks = []
    for b in range(cameras // 8):
        pick = jnp.full((8, width), 4, jnp.int32)
        for i in range(4):
            pick = jnp.where(marks[i] == iota + 8.0 * b, i, pick)
        picks.append(pick)
    yield
    for r in range(9):
        factors = [got_ref[source, slot, 3 * r + m].astype(jnp.float32) for m in range(3)]
        values = [
            factors[0] * wide[0][k] + factors[1] * wide[1][k] + factors[2] * wide[2][k] for k in range(3)
        ]
        for k in range(3):
            for value, out in ((values[k], left_ref), (factors[k], right_ref)):
                table = jnp.concatenate([value, jnp.zeros_like(value)], axis=0)
                for b in range(0, cameras // 8, 2):
                    pair = [
                        jnp.take_along_axis(table, picks[b + half], axis=0, mode="promise_in_bounds")
                        for half in range(2)
                    ]
                    out[pl.ds(r * cameras + 8 * b, 16), pl.ds(column + 2 * k * width, width)] = jnp.concatenate(
                        pair, axis=0
                    ).astype(jnp.bfloat16)
        yield


def schur_kernel(cameras, pieces, got_ref, out_ref, *scratch):
    part, wide = 9 * cameras // pieces, 2 * got_ref.shape[4]
    sums = [pltpu.ACC(unit)((part, wide), jnp.float32) for unit in range(2) for _ in range(pieces)]
    pl.run_scoped(functools.partial(schur_body, cameras, got_ref, out_ref, *scratch), *sums)


def schur_body(cameras, got_ref, out_ref, total_ref, rows_ref, left_a, left_b, right_a, right_b, *sums):
    sources = got_ref.shape[0]
    width = got_ref.shape[4]
    side = 9 * cameras
    lefts, rights = (left_a, left_b), (right_a, right_b)
    count = len(sums) // 2
    sums = (sums[:count], sums[count:])
    part = side // count
    wide = 2 * width
    rows_ref[...] = jnp.zeros_like(rows_ref)
    for right in rights:
        right[pl.ds(side, 2 * wide - side), :] = jnp.zeros((2 * wide - side, 3 * wide), jnp.bfloat16)

    def expand(source, buffer):
        for slot in range(2):
            yield from expand_slot(
                got_ref, source, slot, rows_ref.at[slot], lefts[buffer], rights[buffer], slot * width, cameras,
            )

    def multiply(buffer):
        for k in range(3):
            columns = pl.ds(k * wide, wide)
            for unit in range(2):
                pltpu.matmul_push_rhs(
                    rights[buffer][pl.ds(unit * wide, wide), columns], k % 2, unit, transpose=True
                )
            for piece in range(count):
                value = lefts[buffer][pl.ds(piece * part, part), columns]
                for unit in range(2):
                    pltpu.matmul_acc_lhs(sums[unit][piece], value, k % 2 if piece == 0 else None)
                yield

    def both(source, buffer):
        one = expand(source, buffer)
        two = multiply(1 - buffer)
        each = -(-20 // (3 * count))
        steps, alive = 0, True
        while alive:
            alive = next(two, 1) is None
            steps += 20
            while steps >= 3 * count:
                steps -= 3 * count
                next(one, 1)
        for _ in one:
            pass

    for _ in expand(0, 0):
        pass

    def step(turn, carry):
        both(2 * turn + 1, 1)
        both(jnp.minimum(2 * turn + 2, sources - 1), 0)
        return carry

    lax.fori_loop(0, sources // 2, step, 0)
    for piece in range(count):
        rows = pl.ds(piece * part, part)
        total_ref[rows, 0:wide] = pltpu.matmul_pop(sums[0][piece])
        total_ref[rows, wide:side] = pltpu.matmul_pop(sums[1][piece])[:, : side - wide]
    share = side // out_ref.shape[0]
    full, half = side // width, share // 2
    rest = side - full * width
    for piece in range(out_ref.shape[0]):
        for lane in range(full):
            out_ref[piece, pl.ds(lane * share, share)] = total_ref[
                pl.ds(piece * share, share), lane * width : (lane + 1) * width
            ]
        for step in range(2):
            out_ref[piece, pl.ds(full * share, half), step * rest : (step + 1) * rest] = total_ref[
                pl.ds(piece * share + step * half, half), full * width : side
            ]


def finish_kernel(cameras, lines_ref, *refs):
    pieces, out_ref = refs[:-1], refs[-1]
    share, side = out_ref.shape
    width = pieces[0].shape[2]
    total = pieces[0][0]
    for piece in pieces[1:]:
        total = total + piece[0]
    start = (lax.axis_index("layer") * lax.axis_size("pair") + lax.axis_index("pair")) * share
    first = start // cameras
    row = start + lax.broadcasted_iota(jnp.int32, (share, side), 0)
    column = lax.broadcasted_iota(jnp.int32, (share, side), 1)
    own = jnp.zeros((share, side), jnp.float32)
    for step in range(-(-share // cameras) + 1):
        line = lines_ref[pl.ds(jnp.minimum(first + step, lines_ref.shape[0] - 1), 1), :]
        own = jnp.where(row // cameras == first + step, jnp.broadcast_to(line, (share, side)), own)
    own = jnp.where(row % cameras == column % cameras, own, 0.0)
    full, half = side // width, share // 2
    rest = side - full * width
    for lane in range(full):
        columns = slice(lane * width, (lane + 1) * width)
        out_ref[:, columns] = own[:, columns] - total[lane * share : (lane + 1) * share]
    for step in range(2):
        rows, columns = slice(step * half, (step + 1) * half), slice(full * width, side)
        out_ref[rows, columns] = (
            own[rows, columns] - total[full * share : full * share + half, step * rest : (step + 1) * rest]
        )


def finish(lines, pieces, cameras, share):
    vmem = pl.BlockSpec(memory_space=pltpu.VMEM)
    return pl.pallas_call(
        functools.partial(finish_kernel, cameras),
        out_shape=jax.ShapeDtypeStruct((share, lines.shape[1]), jnp.float32),
        in_specs=[vmem] * (1 + len(pieces)),
        out_specs=vmem,
        compiler_params=pltpu.CompilerParams(vmem_limit_bytes=16 * 1024 * 1024),
        cost_estimate=pl.CostEstimate(flops=200000, bytes_accessed=500000, transcendentals=0),
        name="finish",
    )(lines, *pieces)


def schur_partial(got, cameras, shares):
    width = got.shape[4]
    side = 9 * cameras
    pieces = 9
    vmem = pl.BlockSpec(memory_space=pltpu.VMEM)
    share = side // shares
    lines = side // width * share + share // 2
    return pl.pallas_call(
        functools.partial(schur_kernel, cameras, pieces),
        out_shape=jax.ShapeDtypeStruct((shares, lines + -lines % 8, width), jnp.float32),
        in_specs=[vmem],
        out_specs=vmem,
        scratch_shapes=[
            pltpu.VMEM((side, side), jnp.float32),
            pltpu.VMEM((2, 28, 2, 8, width), jnp.float32),
            pltpu.VMEM((side, 6 * width), jnp.bfloat16),
            pltpu.VMEM((side, 6 * width), jnp.bfloat16),
            pltpu.VMEM((4 * width, 6 * width), jnp.bfloat16),
            pltpu.VMEM((4 * width, 6 * width), jnp.bfloat16),
        ],
        compiler_params=pltpu.CompilerParams(vmem_limit_bytes=32 * 1024 * 1024),
        cost_estimate=pl.CostEstimate(flops=10000000000, bytes_accessed=3000000, transcendentals=0),
        name="schur_partial",
    )(got)


AXES = ("layer", "zp", "zb", "x", "pair")


def local(sizes, jac_blocks, point_blocks, visibility, obs_count, tile_count, route, camera_blocks):
    cameras = camera_blocks.shape[3]
    side = 9 * cameras
    layers, pairs, far, near, across = (lax.axis_size(a) for a in ("layer", "pair", "zp", "zb", "x"))
    shares = layers * pairs

    def site_of(group):
        side_z = group // across % near
        y = (group // (across * near) + pairs - lax.axis_index("zp") + 2 * side_z) % pairs
        return side_z * (across * pairs) + group % across * pairs + y

    packed = pack(
        jac_blocks.transpose(0, 2, 1, 3), point_blocks.transpose(1, 0, 2), visibility, obs_count, tile_count,
        route[:, 0], near * across * pairs, site_of,
    )
    lines = camera_blocks[0].reshape(9, side)
    got = lax.all_to_all(packed, ("zb", "x", "pair"), split_axis=0, concat_axis=0, tiled=True)
    got, lines = lax.optimization_barrier((got, lines))
    partial_value = schur_partial(got, cameras, shares)
    partial_value = partial_value.reshape((layers, pairs) + partial_value.shape[1:])
    layer, row = lax.axis_index("layer"), lax.axis_index("pair")
    theirs = lax.dynamic_index_in_dim(partial_value, 1 - layer, 0, keepdims=False)
    ours = lax.dynamic_index_in_dim(partial_value, layer, 0, keepdims=False)
    ours = ours + lax.ppermute(theirs, "layer", [(0, 1), (1, 0)])
    pieces = []
    for turn in range(far):
        links = []
        for source in itertools.product(*(range(size) for size in sizes)):
            c, zp, zb, x, y = source
            links.append((flat(source, sizes), flat((c, (y + zp + 2 * zb) % far, zb, x, y ^ turn), sizes)))
        piece = lax.dynamic_slice_in_dim(ours, row ^ turn, 1, 0)
        pieces.append(lax.ppermute(piece, AXES, links))
    return finish(lines, pieces, cameras, side // shares)[None]


def flat(place, sizes):
    index = 0
    for coordinate, size in zip(place, sizes):
        index = index * size + coordinate
    return index


def solution(mesh):
    layers, cams, pairs = mesh.devices.shape
    across = 4
    near = 2
    sizes = (layers, cams // (near * across), near, across, pairs)
    split = jax.sharding.Mesh(mesh.devices.reshape(sizes), AXES)
    cam = ("zp", "zb", "x")
    placed = (
        P(AXES, None, None, None),
        P(AXES, None, None),
        P(AXES, None, None),
        P(AXES, None),
        P(AXES),
        P(AXES, None),
        P(cam, None, None, None),
    )
    return jax.shard_map(
        functools.partial(local, sizes),
        mesh=split,
        in_specs=placed,
        out_specs=P(cam, ("layer", "pair"), None),
        check_vma=False,
    )
```

```python
import functools
import itertools

import jax
import jax.numpy as jnp
from jax import lax
from jax.experimental import pallas as pl
from jax.experimental.pallas import tpu as pltpu
from jax.sharding import PartitionSpec as P

GROUPS_OF_ROWS = 30


def pack_kernel(
    site_of, route_hbm, count_hbm, jac_hbm, block_hbm, vis_hbm, obs_hbm, out_ref,
    route_ref, count_ref, block_ref, vis_ref, obs_ref, block_scratch, fill_ref, small_sems, tile_sems,
):
    tiles = jac_hbm.shape[0]
    width = jac_hbm.shape[3]
    places = out_ref.shape[0]
    small = [
        pltpu.make_async_copy(source, target, small_sems.at[index])
        for index, (source, target) in enumerate((
            (route_hbm, route_ref), (count_hbm, count_ref), (block_hbm, block_ref),
            (vis_hbm, vis_ref), (obs_hbm, obs_ref),
        ))
    ]
    for copy in small:
        copy.start()
    dead = jnp.full((4, width), -1.0, jnp.bfloat16)

    def clear(place, carry):
        fill_ref[place] = 0
        out_ref[place, 0, 27] = dead
        out_ref[place, 1, 27] = dead
        return carry

    lax.fori_loop(0, places, clear, 0, unroll=8)
    small[0].wait()

    def send(tile, carry):
        place = site_of(route_ref[tile])
        slot = fill_ref[place]
        fill_ref[place] = slot + 1
        route_ref[tile] = 2 * place + slot
        pltpu.make_async_copy(
            jac_hbm.at[tile], out_ref.at[place, slot, pl.ds(0, 27)], tile_sems.at[tile]
        ).start()
        return carry

    lax.fori_loop(0, tiles, send, 0, unroll=4)
    for copy in small[1:]:
        copy.wait()
    block_scratch[...] = block_ref[...].astype(jnp.float32)
    slot_iota = lax.broadcasted_iota(jnp.int32, (4, width), 0)
    point_iota = lax.broadcasted_iota(jnp.int32, (4, width), 1)

    def fill(tile, carry):
        place = route_ref[tile] // 2
        slot = route_ref[tile] % 2
        obs = jnp.broadcast_to(obs_ref[pl.ds(tile, 1), :], (4, width))
        live = (slot_iota < obs) & (point_iota < count_ref[tile])
        marks = jnp.where(live, vis_ref[tile], -1).astype(jnp.float32).astype(jnp.bfloat16)
        rows = [block_scratch[c, pl.ds(tile, 1), :] for c in range(6)]
        zero = jnp.zeros_like(rows[0])
        out_ref[place, slot, 27] = marks
        out_ref[place, slot, 28] = jnp.concatenate(rows[:4], axis=0).astype(jnp.bfloat16)
        out_ref[place, slot, 29] = jnp.concatenate(rows[4:] + [zero, zero], axis=0).astype(jnp.bfloat16)
        return carry

    lax.fori_loop(0, tiles, fill, 0, unroll=4)

    def finish(tile, carry):
        pltpu.make_async_copy(jac_hbm.at[0], out_ref.at[0, 0, pl.ds(0, 27)], tile_sems.at[tile]).wait()
        return carry

    lax.fori_loop(0, tiles, finish, 0)


def pack(jac, blocks, vis, obs, counts, route, places, site_of):
    tiles, width = jac.shape[0], jac.shape[3]
    anywhere = pl.BlockSpec(memory_space=pltpu.HBM)
    return pl.pallas_call(
        functools.partial(pack_kernel, site_of),
        out_shape=jax.ShapeDtypeStruct((places, 2, GROUPS_OF_ROWS, 4, width), jnp.bfloat16),
        in_specs=[anywhere] * 6,
        out_specs=pl.BlockSpec(memory_space=pltpu.VMEM),
        scratch_shapes=[
            pltpu.SMEM(route.shape, jnp.int32),
            pltpu.SMEM(counts.shape, jnp.int32),
            pltpu.VMEM(blocks.shape, jnp.bfloat16),
            pltpu.VMEM(vis.shape, jnp.int32),
            pltpu.VMEM(obs.shape, jnp.int32),
            pltpu.VMEM(blocks.shape, jnp.float32),
            pltpu.SMEM((places,), jnp.int32),
            pltpu.SemaphoreType.DMA((5,)),
            pltpu.SemaphoreType.DMA((tiles,)),
        ],
        compiler_params=pltpu.CompilerParams(vmem_limit_bytes=60 * 1024 * 1024),
        cost_estimate=pl.CostEstimate(flops=1000000, bytes_accessed=3000000, transcendentals=0),
        name="pack",
    )(route, counts, jac, blocks, vis, obs)


def inverse_rows(first, second):
    xx, yy, zz, xy = (first[c : c + 1] for c in range(4))
    xz, yz = (second[c : c + 1] for c in range(2))
    cxx = yy * zz - yz * yz
    cyy = xx * zz - xz * xz
    czz = xx * yy - xy * xy
    cxy = xz * yz - xy * zz
    cxz = xy * yz - xz * yy
    cyz = xy * xz - xx * yz
    inv_det = 1.0 / (xx * cxx + xy * cxy + xz * cxz)
    ixx, iyy, izz, ixy, ixz, iyz = (c * inv_det for c in (cxx, cyy, czz, cxy, cxz, cyz))
    return ((ixx, ixy, ixz), (ixy, iyy, iyz), (ixz, iyz, izz))


def expand_slot(got_ref, source, slot, rows_ref, left_ref, right_ref, column, cameras):
    width = got_ref.shape[4]
    first = got_ref[source, slot, 28].astype(jnp.float32)
    second = got_ref[source, slot, 29].astype(jnp.float32)
    inverse = inverse_rows(first, second)
    wide = [[jnp.broadcast_to(entry, (4, width)) for entry in line] for line in inverse]
    rows_ref[27, 0, 0:4] = got_ref[source, slot, 27].astype(jnp.float32)
    iota = lax.broadcasted_iota(jnp.int32, (8, width), 0).astype(jnp.float32)
    marks = [jnp.broadcast_to(rows_ref[27, 0, i : i + 1], (8, width)) for i in range(4)]
    picks = []
    for b in range(cameras // 8):
        pick = jnp.full((8, width), 4, jnp.int32)
        for i in range(4):
            pick = jnp.where(marks[i] == iota + 8.0 * b, i, pick)
        picks.append(pick)
    yield
    for r in range(9):
        factors = [got_ref[source, slot, 3 * r + m].astype(jnp.float32) for m in range(3)]
        values = [
            factors[0] * wide[0][k] + factors[1] * wide[1][k] + factors[2] * wide[2][k] for k in range(3)
        ]
        for k in range(3):
            for value, out in ((values[k], left_ref), (factors[k], right_ref)):
                table = jnp.concatenate([value, jnp.zeros_like(value)], axis=0)
                for b in range(0, cameras // 8, 2):
                    pair = [
                        jnp.take_along_axis(table, picks[b + half], axis=0, mode="promise_in_bounds")
                        for half in range(2)
                    ]
                    out[pl.ds(r * cameras + 8 * b, 16), pl.ds(column + 2 * k * width, width)] = jnp.concatenate(
                        pair, axis=0
                    ).astype(jnp.bfloat16)
        yield


def schur_kernel(cameras, pieces, got_ref, out_ref, *scratch):
    part, wide = 9 * cameras // pieces, 2 * got_ref.shape[4]
    sums = [pltpu.ACC(unit)((part, wide), jnp.float32) for unit in range(2) for _ in range(pieces)]
    pl.run_scoped(functools.partial(schur_body, cameras, got_ref, out_ref, *scratch), *sums)


def schur_body(cameras, got_ref, out_ref, total_ref, rows_ref, left_a, left_b, right_a, right_b, *sums):
    sources = got_ref.shape[0]
    width = got_ref.shape[4]
    side = 9 * cameras
    lefts, rights = (left_a, left_b), (right_a, right_b)
    count = len(sums) // 2
    sums = (sums[:count], sums[count:])
    part = side // count
    wide = 2 * width
    rows_ref[...] = jnp.zeros_like(rows_ref)
    for right in rights:
        right[pl.ds(side, 2 * wide - side), :] = jnp.zeros((2 * wide - side, 3 * wide), jnp.bfloat16)

    def expand(source, buffer):
        for slot in range(2):
            yield from expand_slot(
                got_ref, source, slot, rows_ref.at[slot], lefts[buffer], rights[buffer], slot * width, cameras,
            )

    def multiply(buffer):
        for k in range(3):
            columns = pl.ds(k * wide, wide)
            for unit in range(2):
                pltpu.matmul_push_rhs(
                    rights[buffer][pl.ds(unit * wide, wide), columns], k % 2, unit, transpose=True
                )
            for piece in range(count):
                value = lefts[buffer][pl.ds(piece * part, part), columns]
                for unit in range(2):
                    pltpu.matmul_acc_lhs(sums[unit][piece], value, k % 2 if piece == 0 else None)
                yield

    def both(source, buffer):
        one = expand(source, buffer)
        two = multiply(1 - buffer)
        each = -(-20 // (3 * count))
        steps, alive = 0, True
        while alive:
            alive = next(two, 1) is None
            steps += 20
            while steps >= 3 * count:
                steps -= 3 * count
                next(one, 1)
        for _ in one:
            pass

    for _ in expand(0, 0):
        pass

    def step(turn, carry):
        both(2 * turn + 1, 1)
        both(jnp.minimum(2 * turn + 2, sources - 1), 0)
        return carry

    lax.fori_loop(0, sources // 2, step, 0)
    for piece in range(count):
        rows = pl.ds(piece * part, part)
        total_ref[rows, 0:wide] = pltpu.matmul_pop(sums[0][piece])
        total_ref[rows, wide:side] = pltpu.matmul_pop(sums[1][piece])[:, : side - wide]
    share = side // out_ref.shape[0]
    full, half = side // width, share // 2
    rest = side - full * width
    for piece in range(out_ref.shape[0]):
        out_ref[piece, pl.ds(full * share, out_ref.shape[1] - full * share)] = jnp.zeros(
            (out_ref.shape[1] - full * share, width), jnp.float32
        )
        for lane in range(full):
            out_ref[piece, pl.ds(lane * share, share)] = total_ref[
                pl.ds(piece * share, share), lane * width : (lane + 1) * width
            ]
        for step in range(2):
            out_ref[piece, pl.ds(full * share, half), step * rest : (step + 1) * rest] = total_ref[
                pl.ds(piece * share + step * half, half), full * width : side
            ]


def send_kernel(used, ours_ref, came_ref, *out_refs):
    layer, row = lax.axis_index("layer"), lax.axis_index("pair")
    lines, width = came_ref.shape[1:]
    line = lax.broadcasted_iota(jnp.int32, (lines, width), 0)
    for turn, out_ref in enumerate(out_refs):
        value = ours_ref[layer, row ^ turn] + came_ref[row ^ turn]
        largest = jnp.maximum(jnp.max(jnp.abs(value), axis=0, keepdims=True), 2e-34)
        power = jnp.floor(jnp.log2(largest)) - 14.0
        steps = jnp.clip(jnp.round(value * jnp.exp2(-power)), -32767.0, 32767.0)
        steps = jnp.where(line == used, jnp.broadcast_to(power, steps.shape), steps)
        out_ref[...] = steps.astype(jnp.int32).astype(jnp.int16)


def to_send(ours, came, used):
    vmem = pl.BlockSpec(memory_space=pltpu.VMEM)
    shape = jax.ShapeDtypeStruct(came.shape[1:], jnp.int16)
    return pl.pallas_call(
        functools.partial(send_kernel, used),
        out_shape=[shape] * came.shape[0],
        in_specs=[vmem, vmem],
        out_specs=[vmem] * came.shape[0],
        compiler_params=pltpu.CompilerParams(vmem_limit_bytes=16 * 1024 * 1024),
        cost_estimate=pl.CostEstimate(flops=1000000, bytes_accessed=2000000, transcendentals=0),
        name="to_send",
    )(ours, came)


def finish_kernel(cameras, lines_ref, *refs):
    pieces, out_ref = refs[:-1], refs[-1]
    share, side = out_ref.shape
    width = pieces[0].shape[1]
    used = side // width * share + share // 2
    total = None
    for piece in pieces:
        steps = piece[...].astype(jnp.int32).astype(jnp.float32)
        value = steps * jnp.broadcast_to(jnp.exp2(steps[used : used + 1]), steps.shape)
        total = value if total is None else total + value
    start = (lax.axis_index("layer") * lax.axis_size("pair") + lax.axis_index("pair")) * share
    first = start // cameras
    row = start + lax.broadcasted_iota(jnp.int32, (share, side), 0)
    column = lax.broadcasted_iota(jnp.int32, (share, side), 1)
    own = jnp.zeros((share, side), jnp.float32)
    for step in range(-(-share // cameras) + 1):
        line = lines_ref[pl.ds(jnp.minimum(first + step, lines_ref.shape[0] - 1), 1), :]
        own = jnp.where(row // cameras == first + step, jnp.broadcast_to(line, (share, side)), own)
    own = jnp.where(row % cameras == column % cameras, own, 0.0)
    full, half = side // width, share // 2
    rest = side - full * width
    for lane in range(full):
        columns = slice(lane * width, (lane + 1) * width)
        out_ref[:, columns] = own[:, columns] - total[lane * share : (lane + 1) * share]
    for step in range(2):
        rows, columns = slice(step * half, (step + 1) * half), slice(full * width, side)
        out_ref[rows, columns] = (
            own[rows, columns] - total[full * share : full * share + half, step * rest : (step + 1) * rest]
        )


def finish(lines, pieces, cameras, share):
    vmem = pl.BlockSpec(memory_space=pltpu.VMEM)
    return pl.pallas_call(
        functools.partial(finish_kernel, cameras),
        out_shape=jax.ShapeDtypeStruct((share, lines.shape[1]), jnp.float32),
        in_specs=[vmem] * (1 + len(pieces)),
        out_specs=vmem,
        compiler_params=pltpu.CompilerParams(vmem_limit_bytes=16 * 1024 * 1024),
        cost_estimate=pl.CostEstimate(flops=200000, bytes_accessed=500000, transcendentals=0),
        name="finish",
    )(lines, *pieces)


def schur_partial(got, cameras, shares):
    width = got.shape[4]
    side = 9 * cameras
    pieces = 9
    vmem = pl.BlockSpec(memory_space=pltpu.VMEM)
    share = side // shares
    lines = side // width * share + share // 2
    return pl.pallas_call(
        functools.partial(schur_kernel, cameras, pieces),
        out_shape=jax.ShapeDtypeStruct((shares, lines + -lines % 8, width), jnp.float32),
        in_specs=[vmem],
        out_specs=vmem,
        scratch_shapes=[
            pltpu.VMEM((side, side), jnp.float32),
            pltpu.VMEM((2, 28, 2, 8, width), jnp.float32),
            pltpu.VMEM((side, 6 * width), jnp.bfloat16),
            pltpu.VMEM((side, 6 * width), jnp.bfloat16),
            pltpu.VMEM((4 * width, 6 * width), jnp.bfloat16),
            pltpu.VMEM((4 * width, 6 * width), jnp.bfloat16),
        ],
        compiler_params=pltpu.CompilerParams(vmem_limit_bytes=32 * 1024 * 1024),
        cost_estimate=pl.CostEstimate(flops=10000000000, bytes_accessed=3000000, transcendentals=0),
        name="schur_partial",
    )(got)


AXES = ("layer", "zp", "zb", "x", "pair")


def local(sizes, jac_blocks, point_blocks, visibility, obs_count, tile_count, route, camera_blocks):
    cameras = camera_blocks.shape[3]
    side = 9 * cameras
    layers, pairs, far, near, across = (lax.axis_size(a) for a in ("layer", "pair", "zp", "zb", "x"))
    shares = layers * pairs

    def site_of(group):
        side_z = group // across % near
        y = (group // (across * near) + pairs - lax.axis_index("zp") + 2 * side_z) % pairs
        return side_z * (across * pairs) + group % across * pairs + y

    packed = pack(
        jac_blocks.transpose(0, 2, 1, 3), point_blocks.transpose(1, 0, 2), visibility, obs_count, tile_count,
        route[:, 0], near * across * pairs, site_of,
    )
    lines = camera_blocks[0].reshape(9, side)
    got = lax.all_to_all(packed, ("zb", "x", "pair"), split_axis=0, concat_axis=0, tiled=True)
    got, lines = lax.optimization_barrier((got, lines))
    partial_value = schur_partial(got, cameras, shares)
    partial_value = partial_value.reshape((layers, pairs) + partial_value.shape[1:])
    layer = lax.axis_index("layer")
    theirs = lax.dynamic_index_in_dim(partial_value, 1 - layer, 0, keepdims=False)
    came = lax.ppermute(theirs, "layer", [(0, 1), (1, 0)])
    share = side // shares
    width = partial_value.shape[3]
    parcels = to_send(partial_value, came, side // width * share + share // 2)
    pieces = []
    for turn in range(far):
        links = []
        for source in itertools.product(*(range(size) for size in sizes)):
            c, zp, zb, x, y = source
            links.append((flat(source, sizes), flat((c, (y + zp + 2 * zb) % far, zb, x, y ^ turn), sizes)))
        pieces.append(lax.ppermute(parcels[turn], AXES, links))
    return finish(lines, pieces, cameras, share)[None]


def flat(place, sizes):
    index = 0
    for coordinate, size in zip(place, sizes):
        index = index * size + coordinate
    return index


def solution(mesh):
    layers, cams, pairs = mesh.devices.shape
    across = 4
    near = 2
    sizes = (layers, cams // (near * across), near, across, pairs)
    split = jax.sharding.Mesh(mesh.devices.reshape(sizes), AXES)
    cam = ("zp", "zb", "x")
    placed = (
        P(AXES, None, None, None),
        P(AXES, None, None),
        P(AXES, None, None),
        P(AXES, None),
        P(AXES),
        P(AXES, None),
        P(cam, None, None, None),
    )
    return jax.shard_map(
        functools.partial(local, sizes),
        mesh=split,
        in_specs=placed,
        out_specs=P(cam, ("layer", "pair"), None),
        check_vma=False,
    )
```

```python
import functools
import itertools

import jax
import jax.numpy as jnp
from jax import lax
from jax.experimental import pallas as pl
from jax.experimental.pallas import tpu as pltpu
from jax.sharding import PartitionSpec as P

GROUPS_OF_ROWS = 30


def pack_kernel(
    site_of, route_hbm, count_hbm, jac_hbm, block_hbm, vis_hbm, obs_hbm, out_ref,
    route_ref, count_ref, block_ref, vis_ref, obs_ref, block_scratch, fill_ref, small_sems, tile_sems,
):
    tiles = jac_hbm.shape[0]
    width = jac_hbm.shape[3]
    places = out_ref.shape[0]
    small = [
        pltpu.make_async_copy(source, target, small_sems.at[index])
        for index, (source, target) in enumerate((
            (route_hbm, route_ref), (count_hbm, count_ref), (block_hbm, block_ref),
            (vis_hbm, vis_ref), (obs_hbm, obs_ref),
        ))
    ]
    for copy in small:
        copy.start()
    dead = jnp.full((4, width), -1.0, jnp.bfloat16)

    def clear(place, carry):
        fill_ref[place] = 0
        out_ref[place, 0, 27] = dead
        out_ref[place, 1, 27] = dead
        return carry

    lax.fori_loop(0, places, clear, 0, unroll=8)
    small[0].wait()

    def send(tile, carry):
        place = site_of(route_ref[tile])
        slot = fill_ref[place]
        fill_ref[place] = slot + 1
        route_ref[tile] = 2 * place + slot
        pltpu.make_async_copy(
            jac_hbm.at[tile], out_ref.at[place, slot, pl.ds(0, 27)], tile_sems.at[tile]
        ).start()
        return carry

    lax.fori_loop(0, tiles, send, 0, unroll=4)
    for copy in small[1:]:
        copy.wait()
    block_scratch[...] = block_ref[...].astype(jnp.float32)
    slot_iota = lax.broadcasted_iota(jnp.int32, (4, width), 0)
    point_iota = lax.broadcasted_iota(jnp.int32, (4, width), 1)

    def fill(tile, carry):
        place = route_ref[tile] // 2
        slot = route_ref[tile] % 2
        obs = jnp.broadcast_to(obs_ref[pl.ds(tile, 1), :], (4, width))
        live = (slot_iota < obs) & (point_iota < count_ref[tile])
        marks = jnp.where(live, vis_ref[tile], -1).astype(jnp.float32).astype(jnp.bfloat16)
        rows = [block_scratch[c, pl.ds(tile, 1), :] for c in range(6)]
        zero = jnp.zeros_like(rows[0])
        out_ref[place, slot, 27] = marks
        out_ref[place, slot, 28] = jnp.concatenate(rows[:4], axis=0).astype(jnp.bfloat16)
        out_ref[place, slot, 29] = jnp.concatenate(rows[4:] + [zero, zero], axis=0).astype(jnp.bfloat16)
        return carry

    lax.fori_loop(0, tiles, fill, 0, unroll=4)

    def finish(tile, carry):
        pltpu.make_async_copy(jac_hbm.at[0], out_ref.at[0, 0, pl.ds(0, 27)], tile_sems.at[tile]).wait()
        return carry

    lax.fori_loop(0, tiles, finish, 0)


def pack(jac, blocks, vis, obs, counts, route, places, site_of):
    tiles, width = jac.shape[0], jac.shape[3]
    anywhere = pl.BlockSpec(memory_space=pltpu.HBM)
    return pl.pallas_call(
        functools.partial(pack_kernel, site_of),
        out_shape=jax.ShapeDtypeStruct((places, 2, GROUPS_OF_ROWS, 4, width), jnp.bfloat16),
        in_specs=[anywhere] * 6,
        out_specs=pl.BlockSpec(memory_space=pltpu.VMEM),
        scratch_shapes=[
            pltpu.SMEM(route.shape, jnp.int32),
            pltpu.SMEM(counts.shape, jnp.int32),
            pltpu.VMEM(blocks.shape, jnp.bfloat16),
            pltpu.VMEM(vis.shape, jnp.int32),
            pltpu.VMEM(obs.shape, jnp.int32),
            pltpu.VMEM(blocks.shape, jnp.float32),
            pltpu.SMEM((places,), jnp.int32),
            pltpu.SemaphoreType.DMA((5,)),
            pltpu.SemaphoreType.DMA((tiles,)),
        ],
        compiler_params=pltpu.CompilerParams(vmem_limit_bytes=60 * 1024 * 1024),
        cost_estimate=pl.CostEstimate(flops=1000000, bytes_accessed=3000000, transcendentals=0),
        name="pack",
    )(route, counts, jac, blocks, vis, obs)


def inverse_rows(first, second):
    xx, yy, zz, xy = (first[c : c + 1] for c in range(4))
    xz, yz = (second[c : c + 1] for c in range(2))
    cxx = yy * zz - yz * yz
    cyy = xx * zz - xz * xz
    czz = xx * yy - xy * xy
    cxy = xz * yz - xy * zz
    cxz = xy * yz - xz * yy
    cyz = xy * xz - xx * yz
    inv_det = 1.0 / (xx * cxx + xy * cxy + xz * cxz)
    ixx, iyy, izz, ixy, ixz, iyz = (c * inv_det for c in (cxx, cyy, czz, cxy, cxz, cyz))
    return ((ixx, ixy, ixz), (ixy, iyy, iyz), (ixz, iyz, izz))


def expand_slot(got_ref, source, slot, rows_ref, left_ref, right_ref, column, cameras):
    width = got_ref.shape[4]
    first = got_ref[source, slot, 28].astype(jnp.float32)
    second = got_ref[source, slot, 29].astype(jnp.float32)
    inverse = inverse_rows(first, second)
    wide = [[jnp.broadcast_to(entry, (4, width)) for entry in line] for line in inverse]
    rows_ref[27, 0, 0:4] = got_ref[source, slot, 27].astype(jnp.float32)
    iota = lax.broadcasted_iota(jnp.int32, (8, width), 0).astype(jnp.float32)
    marks = [jnp.broadcast_to(rows_ref[27, 0, i : i + 1], (8, width)) for i in range(4)]
    picks = []
    for b in range(cameras // 8):
        pick = jnp.full((8, width), 4, jnp.int32)
        for i in range(4):
            pick = jnp.where(marks[i] == iota + 8.0 * b, i, pick)
        picks.append(pick)
    yield
    for r in range(9):
        factors = [got_ref[source, slot, 3 * r + m].astype(jnp.float32) for m in range(3)]
        values = [
            factors[0] * wide[0][k] + factors[1] * wide[1][k] + factors[2] * wide[2][k] for k in range(3)
        ]
        for k in range(3):
            for value, out in ((values[k], left_ref), (factors[k], right_ref)):
                table = jnp.concatenate([value, jnp.zeros_like(value)], axis=0)
                for b in range(0, cameras // 8, 2):
                    pair = [
                        jnp.take_along_axis(table, picks[b + half], axis=0, mode="promise_in_bounds")
                        for half in range(2)
                    ]
                    out[pl.ds(r * cameras + 8 * b, 16), pl.ds(column + 2 * k * width, width)] = jnp.concatenate(
                        pair, axis=0
                    ).astype(jnp.bfloat16)
        yield


def schur_kernel(cameras, pieces, got_ref, out_ref, *scratch):
    part, wide = 9 * cameras // pieces, 2 * got_ref.shape[4]
    sums = [pltpu.ACC(unit)((part, wide), jnp.float32) for unit in range(2) for _ in range(pieces)]
    pl.run_scoped(functools.partial(schur_body, cameras, got_ref, out_ref, *scratch), *sums)


def schur_body(cameras, got_ref, out_ref, total_ref, rows_ref, left_a, left_b, right_a, right_b, *sums):
    sources = got_ref.shape[0]
    width = got_ref.shape[4]
    side = 9 * cameras
    lefts, rights = (left_a, left_b), (right_a, right_b)
    count = len(sums) // 2
    sums = (sums[:count], sums[count:])
    part = side // count
    wide = 2 * width
    rows_ref[...] = jnp.zeros_like(rows_ref)
    for right in rights:
        right[pl.ds(side, 2 * wide - side), :] = jnp.zeros((2 * wide - side, 3 * wide), jnp.bfloat16)

    def expand(source, buffer):
        for slot in range(2):
            yield from expand_slot(
                got_ref, source, slot, rows_ref.at[slot], lefts[buffer], rights[buffer], slot * width, cameras,
            )

    def multiply(buffer):
        for k in range(3):
            columns = pl.ds(k * wide, wide)
            for unit in range(2):
                pltpu.matmul_push_rhs(
                    rights[buffer][pl.ds(unit * wide, wide), columns], k % 2, unit, transpose=True
                )
            for piece in range(count):
                value = lefts[buffer][pl.ds(piece * part, part), columns]
                for unit in range(2):
                    pltpu.matmul_acc_lhs(sums[unit][piece], value, k % 2 if piece == 0 else None)
                yield

    def both(source, buffer):
        one = expand(source, buffer)
        two = multiply(1 - buffer)
        each = -(-20 // (3 * count))
        steps, alive = 0, True
        while alive:
            alive = next(two, 1) is None
            steps += 20
            while steps >= 3 * count:
                steps -= 3 * count
                next(one, 1)
        for _ in one:
            pass

    for _ in expand(0, 0):
        pass

    def step(turn, carry):
        both(2 * turn + 1, 1)
        both(jnp.minimum(2 * turn + 2, sources - 1), 0)
        return carry

    lax.fori_loop(0, sources // 2, step, 0)
    for piece in range(count):
        rows = pl.ds(piece * part, part)
        total_ref[rows, 0:wide] = pltpu.matmul_pop(sums[0][piece])
        total_ref[rows, wide:side] = pltpu.matmul_pop(sums[1][piece])[:, : side - wide]
    share = side // out_ref.shape[0]
    full, half = side // width, share // 2
    rest = side - full * width
    for piece in range(out_ref.shape[0]):
        out_ref[piece, pl.ds(full * share, out_ref.shape[1] - full * share)] = jnp.zeros(
            (out_ref.shape[1] - full * share, width), jnp.float32
        )
        for lane in range(full):
            out_ref[piece, pl.ds(lane * share, share)] = total_ref[
                pl.ds(piece * share, share), lane * width : (lane + 1) * width
            ]
        for step in range(2):
            out_ref[piece, pl.ds(full * share, half), step * rest : (step + 1) * rest] = total_ref[
                pl.ds(piece * share + step * half, half), full * width : side
            ]


def send_kernel(used, ours_ref, came_ref, *out_refs):
    layer, row = lax.axis_index("layer"), lax.axis_index("pair")
    lines, width = came_ref.shape[1:]
    line = lax.broadcasted_iota(jnp.int32, (lines, width), 0)
    for turn, (out_ref, part) in enumerate((ref, part) for ref in out_refs for part in range(2)):
        value = ours_ref[layer, row ^ turn] + came_ref[row ^ turn]
        largest = jnp.maximum(jnp.max(jnp.abs(value), axis=0, keepdims=True), 2e-34)
        power = jnp.floor(jnp.log2(largest)) - 14.0
        steps = jnp.clip(jnp.round(value * jnp.exp2(-power)), -32767.0, 32767.0)
        steps = jnp.where(line == used, jnp.broadcast_to(power, steps.shape), steps)
        out_ref[part] = steps.astype(jnp.int32).astype(jnp.int16)


def to_send(ours, came, used):
    vmem = pl.BlockSpec(memory_space=pltpu.VMEM)
    parcels = came.shape[0] // 2
    shape = jax.ShapeDtypeStruct((2,) + came.shape[1:], jnp.int16)
    return pl.pallas_call(
        functools.partial(send_kernel, used),
        out_shape=[shape] * parcels,
        in_specs=[vmem, vmem],
        out_specs=[vmem] * parcels,
        compiler_params=pltpu.CompilerParams(vmem_limit_bytes=16 * 1024 * 1024),
        cost_estimate=pl.CostEstimate(flops=1000000, bytes_accessed=2000000, transcendentals=0),
        name="to_send",
    )(ours, came)


def value_of(parcel, part, used):
    steps = parcel[part].astype(jnp.int32).astype(jnp.float32)
    return steps * jnp.broadcast_to(jnp.exp2(steps[used : used + 1]), steps.shape)


def beside_kernel(used, first, second, out_ref):
    out_ref[...] = value_of(first, 1, used) + value_of(second, 1, used)


def for_beside(parcels, used):
    vmem = pl.BlockSpec(memory_space=pltpu.VMEM)
    return pl.pallas_call(
        functools.partial(beside_kernel, used),
        out_shape=jax.ShapeDtypeStruct(parcels[0].shape[1:], jnp.float32),
        in_specs=[vmem, vmem],
        out_specs=vmem,
        compiler_params=pltpu.CompilerParams(vmem_limit_bytes=16 * 1024 * 1024),
        cost_estimate=pl.CostEstimate(flops=100000, bytes_accessed=300000, transcendentals=0),
        name="for_beside",
    )(*parcels)


def finish_kernel(cameras, lines_ref, came_ref, first, second, out_ref):
    share, side = out_ref.shape
    width = came_ref.shape[1]
    used = side // width * share + share // 2
    total = value_of(first, 0, used) + value_of(second, 0, used) + came_ref[...]
    start = (lax.axis_index("layer") * lax.axis_size("pair") + lax.axis_index("pair")) * share
    first = start // cameras
    row = start + lax.broadcasted_iota(jnp.int32, (share, side), 0)
    column = lax.broadcasted_iota(jnp.int32, (share, side), 1)
    own = jnp.zeros((share, side), jnp.float32)
    for step in range(-(-share // cameras) + 1):
        line = lines_ref[pl.ds(jnp.minimum(first + step, lines_ref.shape[0] - 1), 1), :]
        own = jnp.where(row // cameras == first + step, jnp.broadcast_to(line, (share, side)), own)
    own = jnp.where(row % cameras == column % cameras, own, 0.0)
    full, half = side // width, share // 2
    rest = side - full * width
    for lane in range(full):
        columns = slice(lane * width, (lane + 1) * width)
        out_ref[:, columns] = own[:, columns] - total[lane * share : (lane + 1) * share]
    for step in range(2):
        rows, columns = slice(step * half, (step + 1) * half), slice(full * width, side)
        out_ref[rows, columns] = (
            own[rows, columns] - total[full * share : full * share + half, step * rest : (step + 1) * rest]
        )


def finish(lines, pieces, cameras, share):
    vmem = pl.BlockSpec(memory_space=pltpu.VMEM)
    return pl.pallas_call(
        functools.partial(finish_kernel, cameras),
        out_shape=jax.ShapeDtypeStruct((share, lines.shape[1]), jnp.float32),
        in_specs=[vmem] * (1 + len(pieces)),
        out_specs=vmem,
        compiler_params=pltpu.CompilerParams(vmem_limit_bytes=16 * 1024 * 1024),
        cost_estimate=pl.CostEstimate(flops=200000, bytes_accessed=500000, transcendentals=0),
        name="finish",
    )(lines, *pieces)


def schur_partial(got, cameras, shares):
    width = got.shape[4]
    side = 9 * cameras
    pieces = 9
    vmem = pl.BlockSpec(memory_space=pltpu.VMEM)
    share = side // shares
    lines = side // width * share + share // 2
    return pl.pallas_call(
        functools.partial(schur_kernel, cameras, pieces),
        out_shape=jax.ShapeDtypeStruct((shares, lines + -lines % 8, width), jnp.float32),
        in_specs=[vmem],
        out_specs=vmem,
        scratch_shapes=[
            pltpu.VMEM((side, side), jnp.float32),
            pltpu.VMEM((2, 28, 2, 8, width), jnp.float32),
            pltpu.VMEM((side, 6 * width), jnp.bfloat16),
            pltpu.VMEM((side, 6 * width), jnp.bfloat16),
            pltpu.VMEM((4 * width, 6 * width), jnp.bfloat16),
            pltpu.VMEM((4 * width, 6 * width), jnp.bfloat16),
        ],
        compiler_params=pltpu.CompilerParams(vmem_limit_bytes=32 * 1024 * 1024),
        cost_estimate=pl.CostEstimate(flops=10000000000, bytes_accessed=3000000, transcendentals=0),
        name="schur_partial",
    )(got)


AXES = ("layer", "zp", "zb", "x", "pair")


def local(sizes, jac_blocks, point_blocks, visibility, obs_count, tile_count, route, camera_blocks):
    cameras = camera_blocks.shape[3]
    side = 9 * cameras
    layers, pairs, far, near, across = (lax.axis_size(a) for a in ("layer", "pair", "zp", "zb", "x"))
    shares = layers * pairs

    def site_of(group):
        side_z = group // across % near
        y = (group // (across * near) + pairs - lax.axis_index("zp") + 2 * side_z) % pairs
        return side_z * (across * pairs) + group % across * pairs + y

    packed = pack(
        jac_blocks.transpose(0, 2, 1, 3), point_blocks.transpose(1, 0, 2), visibility, obs_count, tile_count,
        route[:, 0], near * across * pairs, site_of,
    )
    lines = camera_blocks[0].reshape(9, side)
    got = lax.all_to_all(packed, ("zb", "x", "pair"), split_axis=0, concat_axis=0, tiled=True)
    got, lines = lax.optimization_barrier((got, lines))
    partial_value = schur_partial(got, cameras, shares)
    partial_value = partial_value.reshape((layers, pairs) + partial_value.shape[1:])
    layer = lax.axis_index("layer")
    theirs = lax.dynamic_index_in_dim(partial_value, 1 - layer, 0, keepdims=False)
    came = lax.ppermute(theirs, "layer", [(0, 1), (1, 0)])
    share = side // shares
    width = partial_value.shape[3]
    parcels = to_send(partial_value, came, side // width * share + share // 2)
    pieces = []
    for turn in range(pairs // 2):
        links = []
        for source in itertools.product(*(range(size) for size in sizes)):
            c, zp, zb, x, y = source
            links.append((flat(source, sizes), flat((c, (y + zp + 2 * zb) % far, zb, x, y ^ (2 * turn)), sizes)))
        pieces.append(lax.ppermute(parcels[turn], AXES, links))
    beside = for_beside(pieces, side // width * share + share // 2)
    pieces.insert(0, lax.ppermute(beside, "pair", [(y, y ^ 1) for y in range(pairs)]))
    return finish(lines, pieces, cameras, share)[None]


def flat(place, sizes):
    index = 0
    for coordinate, size in zip(place, sizes):
        index = index * size + coordinate
    return index


def solution(mesh):
    layers, cams, pairs = mesh.devices.shape
    across = 4
    near = 2
    sizes = (layers, cams // (near * across), near, across, pairs)
    split = jax.sharding.Mesh(mesh.devices.reshape(sizes), AXES)
    cam = ("zp", "zb", "x")
    placed = (
        P(AXES, None, None, None),
        P(AXES, None, None),
        P(AXES, None, None),
        P(AXES, None),
        P(AXES),
        P(AXES, None),
        P(cam, None, None, None),
    )
    return jax.shard_map(
        functools.partial(local, sizes),
        mesh=split,
        in_specs=placed,
        out_specs=P(cam, ("layer", "pair"), None),
        check_vma=False,
    )
```

```python
import functools
import itertools

import jax
import jax.numpy as jnp
from jax import lax
from jax.experimental import pallas as pl
from jax.experimental.pallas import tpu as pltpu
from jax.sharding import PartitionSpec as P

GROUPS_OF_ROWS = 30


def pack_kernel(
    site_of, route_hbm, count_hbm, jac_hbm, block_hbm, vis_hbm, obs_hbm, out_ref,
    route_ref, count_ref, block_ref, vis_ref, obs_ref, block_scratch, fill_ref, small_sems, tile_sems,
):
    tiles = jac_hbm.shape[0]
    width = jac_hbm.shape[3]
    places = out_ref.shape[0]
    small = [
        pltpu.make_async_copy(source, target, small_sems.at[index])
        for index, (source, target) in enumerate((
            (route_hbm, route_ref), (count_hbm, count_ref), (block_hbm, block_ref),
            (vis_hbm, vis_ref), (obs_hbm, obs_ref),
        ))
    ]
    for copy in small:
        copy.start()
    dead = jnp.full((4, width), -1.0, jnp.bfloat16)

    def clear(place, carry):
        fill_ref[place] = 0
        out_ref[place, 0, 27] = dead
        out_ref[place, 1, 27] = dead
        return carry

    lax.fori_loop(0, places, clear, 0, unroll=8)
    small[0].wait()

    def send(tile, carry):
        place = site_of(route_ref[tile])
        slot = fill_ref[place]
        fill_ref[place] = slot + 1
        route_ref[tile] = 2 * place + slot
        pltpu.make_async_copy(
            jac_hbm.at[tile], out_ref.at[place, slot, pl.ds(0, 27)], tile_sems.at[tile]
        ).start()
        return carry

    lax.fori_loop(0, tiles, send, 0, unroll=4)
    for copy in small[1:]:
        copy.wait()
    block_scratch[...] = block_ref[...].astype(jnp.float32)
    slot_iota = lax.broadcasted_iota(jnp.int32, (4, width), 0)
    point_iota = lax.broadcasted_iota(jnp.int32, (4, width), 1)

    def fill(tile, carry):
        place = route_ref[tile] // 2
        slot = route_ref[tile] % 2
        obs = jnp.broadcast_to(obs_ref[pl.ds(tile, 1), :], (4, width))
        live = (slot_iota < obs) & (point_iota < count_ref[tile])
        marks = jnp.where(live, vis_ref[tile], -1).astype(jnp.float32).astype(jnp.bfloat16)
        rows = [block_scratch[c, pl.ds(tile, 1), :] for c in range(6)]
        zero = jnp.zeros_like(rows[0])
        out_ref[place, slot, 27] = marks
        out_ref[place, slot, 28] = jnp.concatenate(rows[:4], axis=0).astype(jnp.bfloat16)
        out_ref[place, slot, 29] = jnp.concatenate(rows[4:] + [zero, zero], axis=0).astype(jnp.bfloat16)
        return carry

    lax.fori_loop(0, tiles, fill, 0, unroll=4)

    def finish(tile, carry):
        pltpu.make_async_copy(jac_hbm.at[0], out_ref.at[0, 0, pl.ds(0, 27)], tile_sems.at[tile]).wait()
        return carry

    lax.fori_loop(0, tiles, finish, 0)


def pack(jac, blocks, vis, obs, counts, route, places, site_of):
    tiles, width = jac.shape[0], jac.shape[3]
    anywhere = pl.BlockSpec(memory_space=pltpu.HBM)
    return pl.pallas_call(
        functools.partial(pack_kernel, site_of),
        out_shape=jax.ShapeDtypeStruct((places, 2, GROUPS_OF_ROWS, 4, width), jnp.bfloat16),
        in_specs=[anywhere] * 6,
        out_specs=pl.BlockSpec(memory_space=pltpu.VMEM),
        scratch_shapes=[
            pltpu.SMEM(route.shape, jnp.int32),
            pltpu.SMEM(counts.shape, jnp.int32),
            pltpu.VMEM(blocks.shape, jnp.bfloat16),
            pltpu.VMEM(vis.shape, jnp.int32),
            pltpu.VMEM(obs.shape, jnp.int32),
            pltpu.VMEM(blocks.shape, jnp.float32),
            pltpu.SMEM((places,), jnp.int32),
            pltpu.SemaphoreType.DMA((5,)),
            pltpu.SemaphoreType.DMA((tiles,)),
        ],
        compiler_params=pltpu.CompilerParams(vmem_limit_bytes=60 * 1024 * 1024),
        cost_estimate=pl.CostEstimate(flops=1000000, bytes_accessed=3000000, transcendentals=0),
        name="pack",
    )(route, counts, jac, blocks, vis, obs)


def inverse_rows(first, second):
    xx, yy, zz, xy = (first[c : c + 1] for c in range(4))
    xz, yz = (second[c : c + 1] for c in range(2))
    cxx = yy * zz - yz * yz
    cyy = xx * zz - xz * xz
    czz = xx * yy - xy * xy
    cxy = xz * yz - xy * zz
    cxz = xy * yz - xz * yy
    cyz = xy * xz - xx * yz
    inv_det = 1.0 / (xx * cxx + xy * cxy + xz * cxz)
    ixx, iyy, izz, ixy, ixz, iyz = (c * inv_det for c in (cxx, cyy, czz, cxy, cxz, cyz))
    return ((ixx, ixy, ixz), (ixy, iyy, iyz), (ixz, iyz, izz))


def expand_slot(got_ref, source, slot, rows_ref, left_ref, right_ref, column, cameras):
    width = got_ref.shape[4]
    first = got_ref[source, slot, 28].astype(jnp.float32)
    second = got_ref[source, slot, 29].astype(jnp.float32)
    inverse = inverse_rows(first, second)
    wide = [[jnp.broadcast_to(entry, (4, width)) for entry in line] for line in inverse]
    rows_ref[27, 0, 0:4] = got_ref[source, slot, 27].astype(jnp.float32)
    iota = lax.broadcasted_iota(jnp.int32, (8, width), 0).astype(jnp.float32)
    marks = [jnp.broadcast_to(rows_ref[27, 0, i : i + 1], (8, width)) for i in range(4)]
    picks = []
    for b in range(cameras // 8):
        pick = jnp.full((8, width), 4, jnp.int32)
        for i in range(4):
            pick = jnp.where(marks[i] == iota + 8.0 * b, i, pick)
        picks.append(pick)
    yield
    for r in range(9):
        factors = [got_ref[source, slot, 3 * r + m].astype(jnp.float32) for m in range(3)]
        values = [
            factors[0] * wide[0][k] + factors[1] * wide[1][k] + factors[2] * wide[2][k] for k in range(3)
        ]
        for k in range(3):
            for value, out in ((values[k], left_ref), (factors[k], right_ref)):
                table = jnp.concatenate([value, jnp.zeros_like(value)], axis=0)
                for b in range(0, cameras // 8, 2):
                    pair = [
                        jnp.take_along_axis(table, picks[b + half], axis=0, mode="promise_in_bounds")
                        for half in range(2)
                    ]
                    out[pl.ds(r * cameras + 8 * b, 16), pl.ds(column + 2 * k * width, width)] = jnp.concatenate(
                        pair, axis=0
                    ).astype(jnp.bfloat16)
        yield


def schur_kernel(cameras, pieces, got_ref, out_ref, *scratch):
    part, wide = 9 * cameras // pieces, 2 * got_ref.shape[4]
    sums = [pltpu.ACC(unit)((part, wide), jnp.float32) for unit in range(2) for _ in range(pieces)]
    pl.run_scoped(functools.partial(schur_body, cameras, got_ref, out_ref, *scratch), *sums)


def schur_body(cameras, got_ref, out_ref, total_ref, rows_ref, left_a, left_b, right_a, right_b, *sums):
    sources = got_ref.shape[0]
    width = got_ref.shape[4]
    side = 9 * cameras
    lefts, rights = (left_a, left_b), (right_a, right_b)
    count = len(sums) // 2
    sums = (sums[:count], sums[count:])
    part = side // count
    wide = 2 * width
    rows_ref[...] = jnp.zeros_like(rows_ref)
    for right in rights:
        right[pl.ds(side, 2 * wide - side), :] = jnp.zeros((2 * wide - side, 3 * wide), jnp.bfloat16)

    def expand(source, buffer):
        for slot in range(2):
            yield from expand_slot(
                got_ref, source, slot, rows_ref.at[slot], lefts[buffer], rights[buffer], slot * width, cameras,
            )

    def multiply(buffer):
        for k in range(3):
            columns = pl.ds(k * wide, wide)
            for unit in range(2):
                pltpu.matmul_push_rhs(
                    rights[buffer][pl.ds(unit * wide, wide), columns], k % 2, unit, transpose=True
                )
            for piece in range(count):
                value = lefts[buffer][pl.ds(piece * part, part), columns]
                for unit in range(2):
                    pltpu.matmul_acc_lhs(sums[unit][piece], value, k % 2 if piece == 0 else None)
                yield

    def both(source, buffer):
        one = expand(source, buffer)
        two = multiply(1 - buffer)
        each = -(-20 // (3 * count))
        steps, alive = 0, True
        while alive:
            alive = next(two, 1) is None
            steps += 20
            while steps >= 3 * count:
                steps -= 3 * count
                next(one, 1)
        for _ in one:
            pass

    for _ in expand(0, 0):
        pass

    def step(turn, carry):
        both(2 * turn + 1, 1)
        both(jnp.minimum(2 * turn + 2, sources - 1), 0)
        return carry

    lax.fori_loop(0, sources // 2, step, 0)
    for piece in range(count):
        rows = pl.ds(piece * part, part)
        total_ref[rows, 0:wide] = pltpu.matmul_pop(sums[0][piece])
        total_ref[rows, wide:side] = pltpu.matmul_pop(sums[1][piece])[:, : side - wide]
    share = side // out_ref.shape[0]
    full, half = side // width, share // 2
    rest = side - full * width
    for piece in range(out_ref.shape[0]):
        out_ref[piece, pl.ds(full * share, out_ref.shape[1] - full * share)] = jnp.zeros(
            (out_ref.shape[1] - full * share, width), jnp.float32
        )
        for lane in range(full):
            out_ref[piece, pl.ds(lane * share, share)] = total_ref[
                pl.ds(piece * share, share), lane * width : (lane + 1) * width
            ]
        for step in range(2):
            out_ref[piece, pl.ds(full * share, half), step * rest : (step + 1) * rest] = total_ref[
                pl.ds(piece * share + step * half, half), full * width : side
            ]


def send_kernel(used, ours_ref, came_ref, *out_refs):
    layer, row = lax.axis_index("layer"), lax.axis_index("pair")
    lines, width = came_ref.shape[1:]
    line = lax.broadcasted_iota(jnp.int32, (lines, width), 0)
    for turn, out_ref in enumerate(out_refs):
        value = ours_ref[layer, row ^ turn] + came_ref[row ^ turn]
        largest = jnp.maximum(jnp.max(jnp.abs(value), axis=0, keepdims=True), 2e-34)
        power = jnp.floor(jnp.log2(largest)) - 14.0
        steps = jnp.clip(jnp.round(value * jnp.exp2(-power)), -32767.0, 32767.0)
        steps = jnp.where(line == used, jnp.broadcast_to(power, steps.shape), steps)
        out_ref[...] = steps.astype(jnp.int32).astype(jnp.int16)


def to_send(ours, came, used):
    vmem = pl.BlockSpec(memory_space=pltpu.VMEM)
    shape = jax.ShapeDtypeStruct(came.shape[1:], jnp.int16)
    return pl.pallas_call(
        functools.partial(send_kernel, used),
        out_shape=[shape] * came.shape[0],
        in_specs=[vmem, vmem],
        out_specs=[vmem] * came.shape[0],
        compiler_params=pltpu.CompilerParams(vmem_limit_bytes=16 * 1024 * 1024),
        cost_estimate=pl.CostEstimate(flops=1000000, bytes_accessed=2000000, transcendentals=0),
        name="to_send",
    )(ours, came)


def finish_kernel(cameras, lines_ref, *refs):
    pieces, out_ref = refs[:-1], refs[-1]
    share, _, side = out_ref.shape
    width = pieces[0].shape[1]
    used = side // width * share + share // 2
    total = None
    for piece in pieces:
        steps = piece[...].astype(jnp.int32).astype(jnp.float32)
        value = steps * jnp.broadcast_to(jnp.exp2(steps[used : used + 1]), steps.shape)
        total = value if total is None else total + value
    start = (lax.axis_index("layer") * lax.axis_size("pair") + lax.axis_index("pair")) * share
    first = start // cameras
    row = start + lax.broadcasted_iota(jnp.int32, (share, side), 0)
    column = lax.broadcasted_iota(jnp.int32, (share, side), 1)
    own = jnp.zeros((share, side), jnp.float32)
    for step in range(-(-share // cameras) + 1):
        line = lines_ref[pl.ds(jnp.minimum(first + step, lines_ref.shape[0] - 1), 1), :]
        own = jnp.where(row // cameras == first + step, jnp.broadcast_to(line, (share, side)), own)
    own = jnp.where(row % cameras == column % cameras, own, 0.0)
    full, half = side // width, share // 2
    rest = side - full * width
    for lane in range(full):
        columns = slice(lane * width, (lane + 1) * width)
        out_ref[:, 0, columns] = own[:, columns] - total[lane * share : (lane + 1) * share]
    for step in range(2):
        rows, columns = slice(step * half, (step + 1) * half), slice(full * width, side)
        out_ref[rows, 0, columns] = (
            own[rows, columns] - total[full * share : full * share + half, step * rest : (step + 1) * rest]
        )


def finish(lines, pieces, cameras, share):
    vmem = pl.BlockSpec(memory_space=pltpu.VMEM)
    return pl.pallas_call(
        functools.partial(finish_kernel, cameras),
        out_shape=jax.ShapeDtypeStruct((share, 1, lines.shape[1]), jnp.float32),
        in_specs=[vmem] * (1 + len(pieces)),
        out_specs=vmem,
        compiler_params=pltpu.CompilerParams(vmem_limit_bytes=16 * 1024 * 1024),
        cost_estimate=pl.CostEstimate(flops=200000, bytes_accessed=500000, transcendentals=0),
        name="finish",
    )(lines, *pieces)


def schur_partial(got, cameras, shares):
    width = got.shape[4]
    side = 9 * cameras
    pieces = 9
    vmem = pl.BlockSpec(memory_space=pltpu.VMEM)
    share = side // shares
    lines = side // width * share + share // 2
    return pl.pallas_call(
        functools.partial(schur_kernel, cameras, pieces),
        out_shape=jax.ShapeDtypeStruct((shares, lines + -lines % 8, width), jnp.float32),
        in_specs=[vmem],
        out_specs=vmem,
        scratch_shapes=[
            pltpu.VMEM((side, side), jnp.float32),
            pltpu.VMEM((2, 28, 2, 8, width), jnp.float32),
            pltpu.VMEM((side, 6 * width), jnp.bfloat16),
            pltpu.VMEM((side, 6 * width), jnp.bfloat16),
            pltpu.VMEM((4 * width, 6 * width), jnp.bfloat16),
            pltpu.VMEM((4 * width, 6 * width), jnp.bfloat16),
        ],
        compiler_params=pltpu.CompilerParams(vmem_limit_bytes=32 * 1024 * 1024),
        cost_estimate=pl.CostEstimate(flops=10000000000, bytes_accessed=3000000, transcendentals=0),
        name="schur_partial",
    )(got)


AXES = ("layer", "zp", "zb", "x", "pair")


def local(sizes, jac_blocks, point_blocks, visibility, obs_count, tile_count, route, camera_blocks):
    cameras = camera_blocks.shape[3]
    side = 9 * cameras
    layers, pairs, far, near, across = (lax.axis_size(a) for a in ("layer", "pair", "zp", "zb", "x"))
    shares = layers * pairs

    def site_of(group):
        side_z = group // across % near
        y = (group // (across * near) + pairs - lax.axis_index("zp") + 2 * side_z) % pairs
        return side_z * (across * pairs) + group % across * pairs + y

    packed = pack(
        jac_blocks.transpose(0, 2, 1, 3), point_blocks.transpose(1, 0, 2), visibility, obs_count, tile_count,
        route[:, 0], near * across * pairs, site_of,
    )
    lines = camera_blocks[0].reshape(9, side)
    got = lax.all_to_all(packed, ("zb", "x", "pair"), split_axis=0, concat_axis=0, tiled=True)
    got, lines = lax.optimization_barrier((got, lines))
    partial_value = schur_partial(got, cameras, shares)
    partial_value = partial_value.reshape((layers, pairs) + partial_value.shape[1:])
    layer = lax.axis_index("layer")
    theirs = lax.dynamic_index_in_dim(partial_value, 1 - layer, 0, keepdims=False)
    came = lax.ppermute(theirs, "layer", [(0, 1), (1, 0)])
    share = side // shares
    width = partial_value.shape[3]
    parcels = to_send(partial_value, came, side // width * share + share // 2)
    pieces = []
    for turn in sorted(range(far), key=lambda turn: -min(turn, pairs - turn)):
        links = []
        for source in itertools.product(*(range(size) for size in sizes)):
            c, zp, zb, x, y = source
            links.append((flat(source, sizes), flat((c, (y + zp + 2 * zb) % far, zb, x, y ^ turn), sizes)))
        pieces.append(lax.ppermute(parcels[turn], AXES, links))
    return finish(lines, pieces, cameras, share).transpose(1, 0, 2)


def flat(place, sizes):
    index = 0
    for coordinate, size in zip(place, sizes):
        index = index * size + coordinate
    return index


def solution(mesh):
    layers, cams, pairs = mesh.devices.shape
    across = 4
    near = 2
    sizes = (layers, cams // (near * across), near, across, pairs)
    split = jax.sharding.Mesh(mesh.devices.reshape(sizes), AXES)
    cam = ("zp", "zb", "x")
    placed = (
        P(AXES, None, None, None),
        P(AXES, None, None),
        P(AXES, None, None),
        P(AXES, None),
        P(AXES),
        P(AXES, None),
        P(cam, None, None, None),
    )
    return jax.shard_map(
        functools.partial(local, sizes),
        mesh=split,
        in_specs=placed,
        out_specs=P(cam, ("layer", "pair"), None),
        check_vma=False,
    )
```

```python
import functools
import itertools

import jax
import jax.numpy as jnp
from jax import lax
from jax.experimental import pallas as pl
from jax.experimental.pallas import tpu as pltpu
from jax.sharding import PartitionSpec as P

GROUPS_OF_ROWS = 30


def pack_kernel(
    site_of, route_hbm, count_hbm, jac_hbm, block_hbm, vis_hbm, obs_hbm, out_ref,
    route_ref, count_ref, block_ref, vis_ref, obs_ref, block_scratch, fill_ref, small_sems, tile_sems,
):
    tiles = jac_hbm.shape[0]
    width = jac_hbm.shape[3]
    places = out_ref.shape[0]
    small = [
        pltpu.make_async_copy(source, target, small_sems.at[index])
        for index, (source, target) in enumerate((
            (route_hbm, route_ref), (count_hbm, count_ref), (block_hbm, block_ref),
            (vis_hbm, vis_ref), (obs_hbm, obs_ref),
        ))
    ]
    for copy in small:
        copy.start()
    dead = jnp.full((4, width), -1.0, jnp.bfloat16)

    def clear(place, carry):
        fill_ref[place] = 0
        out_ref[place, 0, 27] = dead
        out_ref[place, 1, 27] = dead
        return carry

    lax.fori_loop(0, places, clear, 0, unroll=8)
    plane = lax.axis_index("zp")
    small[0].wait()

    def send(tile, carry):
        place = site_of(route_ref[tile], plane)
        slot = fill_ref[place]
        fill_ref[place] = slot + 1
        route_ref[tile] = 2 * place + slot
        pltpu.make_async_copy(
            jac_hbm.at[tile], out_ref.at[place, slot, pl.ds(0, 27)], tile_sems.at[tile]
        ).start()
        return carry

    lax.fori_loop(0, tiles, send, 0, unroll=4)
    for copy in small[1:]:
        copy.wait()
    block_scratch[...] = block_ref[...].astype(jnp.float32)
    slot_iota = lax.broadcasted_iota(jnp.int32, (4, width), 0)
    point_iota = lax.broadcasted_iota(jnp.int32, (4, width), 1)

    def fill(tile, carry):
        place = route_ref[tile] >> 1
        slot = route_ref[tile] & 1
        obs = jnp.broadcast_to(obs_ref[pl.ds(tile, 1), :], (4, width))
        live = (slot_iota < obs) & (point_iota < count_ref[tile])
        marks = jnp.where(live, vis_ref[tile], -1).astype(jnp.float32).astype(jnp.bfloat16)
        rows = [block_scratch[c, pl.ds(tile, 1), :] for c in range(6)]
        zero = jnp.zeros_like(rows[0])
        out_ref[place, slot, 27] = marks
        out_ref[place, slot, 28] = jnp.concatenate(rows[:4], axis=0).astype(jnp.bfloat16)
        out_ref[place, slot, 29] = jnp.concatenate(rows[4:] + [zero, zero], axis=0).astype(jnp.bfloat16)
        return carry

    lax.fori_loop(0, tiles, fill, 0, unroll=4)

    def finish(tile, carry):
        pltpu.make_async_copy(jac_hbm.at[0], out_ref.at[0, 0, pl.ds(0, 27)], tile_sems.at[tile]).wait()
        return carry

    lax.fori_loop(0, tiles, finish, 0)


def pack(jac, blocks, vis, obs, counts, route, places, site_of):
    tiles, width = jac.shape[0], jac.shape[3]
    anywhere = pl.BlockSpec(memory_space=pltpu.HBM)
    return pl.pallas_call(
        functools.partial(pack_kernel, site_of),
        out_shape=jax.ShapeDtypeStruct((places, 2, GROUPS_OF_ROWS, 4, width), jnp.bfloat16),
        in_specs=[anywhere] * 6,
        out_specs=pl.BlockSpec(memory_space=pltpu.VMEM),
        scratch_shapes=[
            pltpu.SMEM(route.shape, jnp.int32),
            pltpu.SMEM(counts.shape, jnp.int32),
            pltpu.VMEM(blocks.shape, jnp.bfloat16),
            pltpu.VMEM(vis.shape, jnp.int32),
            pltpu.VMEM(obs.shape, jnp.int32),
            pltpu.VMEM(blocks.shape, jnp.float32),
            pltpu.SMEM((places,), jnp.int32),
            pltpu.SemaphoreType.DMA((5,)),
            pltpu.SemaphoreType.DMA((tiles,)),
        ],
        compiler_params=pltpu.CompilerParams(vmem_limit_bytes=60 * 1024 * 1024),
        cost_estimate=pl.CostEstimate(flops=1000000, bytes_accessed=3000000, transcendentals=0),
        name="pack",
    )(route, counts, jac, blocks, vis, obs)


def inverse_rows(first, second):
    xx, yy, zz, xy = (first[c : c + 1] for c in range(4))
    xz, yz = (second[c : c + 1] for c in range(2))
    cxx = yy * zz - yz * yz
    cyy = xx * zz - xz * xz
    czz = xx * yy - xy * xy
    cxy = xz * yz - xy * zz
    cxz = xy * yz - xz * yy
    cyz = xy * xz - xx * yz
    inv_det = 1.0 / (xx * cxx + xy * cxy + xz * cxz)
    ixx, iyy, izz, ixy, ixz, iyz = (c * inv_det for c in (cxx, cyy, czz, cxy, cxz, cyz))
    return ((ixx, ixy, ixz), (ixy, iyy, iyz), (ixz, iyz, izz))


def expand_slot(got_ref, source, slot, rows_ref, left_ref, right_ref, column, cameras):
    width = got_ref.shape[4]
    first = got_ref[source, slot, 28].astype(jnp.float32)
    second = got_ref[source, slot, 29].astype(jnp.float32)
    inverse = inverse_rows(first, second)
    wide = [[jnp.broadcast_to(entry, (4, width)) for entry in line] for line in inverse]
    rows_ref[27, 0, 0:4] = got_ref[source, slot, 27].astype(jnp.float32)
    iota = lax.broadcasted_iota(jnp.int32, (8, width), 0).astype(jnp.float32)
    marks = [jnp.broadcast_to(rows_ref[27, 0, i : i + 1], (8, width)) for i in range(4)]
    picks = []
    for b in range(cameras // 8):
        pick = jnp.full((8, width), 4, jnp.int32)
        for i in range(4):
            pick = jnp.where(marks[i] == iota + 8.0 * b, i, pick)
        picks.append(pick)
    yield
    for r in range(9):
        factors = [got_ref[source, slot, 3 * r + m].astype(jnp.float32) for m in range(3)]
        values = [
            factors[0] * wide[0][k] + factors[1] * wide[1][k] + factors[2] * wide[2][k] for k in range(3)
        ]
        for k in range(3):
            for value, out in ((values[k], left_ref), (factors[k], right_ref)):
                table = jnp.concatenate([value, jnp.zeros_like(value)], axis=0)
                for b in range(0, cameras // 8, 2):
                    pair = [
                        jnp.take_along_axis(table, picks[b + half], axis=0, mode="promise_in_bounds")
                        for half in range(2)
                    ]
                    out[pl.ds(r * cameras + 8 * b, 16), pl.ds(column + 2 * k * width, width)] = jnp.concatenate(
                        pair, axis=0
                    ).astype(jnp.bfloat16)
        yield


def schur_kernel(cameras, pieces, got_ref, out_ref, *scratch):
    part, wide = 9 * cameras // pieces, 2 * got_ref.shape[4]
    sums = [pltpu.ACC(unit)((part, wide), jnp.float32) for unit in range(2) for _ in range(pieces)]
    pl.run_scoped(functools.partial(schur_body, cameras, got_ref, out_ref, *scratch), *sums)


def schur_body(cameras, got_ref, out_ref, total_ref, rows_ref, left_a, left_b, right_a, right_b, *sums):
    sources = got_ref.shape[0]
    width = got_ref.shape[4]
    side = 9 * cameras
    lefts, rights = (left_a, left_b), (right_a, right_b)
    count = len(sums) // 2
    sums = (sums[:count], sums[count:])
    part = side // count
    wide = 2 * width
    rows_ref[...] = jnp.zeros_like(rows_ref)
    for right in rights:
        right[pl.ds(side, 2 * wide - side), :] = jnp.zeros((2 * wide - side, 3 * wide), jnp.bfloat16)

    def expand(source, buffer):
        for slot in range(2):
            yield from expand_slot(
                got_ref, source, slot, rows_ref.at[slot], lefts[buffer], rights[buffer], slot * width, cameras,
            )

    def multiply(buffer):
        for k in range(3):
            columns = pl.ds(k * wide, wide)
            for unit in range(2):
                pltpu.matmul_push_rhs(
                    rights[buffer][pl.ds(unit * wide, wide), columns], k % 2, unit, transpose=True
                )
            for piece in range(count):
                value = lefts[buffer][pl.ds(piece * part, part), columns]
                for unit in range(2):
                    pltpu.matmul_acc_lhs(sums[unit][piece], value, k % 2 if piece == 0 else None)
                yield

    def both(source, buffer):
        one = expand(source, buffer)
        two = multiply(1 - buffer)
        each = -(-20 // (3 * count))
        steps, alive = 0, True
        while alive:
            alive = next(two, 1) is None
            steps += 20
            while steps >= 3 * count:
                steps -= 3 * count
                next(one, 1)
        for _ in one:
            pass

    for _ in expand(0, 0):
        pass

    def step(turn, carry):
        both(2 * turn + 1, 1)
        both(jnp.minimum(2 * turn + 2, sources - 1), 0)
        return carry

    lax.fori_loop(0, sources // 2, step, 0)
    for piece in range(count):
        rows = pl.ds(piece * part, part)
        total_ref[rows, 0:wide] = pltpu.matmul_pop(sums[0][piece])
        total_ref[rows, wide:side] = pltpu.matmul_pop(sums[1][piece])[:, : side - wide]
    share = side // out_ref.shape[0]
    full, half = side // width, share // 2
    rest = side - full * width
    for piece in range(out_ref.shape[0]):
        out_ref[piece, pl.ds(full * share, out_ref.shape[1] - full * share)] = jnp.zeros(
            (out_ref.shape[1] - full * share, width), jnp.float32
        )
        for lane in range(full):
            out_ref[piece, pl.ds(lane * share, share)] = total_ref[
                pl.ds(piece * share, share), lane * width : (lane + 1) * width
            ]
        for step in range(2):
            out_ref[piece, pl.ds(full * share, half), step * rest : (step + 1) * rest] = total_ref[
                pl.ds(piece * share + step * half, half), full * width : side
            ]


def send_kernel(used, ours_ref, came_ref, *out_refs):
    layer, row = lax.axis_index("layer"), lax.axis_index("pair")
    lines, width = came_ref.shape[1:]
    line = lax.broadcasted_iota(jnp.int32, (lines, width), 0)
    for turn, out_ref in enumerate(out_refs):
        value = ours_ref[layer, row ^ turn] + came_ref[row ^ turn]
        largest = jnp.maximum(jnp.max(jnp.abs(value), axis=0, keepdims=True), 2e-34)
        power = jnp.floor(jnp.log2(largest)) - 14.0
        steps = jnp.clip(jnp.round(value * jnp.exp2(-power)), -32767.0, 32767.0)
        steps = jnp.where(line == used, jnp.broadcast_to(power, steps.shape), steps)
        out_ref[...] = steps.astype(jnp.int32).astype(jnp.int16)


def to_send(ours, came, used):
    vmem = pl.BlockSpec(memory_space=pltpu.VMEM)
    shape = jax.ShapeDtypeStruct(came.shape[1:], jnp.int16)
    return pl.pallas_call(
        functools.partial(send_kernel, used),
        out_shape=[shape] * came.shape[0],
        in_specs=[vmem, vmem],
        out_specs=[vmem] * came.shape[0],
        compiler_params=pltpu.CompilerParams(vmem_limit_bytes=16 * 1024 * 1024),
        cost_estimate=pl.CostEstimate(flops=1000000, bytes_accessed=2000000, transcendentals=0),
        name="to_send",
    )(ours, came)


def finish_kernel(cameras, lines_ref, *refs):
    pieces, out_ref = refs[:-1], refs[-1]
    share, _, side = out_ref.shape
    width = pieces[0].shape[1]
    used = side // width * share + share // 2
    total = None
    for piece in pieces:
        steps = piece[...].astype(jnp.int32).astype(jnp.float32)
        value = steps * jnp.broadcast_to(jnp.exp2(steps[used : used + 1]), steps.shape)
        total = value if total is None else total + value
    start = (lax.axis_index("layer") * lax.axis_size("pair") + lax.axis_index("pair")) * share
    first = start // cameras
    row = start + lax.broadcasted_iota(jnp.int32, (share, side), 0)
    column = lax.broadcasted_iota(jnp.int32, (share, side), 1)
    own = jnp.zeros((share, side), jnp.float32)
    for step in range(-(-share // cameras) + 1):
        line = lines_ref[pl.ds(jnp.minimum(first + step, lines_ref.shape[0] - 1), 1), :]
        own = jnp.where(row // cameras == first + step, jnp.broadcast_to(line, (share, side)), own)
    own = jnp.where(row % cameras == column % cameras, own, 0.0)
    full, half = side // width, share // 2
    rest = side - full * width
    for lane in range(full):
        columns = slice(lane * width, (lane + 1) * width)
        out_ref[:, 0, columns] = own[:, columns] - total[lane * share : (lane + 1) * share]
    for step in range(2):
        rows, columns = slice(step * half, (step + 1) * half), slice(full * width, side)
        out_ref[rows, 0, columns] = (
            own[rows, columns] - total[full * share : full * share + half, step * rest : (step + 1) * rest]
        )


def finish(lines, pieces, cameras, share):
    vmem = pl.BlockSpec(memory_space=pltpu.VMEM)
    return pl.pallas_call(
        functools.partial(finish_kernel, cameras),
        out_shape=jax.ShapeDtypeStruct((share, 1, lines.shape[1]), jnp.float32),
        in_specs=[vmem] * (1 + len(pieces)),
        out_specs=vmem,
        compiler_params=pltpu.CompilerParams(vmem_limit_bytes=16 * 1024 * 1024),
        cost_estimate=pl.CostEstimate(flops=200000, bytes_accessed=500000, transcendentals=0),
        name="finish",
    )(lines, *pieces)


def schur_partial(got, cameras, shares):
    width = got.shape[4]
    side = 9 * cameras
    pieces = 9
    vmem = pl.BlockSpec(memory_space=pltpu.VMEM)
    share = side // shares
    lines = side // width * share + share // 2
    return pl.pallas_call(
        functools.partial(schur_kernel, cameras, pieces),
        out_shape=jax.ShapeDtypeStruct((shares, lines + -lines % 8, width), jnp.float32),
        in_specs=[vmem],
        out_specs=vmem,
        scratch_shapes=[
            pltpu.VMEM((side, side), jnp.float32),
            pltpu.VMEM((2, 28, 2, 8, width), jnp.float32),
            pltpu.VMEM((side, 6 * width), jnp.bfloat16),
            pltpu.VMEM((side, 6 * width), jnp.bfloat16),
            pltpu.VMEM((4 * width, 6 * width), jnp.bfloat16),
            pltpu.VMEM((4 * width, 6 * width), jnp.bfloat16),
        ],
        compiler_params=pltpu.CompilerParams(vmem_limit_bytes=32 * 1024 * 1024),
        cost_estimate=pl.CostEstimate(flops=10000000000, bytes_accessed=3000000, transcendentals=0),
        name="schur_partial",
    )(got)


AXES = ("layer", "zp", "zb", "x", "pair")


def local(sizes, jac_blocks, point_blocks, visibility, obs_count, tile_count, route, camera_blocks):
    cameras = camera_blocks.shape[3]
    side = 9 * cameras
    layers, pairs, far, near, across = (lax.axis_size(a) for a in ("layer", "pair", "zp", "zb", "x"))
    shares = layers * pairs

    def site_of(group, plane):
        side_z = (group >> bits(across)) & (near - 1)
        y = ((group >> bits(across * near)) + pairs - plane + 2 * side_z) & (pairs - 1)
        return side_z * (across * pairs) + (group & (across - 1)) * pairs + y

    packed = pack(
        jac_blocks.transpose(0, 2, 1, 3), point_blocks.transpose(1, 0, 2), visibility, obs_count, tile_count,
        route[:, 0], near * across * pairs, site_of,
    )
    lines = camera_blocks[0].reshape(9, side)
    got = lax.all_to_all(packed, ("zb", "x", "pair"), split_axis=0, concat_axis=0, tiled=True)
    got, lines = lax.optimization_barrier((got, lines))
    partial_value = schur_partial(got, cameras, shares)
    partial_value = partial_value.reshape((layers, pairs) + partial_value.shape[1:])
    layer = lax.axis_index("layer")
    theirs = lax.dynamic_index_in_dim(partial_value, 1 - layer, 0, keepdims=False)
    came = lax.ppermute(theirs, "layer", [(0, 1), (1, 0)])
    share = side // shares
    width = partial_value.shape[3]
    parcels = to_send(partial_value, came, side // width * share + share // 2)
    pieces = []
    for turn in sorted(range(far), key=lambda turn: -min(turn, pairs - turn)):
        links = []
        for source in itertools.product(*(range(size) for size in sizes)):
            c, zp, zb, x, y = source
            links.append((flat(source, sizes), flat((c, (y + zp + 2 * zb) % far, zb, x, y ^ turn), sizes)))
        pieces.append(lax.ppermute(parcels[turn], AXES, links))
    return finish(lines, pieces, cameras, share).transpose(1, 0, 2)


def bits(size):
    assert size & (size - 1) == 0
    return size.bit_length() - 1


def flat(place, sizes):
    index = 0
    for coordinate, size in zip(place, sizes):
        index = index * size + coordinate
    return index


def solution(mesh):
    layers, cams, pairs = mesh.devices.shape
    across = 4
    near = 2
    sizes = (layers, cams // (near * across), near, across, pairs)
    split = jax.sharding.Mesh(mesh.devices.reshape(sizes), AXES)
    cam = ("zp", "zb", "x")
    placed = (
        P(AXES, None, None, None),
        P(AXES, None, None),
        P(AXES, None, None),
        P(AXES, None),
        P(AXES),
        P(AXES, None),
        P(cam, None, None, None),
    )
    return jax.shard_map(
        functools.partial(local, sizes),
        mesh=split,
        in_specs=placed,
        out_specs=P(cam, ("layer", "pair"), None),
        check_vma=False,
    )
```

```python
import functools
import itertools

import jax
import jax.numpy as jnp
from jax import lax
from jax.experimental import pallas as pl
from jax.experimental.pallas import tpu as pltpu
from jax.sharding import PartitionSpec as P

GROUPS_OF_ROWS = 30


def pack_kernel(
    site_of, route_hbm, count_hbm, jac_hbm, block_hbm, vis_hbm, obs_hbm, out_ref,
    route_ref, count_ref, block_ref, vis_ref, obs_ref, block_scratch, fill_ref, small_sems, tile_sems,
):
    tiles = jac_hbm.shape[0]
    width = jac_hbm.shape[3]
    places = out_ref.shape[0]
    small = [
        pltpu.make_async_copy(source, target, small_sems.at[index])
        for index, (source, target) in enumerate((
            (route_hbm, route_ref), (count_hbm, count_ref), (block_hbm, block_ref),
            (vis_hbm, vis_ref), (obs_hbm, obs_ref),
        ))
    ]
    for copy in small:
        copy.start()
    dead = jnp.full((4, width), -1.0, jnp.bfloat16)

    def clear(place, carry):
        fill_ref[place] = 0
        out_ref[place, 0, 27] = dead
        out_ref[place, 1, 27] = dead
        return carry

    lax.fori_loop(0, places, clear, 0, unroll=8)
    plane = lax.axis_index("zp")
    small[0].wait()

    def send(tile, carry):
        place = site_of(route_ref[tile], plane)
        slot = fill_ref[place]
        fill_ref[place] = slot + 1
        route_ref[tile] = 2 * place + slot
        pltpu.make_async_copy(
            jac_hbm.at[tile], out_ref.at[place, slot, pl.ds(0, 27)], tile_sems.at[tile]
        ).start()
        return carry

    lax.fori_loop(0, tiles, send, 0, unroll=4)
    for copy in small[1:]:
        copy.wait()
    block_scratch[...] = block_ref[...].astype(jnp.float32)
    slot_iota = lax.broadcasted_iota(jnp.int32, (4, width), 0)
    point_iota = lax.broadcasted_iota(jnp.int32, (4, width), 1)

    def fill(tile, carry):
        place = route_ref[tile] >> 1
        slot = route_ref[tile] & 1
        obs = jnp.broadcast_to(obs_ref[pl.ds(tile, 1), :], (4, width))
        live = (slot_iota < obs) & (point_iota < count_ref[tile])
        marks = jnp.where(live, vis_ref[tile], -1).astype(jnp.float32).astype(jnp.bfloat16)
        rows = [block_scratch[c, pl.ds(tile, 1), :] for c in range(6)]
        zero = jnp.zeros_like(rows[0])
        out_ref[place, slot, 27] = marks
        out_ref[place, slot, 28] = jnp.concatenate(rows[:4], axis=0).astype(jnp.bfloat16)
        out_ref[place, slot, 29] = jnp.concatenate(rows[4:] + [zero, zero], axis=0).astype(jnp.bfloat16)
        return carry

    lax.fori_loop(0, tiles, fill, 0, unroll=4)

    def finish(tile, carry):
        pltpu.make_async_copy(jac_hbm.at[0], out_ref.at[0, 0, pl.ds(0, 27)], tile_sems.at[tile]).wait()
        return carry

    lax.fori_loop(0, tiles, finish, 0)


def pack(jac, blocks, vis, obs, counts, route, places, site_of):
    tiles, width = jac.shape[0], jac.shape[3]
    anywhere = pl.BlockSpec(memory_space=pltpu.HBM)
    return pl.pallas_call(
        functools.partial(pack_kernel, site_of),
        out_shape=jax.ShapeDtypeStruct((places, 2, GROUPS_OF_ROWS, 4, width), jnp.bfloat16),
        in_specs=[anywhere] * 6,
        out_specs=pl.BlockSpec(memory_space=pltpu.VMEM),
        scratch_shapes=[
            pltpu.SMEM(route.shape, jnp.int32),
            pltpu.SMEM(counts.shape, jnp.int32),
            pltpu.VMEM(blocks.shape, jnp.bfloat16),
            pltpu.VMEM(vis.shape, jnp.int32),
            pltpu.VMEM(obs.shape, jnp.int32),
            pltpu.VMEM(blocks.shape, jnp.float32),
            pltpu.SMEM((places,), jnp.int32),
            pltpu.SemaphoreType.DMA((5,)),
            pltpu.SemaphoreType.DMA((tiles,)),
        ],
        compiler_params=pltpu.CompilerParams(vmem_limit_bytes=60 * 1024 * 1024),
        cost_estimate=pl.CostEstimate(flops=1000000, bytes_accessed=3000000, transcendentals=0),
        name="pack",
    )(route, counts, jac, blocks, vis, obs)


def inverse_rows(first, second):
    xx, yy, zz, xy = (first[c : c + 1] for c in range(4))
    xz, yz = (second[c : c + 1] for c in range(2))
    cxx = yy * zz - yz * yz
    cyy = xx * zz - xz * xz
    czz = xx * yy - xy * xy
    cxy = xz * yz - xy * zz
    cxz = xy * yz - xz * yy
    cyz = xy * xz - xx * yz
    inv_det = 1.0 / (xx * cxx + xy * cxy + xz * cxz)
    ixx, iyy, izz, ixy, ixz, iyz = (c * inv_det for c in (cxx, cyy, czz, cxy, cxz, cyz))
    return ((ixx, ixy, ixz), (ixy, iyy, iyz), (ixz, iyz, izz))


def expand_slot(got_ref, source, slot, rows_ref, left_ref, right_ref, column, cameras):
    width = got_ref.shape[4]
    first = got_ref[source, slot, 28].astype(jnp.float32)
    second = got_ref[source, slot, 29].astype(jnp.float32)
    inverse = inverse_rows(first, second)
    wide = [[jnp.broadcast_to(entry, (4, width)) for entry in line] for line in inverse]
    rows_ref[27, 0, 0:4] = got_ref[source, slot, 27].astype(jnp.float32)
    iota = lax.broadcasted_iota(jnp.int32, (8, width), 0).astype(jnp.float32)
    marks = [jnp.broadcast_to(rows_ref[27, 0, i : i + 1], (8, width)) for i in range(4)]
    picks = []
    for b in range(cameras // 8):
        pick = jnp.full((8, width), 4, jnp.int32)
        for i in range(4):
            pick = jnp.where(marks[i] == iota + 8.0 * b, i, pick)
        picks.append(pick)
    yield
    for r in range(9):
        factors = [got_ref[source, slot, 3 * r + m].astype(jnp.float32) for m in range(3)]
        values = [
            factors[0] * wide[0][k] + factors[1] * wide[1][k] + factors[2] * wide[2][k] for k in range(3)
        ]
        for k in range(3):
            for value, out in ((values[k], left_ref), (factors[k], right_ref)):
                table = jnp.concatenate([value, jnp.zeros_like(value)], axis=0)
                for b in range(0, cameras // 8, 2):
                    pair = [
                        jnp.take_along_axis(table, picks[b + half], axis=0, mode="promise_in_bounds")
                        for half in range(2)
                    ]
                    out[pl.ds(r * cameras + 8 * b, 16), pl.ds(column + 2 * k * width, width)] = jnp.concatenate(
                        pair, axis=0
                    ).astype(jnp.bfloat16)
        yield


def schur_kernel(cameras, pieces, got_ref, out_ref, *scratch):
    part, wide = 9 * cameras // pieces, 2 * got_ref.shape[4]
    sums = [pltpu.ACC(unit)((part, wide), jnp.float32) for unit in range(2) for _ in range(pieces)]
    pl.run_scoped(functools.partial(schur_body, cameras, got_ref, out_ref, *scratch), *sums)


def schur_body(cameras, got_ref, out_ref, total_ref, rows_ref, left_a, left_b, right_a, right_b, *sums):
    sources = got_ref.shape[0]
    width = got_ref.shape[4]
    side = 9 * cameras
    lefts, rights = (left_a, left_b), (right_a, right_b)
    count = len(sums) // 2
    sums = (sums[:count], sums[count:])
    part = side // count
    wide = 2 * width
    rows_ref[...] = jnp.zeros_like(rows_ref)
    for right in rights:
        right[pl.ds(side, 2 * wide - side), :] = jnp.zeros((2 * wide - side, 3 * wide), jnp.bfloat16)

    def expand(source, buffer):
        for slot in range(2):
            yield from expand_slot(
                got_ref, source, slot, rows_ref.at[slot], lefts[buffer], rights[buffer], slot * width, cameras,
            )

    def multiply(buffer):
        for k in range(3):
            columns = pl.ds(k * wide, wide)
            for unit in range(2):
                pltpu.matmul_push_rhs(
                    rights[buffer][pl.ds(unit * wide, wide), columns], k % 2, unit, transpose=True
                )
            for piece in range(count):
                value = lefts[buffer][pl.ds(piece * part, part), columns]
                for unit in range(2):
                    pltpu.matmul_acc_lhs(sums[unit][piece], value, k % 2 if piece == 0 else None)
                yield

    def both(source, buffer):
        one = expand(source, buffer)
        two = multiply(1 - buffer)
        each = -(-20 // (3 * count))
        steps, alive = 0, True
        while alive:
            alive = next(two, 1) is None
            steps += 20
            while steps >= 3 * count:
                steps -= 3 * count
                next(one, 1)
        for _ in one:
            pass

    for _ in expand(0, 0):
        pass

    def step(turn, carry):
        both(2 * turn + 1, 1)
        both(jnp.minimum(2 * turn + 2, sources - 1), 0)
        return carry

    lax.fori_loop(0, sources // 2, step, 0)
    for piece in range(count):
        rows = pl.ds(piece * part, part)
        total_ref[rows, 0:wide] = pltpu.matmul_pop(sums[0][piece])
        total_ref[rows, wide:side] = pltpu.matmul_pop(sums[1][piece])[:, : side - wide]
    share = side // out_ref.shape[0]
    full, half = side // width, share // 2
    rest = side - full * width
    for piece in range(out_ref.shape[0]):
        out_ref[piece, pl.ds(full * share, out_ref.shape[1] - full * share)] = jnp.zeros(
            (out_ref.shape[1] - full * share, width), jnp.float32
        )
        for lane in range(full):
            out_ref[piece, pl.ds(lane * share, share)] = total_ref[
                pl.ds(piece * share, share), lane * width : (lane + 1) * width
            ]
        for step in range(2):
            out_ref[piece, pl.ds(full * share, half), step * rest : (step + 1) * rest] = total_ref[
                pl.ds(piece * share + step * half, half), full * width : side
            ]


def send_kernel(used, ours_ref, came_ref, *out_refs):
    layer, row = lax.axis_index("layer"), lax.axis_index("pair")
    lines, width = came_ref.shape[1:]
    line = lax.broadcasted_iota(jnp.int32, (lines, width), 0)
    for turn, out_ref in enumerate(out_refs):
        value = ours_ref[layer, row ^ turn] + came_ref[row ^ turn]
        largest = jnp.maximum(jnp.max(jnp.abs(value), axis=0, keepdims=True), 2e-34)
        power = jnp.floor(jnp.log2(largest)) - 14.0
        steps = jnp.clip(jnp.round(value * jnp.exp2(-power)), -32767.0, 32767.0)
        steps = jnp.where(line == used, jnp.broadcast_to(power, steps.shape), steps)
        out_ref[...] = steps.astype(jnp.int32).astype(jnp.int16)


def to_send(ours, came, used):
    vmem = pl.BlockSpec(memory_space=pltpu.VMEM)
    shape = jax.ShapeDtypeStruct(came.shape[1:], jnp.int16)
    return pl.pallas_call(
        functools.partial(send_kernel, used),
        out_shape=[shape] * came.shape[0],
        in_specs=[vmem, vmem],
        out_specs=[vmem] * came.shape[0],
        compiler_params=pltpu.CompilerParams(vmem_limit_bytes=16 * 1024 * 1024),
        cost_estimate=pl.CostEstimate(flops=1000000, bytes_accessed=2000000, transcendentals=0),
        name="to_send",
    )(ours, came)


def own_kernel(cameras, lines_ref, out_ref):
    share, side = out_ref.shape
    start = (lax.axis_index("layer") * lax.axis_size("pair") + lax.axis_index("pair")) * share
    first = start // cameras
    row = start + lax.broadcasted_iota(jnp.int32, (share, side), 0)
    column = lax.broadcasted_iota(jnp.int32, (share, side), 1)
    own = jnp.zeros((share, side), jnp.float32)
    for step in range(-(-share // cameras) + 1):
        line = lines_ref[pl.ds(jnp.minimum(first + step, lines_ref.shape[0] - 1), 1), :]
        own = jnp.where(row // cameras == first + step, jnp.broadcast_to(line, (share, side)), own)
    out_ref[...] = jnp.where(row % cameras == column % cameras, own, 0.0)


def own_blocks(lines, cameras, share):
    vmem = pl.BlockSpec(memory_space=pltpu.VMEM)
    return pl.pallas_call(
        functools.partial(own_kernel, cameras),
        out_shape=jax.ShapeDtypeStruct((share, lines.shape[1]), jnp.float32),
        in_specs=[vmem],
        out_specs=vmem,
        compiler_params=pltpu.CompilerParams(vmem_limit_bytes=16 * 1024 * 1024),
        cost_estimate=pl.CostEstimate(flops=200000, bytes_accessed=100000, transcendentals=0),
        name="own_blocks",
    )(lines)


def finish_kernel(own_ref, *refs):
    pieces, out_ref = refs[:-1], refs[-1]
    share, _, side = out_ref.shape
    width = pieces[0].shape[1]
    used = side // width * share + share // 2
    total = None
    for piece in pieces:
        steps = piece[...].astype(jnp.int32).astype(jnp.float32)
        value = steps * jnp.broadcast_to(jnp.exp2(steps[used : used + 1]), steps.shape)
        total = value if total is None else total + value
    own = own_ref[...]
    full, half = side // width, share // 2
    rest = side - full * width
    for lane in range(full):
        columns = slice(lane * width, (lane + 1) * width)
        out_ref[:, 0, columns] = own[:, columns] - total[lane * share : (lane + 1) * share]
    for step in range(2):
        rows, columns = slice(step * half, (step + 1) * half), slice(full * width, side)
        out_ref[rows, 0, columns] = (
            own[rows, columns] - total[full * share : full * share + half, step * rest : (step + 1) * rest]
        )


def finish(own, pieces):
    share, side = own.shape
    vmem = pl.BlockSpec(memory_space=pltpu.VMEM)
    return pl.pallas_call(
        finish_kernel,
        out_shape=jax.ShapeDtypeStruct((share, 1, side), jnp.float32),
        in_specs=[vmem] * (1 + len(pieces)),
        out_specs=vmem,
        compiler_params=pltpu.CompilerParams(vmem_limit_bytes=16 * 1024 * 1024),
        cost_estimate=pl.CostEstimate(flops=200000, bytes_accessed=500000, transcendentals=0),
        name="finish",
    )(own, *pieces)


def schur_partial(got, cameras, shares):
    width = got.shape[4]
    side = 9 * cameras
    pieces = 9
    vmem = pl.BlockSpec(memory_space=pltpu.VMEM)
    share = side // shares
    lines = side // width * share + share // 2
    return pl.pallas_call(
        functools.partial(schur_kernel, cameras, pieces),
        out_shape=jax.ShapeDtypeStruct((shares, lines + -lines % 8, width), jnp.float32),
        in_specs=[vmem],
        out_specs=vmem,
        scratch_shapes=[
            pltpu.VMEM((side, side), jnp.float32),
            pltpu.VMEM((2, 28, 2, 8, width), jnp.float32),
            pltpu.VMEM((side, 6 * width), jnp.bfloat16),
            pltpu.VMEM((side, 6 * width), jnp.bfloat16),
            pltpu.VMEM((4 * width, 6 * width), jnp.bfloat16),
            pltpu.VMEM((4 * width, 6 * width), jnp.bfloat16),
        ],
        compiler_params=pltpu.CompilerParams(vmem_limit_bytes=32 * 1024 * 1024),
        cost_estimate=pl.CostEstimate(flops=10000000000, bytes_accessed=3000000, transcendentals=0),
        name="schur_partial",
    )(got)


AXES = ("layer", "zp", "zb", "x", "pair")


def local(sizes, jac_blocks, point_blocks, visibility, obs_count, tile_count, route, camera_blocks):
    cameras = camera_blocks.shape[3]
    side = 9 * cameras
    layers, pairs, far, near, across = (lax.axis_size(a) for a in ("layer", "pair", "zp", "zb", "x"))
    shares = layers * pairs

    def site_of(group, plane):
        side_z = (group >> bits(across)) & (near - 1)
        y = ((group >> bits(across * near)) + pairs - plane + 2 * side_z) & (pairs - 1)
        return side_z * (across * pairs) + (group & (across - 1)) * pairs + y

    packed = pack(
        jac_blocks.transpose(0, 2, 1, 3), point_blocks.transpose(1, 0, 2), visibility, obs_count, tile_count,
        route[:, 0], near * across * pairs, site_of,
    )
    own = own_blocks(camera_blocks[0].reshape(9, side), cameras, side // shares)
    got = lax.all_to_all(packed, ("zb", "x", "pair"), split_axis=0, concat_axis=0, tiled=True)
    got, own = lax.optimization_barrier((got, own))
    partial_value = schur_partial(got, cameras, shares)
    partial_value = partial_value.reshape((layers, pairs) + partial_value.shape[1:])
    layer = lax.axis_index("layer")
    theirs = lax.dynamic_index_in_dim(partial_value, 1 - layer, 0, keepdims=False)
    came = lax.ppermute(theirs, "layer", [(0, 1), (1, 0)])
    share = side // shares
    width = partial_value.shape[3]
    parcels = to_send(partial_value, came, side // width * share + share // 2)
    pieces = []
    for turn in sorted(range(far), key=lambda turn: -min(turn, pairs - turn)):
        links = []
        for source in itertools.product(*(range(size) for size in sizes)):
            c, zp, zb, x, y = source
            links.append((flat(source, sizes), flat((c, (y + zp + 2 * zb) % far, zb, x, y ^ turn), sizes)))
        pieces.append(lax.ppermute(parcels[turn], AXES, links))
    return finish(own, pieces).transpose(1, 0, 2)


def bits(size):
    assert size & (size - 1) == 0
    return size.bit_length() - 1


def flat(place, sizes):
    index = 0
    for coordinate, size in zip(place, sizes):
        index = index * size + coordinate
    return index


def solution(mesh):
    layers, cams, pairs = mesh.devices.shape
    across = 4
    near = 2
    sizes = (layers, cams // (near * across), near, across, pairs)
    split = jax.sharding.Mesh(mesh.devices.reshape(sizes), AXES)
    cam = ("zp", "zb", "x")
    placed = (
        P(AXES, None, None, None),
        P(AXES, None, None),
        P(AXES, None, None),
        P(AXES, None),
        P(AXES),
        P(AXES, None),
        P(cam, None, None, None),
    )
    return jax.shard_map(
        functools.partial(local, sizes),
        mesh=split,
        in_specs=placed,
        out_specs=P(cam, ("layer", "pair"), None),
        check_vma=False,
    )
```

```python
import functools
import itertools

import jax
import jax.numpy as jnp
from jax import lax
from jax.experimental import pallas as pl
from jax.experimental.pallas import tpu as pltpu
from jax.sharding import PartitionSpec as P

GROUPS_OF_ROWS = 30


def pack_kernel(
    site_of, route_hbm, count_hbm, jac_hbm, block_hbm, vis_hbm, obs_hbm, out_ref,
    route_ref, count_ref, block_ref, vis_ref, obs_ref, block_scratch, fill_ref, small_sems, tile_sems,
):
    tiles = jac_hbm.shape[0]
    width = jac_hbm.shape[3]
    places = out_ref.shape[0]
    small = [
        pltpu.make_async_copy(source, target, small_sems.at[index])
        for index, (source, target) in enumerate((
            (route_hbm, route_ref), (count_hbm, count_ref), (block_hbm, block_ref),
            (vis_hbm, vis_ref), (obs_hbm, obs_ref),
        ))
    ]
    for copy in small:
        copy.start()
    dead = jnp.full((4, width), -1.0, jnp.bfloat16)

    def clear(place, carry):
        fill_ref[place] = 0
        out_ref[place, 0, 27] = dead
        out_ref[place, 1, 27] = dead
        return carry

    lax.fori_loop(0, places, clear, 0, unroll=8)
    plane = lax.axis_index("zp")
    small[0].wait()

    def send(tile, carry):
        place = site_of(route_ref[tile], plane)
        slot = fill_ref[place]
        fill_ref[place] = slot + 1
        route_ref[tile] = 2 * place + slot
        pltpu.make_async_copy(
            jac_hbm.at[tile], out_ref.at[place, slot, pl.ds(0, 27)], tile_sems.at[tile]
        ).start()
        return carry

    lax.fori_loop(0, tiles, send, 0, unroll=4)
    for copy in small[1:]:
        copy.wait()
    block_scratch[...] = block_ref[...].astype(jnp.float32)
    slot_iota = lax.broadcasted_iota(jnp.int32, (4, width), 0)
    point_iota = lax.broadcasted_iota(jnp.int32, (4, width), 1)

    def fill(tile, carry):
        place = route_ref[tile] >> 1
        slot = route_ref[tile] & 1
        obs = jnp.broadcast_to(obs_ref[pl.ds(tile, 1), :], (4, width))
        live = (slot_iota < obs) & (point_iota < count_ref[tile])
        marks = jnp.where(live, vis_ref[tile], -1).astype(jnp.float32).astype(jnp.bfloat16)
        rows = [block_scratch[c, pl.ds(tile, 1), :] for c in range(6)]
        zero = jnp.zeros_like(rows[0])
        out_ref[place, slot, 27] = marks
        out_ref[place, slot, 28] = jnp.concatenate(rows[:4], axis=0).astype(jnp.bfloat16)
        out_ref[place, slot, 29] = jnp.concatenate(rows[4:] + [zero, zero], axis=0).astype(jnp.bfloat16)
        return carry

    lax.fori_loop(0, tiles, fill, 0, unroll=4)

    def finish(tile, carry):
        pltpu.make_async_copy(jac_hbm.at[0], out_ref.at[0, 0, pl.ds(0, 27)], tile_sems.at[tile]).wait()
        return carry

    lax.fori_loop(0, tiles, finish, 0)


def pack(jac, blocks, vis, obs, counts, route, places, site_of):
    tiles, width = jac.shape[0], jac.shape[3]
    anywhere = pl.BlockSpec(memory_space=pltpu.HBM)
    return pl.pallas_call(
        functools.partial(pack_kernel, site_of),
        out_shape=jax.ShapeDtypeStruct((places, 2, GROUPS_OF_ROWS, 4, width), jnp.bfloat16),
        in_specs=[anywhere] * 6,
        out_specs=pl.BlockSpec(memory_space=pltpu.VMEM),
        scratch_shapes=[
            pltpu.SMEM(route.shape, jnp.int32),
            pltpu.SMEM(counts.shape, jnp.int32),
            pltpu.VMEM(blocks.shape, jnp.bfloat16),
            pltpu.VMEM(vis.shape, jnp.int32),
            pltpu.VMEM(obs.shape, jnp.int32),
            pltpu.VMEM(blocks.shape, jnp.float32),
            pltpu.SMEM((places,), jnp.int32),
            pltpu.SemaphoreType.DMA((5,)),
            pltpu.SemaphoreType.DMA((tiles,)),
        ],
        compiler_params=pltpu.CompilerParams(vmem_limit_bytes=60 * 1024 * 1024),
        cost_estimate=pl.CostEstimate(flops=1000000, bytes_accessed=3000000, transcendentals=0),
        name="pack",
    )(route, counts, jac, blocks, vis, obs)


def inverse_rows(first, second):
    xx, yy, zz, xy = (first[c : c + 1] for c in range(4))
    xz, yz = (second[c : c + 1] for c in range(2))
    cxx = yy * zz - yz * yz
    cyy = xx * zz - xz * xz
    czz = xx * yy - xy * xy
    cxy = xz * yz - xy * zz
    cxz = xy * yz - xz * yy
    cyz = xy * xz - xx * yz
    inv_det = 1.0 / (xx * cxx + xy * cxy + xz * cxz)
    ixx, iyy, izz, ixy, ixz, iyz = (c * inv_det for c in (cxx, cyy, czz, cxy, cxz, cyz))
    return ((ixx, ixy, ixz), (ixy, iyy, iyz), (ixz, iyz, izz))


def expand_slot(got_ref, source, slot, rows_ref, left_ref, right_ref, column, cameras):
    width = got_ref.shape[4]
    first = got_ref[source, slot, 28].astype(jnp.float32)
    second = got_ref[source, slot, 29].astype(jnp.float32)
    inverse = inverse_rows(first, second)
    wide = [[jnp.broadcast_to(entry, (4, width)) for entry in line] for line in inverse]
    rows_ref[27, 0, 0:4] = got_ref[source, slot, 27].astype(jnp.float32)
    iota = lax.broadcasted_iota(jnp.int32, (8, width), 0).astype(jnp.float32)
    marks = [jnp.broadcast_to(rows_ref[27, 0, i : i + 1], (8, width)) for i in range(4)]
    picks = []
    for b in range(cameras // 8):
        pick = jnp.full((8, width), 4, jnp.int32)
        for i in range(4):
            pick = jnp.where(marks[i] == iota + 8.0 * b, i, pick)
        picks.append(pick)
    yield
    for r in range(9):
        factors = [got_ref[source, slot, 3 * r + m].astype(jnp.float32) for m in range(3)]
        values = [
            factors[0] * wide[0][k] + factors[1] * wide[1][k] + factors[2] * wide[2][k] for k in range(3)
        ]
        for k in range(3):
            for value, out in ((values[k], left_ref), (factors[k], right_ref)):
                table = jnp.concatenate([value, jnp.zeros_like(value)], axis=0)
                for b in range(0, cameras // 8, 2):
                    pair = [
                        jnp.take_along_axis(table, picks[b + half], axis=0, mode="promise_in_bounds")
                        for half in range(2)
                    ]
                    out[pl.ds(r * cameras + 8 * b, 16), pl.ds(column + 2 * k * width, width)] = jnp.concatenate(
                        pair, axis=0
                    ).astype(jnp.bfloat16)
        yield


def schur_kernel(cameras, pieces, got_ref, out_ref, *scratch):
    part, wide = 9 * cameras // pieces, 2 * got_ref.shape[4]
    sums = [pltpu.ACC(unit)((part, wide), jnp.float32) for unit in range(2) for _ in range(pieces)]
    pl.run_scoped(functools.partial(schur_body, cameras, got_ref, out_ref, *scratch), *sums)


def schur_body(cameras, got_ref, out_ref, total_ref, rows_ref, left_a, left_b, right_a, right_b, *sums):
    sources = got_ref.shape[0]
    width = got_ref.shape[4]
    side = 9 * cameras
    lefts, rights = (left_a, left_b), (right_a, right_b)
    count = len(sums) // 2
    sums = (sums[:count], sums[count:])
    part = side // count
    wide = 2 * width
    rows_ref[...] = jnp.zeros_like(rows_ref)
    for right in rights:
        right[pl.ds(side, 2 * wide - side), :] = jnp.zeros((2 * wide - side, 3 * wide), jnp.bfloat16)

    def expand(source, buffer):
        for slot in range(2):
            yield from expand_slot(
                got_ref, source, slot, rows_ref.at[slot], lefts[buffer], rights[buffer], slot * width, cameras,
            )

    def multiply(buffer):
        for k in range(3):
            columns = pl.ds(k * wide, wide)
            for unit in range(2):
                pltpu.matmul_push_rhs(
                    rights[buffer][pl.ds(unit * wide, wide), columns], k % 2, unit, transpose=True
                )
            for piece in range(count):
                value = lefts[buffer][pl.ds(piece * part, part), columns]
                for unit in range(2):
                    pltpu.matmul_acc_lhs(sums[unit][piece], value, k % 2 if piece == 0 else None)
                yield

    def both(source, buffer):
        one = expand(source, buffer)
        two = multiply(1 - buffer)
        each = -(-20 // (3 * count))
        steps, alive = 0, True
        while alive:
            alive = next(two, 1) is None
            steps += 20
            while steps >= 3 * count:
                steps -= 3 * count
                next(one, 1)
        for _ in one:
            pass

    for _ in expand(0, 0):
        pass

    def step(turn, carry):
        both(2 * turn + 1, 1)
        both(jnp.minimum(2 * turn + 2, sources - 1), 0)
        return carry

    lax.fori_loop(0, sources // 2, step, 0)
    for piece in range(count):
        rows = pl.ds(piece * part, part)
        total_ref[rows, 0:wide] = pltpu.matmul_pop(sums[0][piece])
        total_ref[rows, wide:side] = pltpu.matmul_pop(sums[1][piece])[:, : side - wide]
    share = side // out_ref.shape[0]
    full, half = side // width, share // 2
    rest = side - full * width
    for piece in range(out_ref.shape[0]):
        out_ref[piece, pl.ds(full * share, out_ref.shape[1] - full * share)] = jnp.zeros(
            (out_ref.shape[1] - full * share, width), jnp.float32
        )
        for lane in range(full):
            out_ref[piece, pl.ds(lane * share, share)] = total_ref[
                pl.ds(piece * share, share), lane * width : (lane + 1) * width
            ]
        for step in range(2):
            out_ref[piece, pl.ds(full * share, half), step * rest : (step + 1) * rest] = total_ref[
                pl.ds(piece * share + step * half, half), full * width : side
            ]


def send_kernel(used, ours_ref, came_ref, *out_refs):
    layer, row = lax.axis_index("layer"), lax.axis_index("pair")
    lines, width = came_ref.shape[1:]
    line = lax.broadcasted_iota(jnp.int32, (lines, width), 0)
    for turn, out_ref in enumerate(out_refs):
        value = ours_ref[layer, row ^ turn] + came_ref[row ^ turn]
        largest = jnp.maximum(jnp.max(jnp.abs(value), axis=0, keepdims=True), 2e-34)
        power = jnp.floor(jnp.log2(largest)) - 14.0
        steps = jnp.clip(jnp.round(value * jnp.exp2(-power)), -32767.0, 32767.0)
        steps = jnp.where(line == used, jnp.broadcast_to(power, steps.shape), steps)
        out_ref[...] = steps.astype(jnp.int32).astype(jnp.int16)


def to_send(ours, came, used):
    vmem = pl.BlockSpec(memory_space=pltpu.VMEM)
    shape = jax.ShapeDtypeStruct(came.shape[1:], jnp.int16)
    return pl.pallas_call(
        functools.partial(send_kernel, used),
        out_shape=[shape] * came.shape[0],
        in_specs=[vmem, vmem],
        out_specs=[vmem] * came.shape[0],
        compiler_params=pltpu.CompilerParams(vmem_limit_bytes=16 * 1024 * 1024),
        cost_estimate=pl.CostEstimate(flops=1000000, bytes_accessed=2000000, transcendentals=0),
        name="to_send",
    )(ours, came)


def own_kernel(cameras, lines_ref, out_ref):
    share, side = out_ref.shape
    start = (lax.axis_index("layer") * lax.axis_size("pair") + lax.axis_index("pair")) * share
    first = start // cameras
    row = start + lax.broadcasted_iota(jnp.int32, (share, side), 0)
    column = lax.broadcasted_iota(jnp.int32, (share, side), 1)
    own = jnp.zeros((share, side), jnp.float32)
    for step in range(-(-share // cameras) + 1):
        line = lines_ref[pl.ds(jnp.minimum(first + step, lines_ref.shape[0] - 1), 1), :]
        own = jnp.where(row // cameras == first + step, jnp.broadcast_to(line, (share, side)), own)
    out_ref[...] = jnp.where(row % cameras == column % cameras, own, 0.0)


def own_blocks(lines, cameras, share):
    vmem = pl.BlockSpec(memory_space=pltpu.VMEM)
    return pl.pallas_call(
        functools.partial(own_kernel, cameras),
        out_shape=jax.ShapeDtypeStruct((share, lines.shape[1]), jnp.float32),
        in_specs=[vmem],
        out_specs=vmem,
        compiler_params=pltpu.CompilerParams(vmem_limit_bytes=16 * 1024 * 1024),
        cost_estimate=pl.CostEstimate(flops=200000, bytes_accessed=100000, transcendentals=0),
        name="own_blocks",
    )(lines)


def finish_kernel(own_ref, *refs):
    pieces, out_ref = refs[:-1], refs[-1]
    share, _, side = out_ref.shape
    width = pieces[0].shape[1]
    used = side // width * share + share // 2
    total = None
    for piece in pieces:
        steps = piece[...].astype(jnp.int32).astype(jnp.float32)
        value = steps * jnp.broadcast_to(jnp.exp2(steps[used : used + 1]), steps.shape)
        total = value if total is None else total + value
    own = own_ref[...]
    full, half = side // width, share // 2
    rest = side - full * width
    for lane in range(full):
        columns = slice(lane * width, (lane + 1) * width)
        out_ref[:, 0, columns] = own[:, columns] - total[lane * share : (lane + 1) * share]
    for step in range(2):
        rows, columns = slice(step * half, (step + 1) * half), slice(full * width, side)
        out_ref[rows, 0, columns] = (
            own[rows, columns] - total[full * share : full * share + half, step * rest : (step + 1) * rest]
        )


def finish(own, pieces):
    share, side = own.shape
    vmem = pl.BlockSpec(memory_space=pltpu.VMEM)
    return pl.pallas_call(
        finish_kernel,
        out_shape=jax.ShapeDtypeStruct((share, 1, side), jnp.float32),
        in_specs=[vmem] * (1 + len(pieces)),
        out_specs=vmem,
        compiler_params=pltpu.CompilerParams(vmem_limit_bytes=16 * 1024 * 1024),
        cost_estimate=pl.CostEstimate(flops=200000, bytes_accessed=500000, transcendentals=0),
        name="finish",
    )(own, *pieces)


def schur_partial(got, cameras, shares):
    width = got.shape[4]
    side = 9 * cameras
    pieces = 9
    vmem = pl.BlockSpec(memory_space=pltpu.VMEM)
    share = side // shares
    lines = side // width * share + share // 2
    return pl.pallas_call(
        functools.partial(schur_kernel, cameras, pieces),
        out_shape=jax.ShapeDtypeStruct((shares, lines + -lines % 8, width), jnp.float32),
        in_specs=[vmem],
        out_specs=vmem,
        scratch_shapes=[
            pltpu.VMEM((side, side), jnp.float32),
            pltpu.VMEM((2, 28, 2, 8, width), jnp.float32),
            pltpu.VMEM((side, 6 * width), jnp.bfloat16),
            pltpu.VMEM((side, 6 * width), jnp.bfloat16),
            pltpu.VMEM((4 * width, 6 * width), jnp.bfloat16),
            pltpu.VMEM((4 * width, 6 * width), jnp.bfloat16),
        ],
        compiler_params=pltpu.CompilerParams(vmem_limit_bytes=32 * 1024 * 1024),
        cost_estimate=pl.CostEstimate(flops=10000000000, bytes_accessed=3000000, transcendentals=0),
        name="schur_partial",
    )(got)


AXES = ("layer", "zp", "zb", "x", "pair")


def local(sizes, jac_blocks, point_blocks, visibility, obs_count, tile_count, route, camera_blocks):
    cameras = camera_blocks.shape[3]
    side = 9 * cameras
    layers, pairs, far, near, across = (lax.axis_size(a) for a in ("layer", "pair", "zp", "zb", "x"))
    shares = layers * pairs

    def site_of(group, plane):
        side_z = (group >> bits(across)) & (near - 1)
        y = ((group >> bits(across * near)) + pairs - plane + 2 * side_z) & (pairs - 1)
        return side_z * (across * pairs) + (group & (across - 1)) * pairs + y

    packed = pack(
        jac_blocks.transpose(0, 2, 1, 3), point_blocks.transpose(1, 0, 2), visibility, obs_count, tile_count,
        route[:, 0], near * across * pairs, site_of,
    )
    own = own_blocks(camera_blocks[0].reshape(9, side), cameras, side // shares)
    got = lax.all_to_all(packed, ("zb", "x", "pair"), split_axis=0, concat_axis=0, tiled=True)
    got, own = lax.optimization_barrier((got, own))
    partial_value = schur_partial(got, cameras, shares)
    partial_value = partial_value.reshape((layers, pairs) + partial_value.shape[1:])
    layer = lax.axis_index("layer")
    theirs = lax.dynamic_index_in_dim(partial_value, 1 - layer, 0, keepdims=False)
    came = lax.ppermute(theirs, "layer", [(0, 1), (1, 0)])
    share = side // shares
    width = partial_value.shape[3]
    parcels = to_send(partial_value, came, side // width * share + share // 2)
    pieces = []
    for turn in sorted(range(far), key=lambda turn: (turn % 2, -turn)):
        links = []
        for source in itertools.product(*(range(size) for size in sizes)):
            c, zp, zb, x, y = source
            links.append((flat(source, sizes), flat((c, (y + zp + 2 * zb) % far, zb, x, y ^ turn), sizes)))
        pieces.append(lax.ppermute(parcels[turn], AXES, links))
    return finish(own, pieces).transpose(1, 0, 2)


def bits(size):
    assert size & (size - 1) == 0
    return size.bit_length() - 1


def flat(place, sizes):
    index = 0
    for coordinate, size in zip(place, sizes):
        index = index * size + coordinate
    return index


def solution(mesh):
    layers, cams, pairs = mesh.devices.shape
    across = 4
    near = 2
    sizes = (layers, cams // (near * across), near, across, pairs)
    split = jax.sharding.Mesh(mesh.devices.reshape(sizes), AXES)
    cam = ("zp", "zb", "x")
    placed = (
        P(AXES, None, None, None),
        P(AXES, None, None),
        P(AXES, None, None),
        P(AXES, None),
        P(AXES),
        P(AXES, None),
        P(cam, None, None, None),
    )
    return jax.shard_map(
        functools.partial(local, sizes),
        mesh=split,
        in_specs=placed,
        out_specs=P(cam, ("layer", "pair"), None),
        check_vma=False,
    )
```
